32 devices in a mesh: dp: 8 (over y, x, core), tensor: 4 (over z).
Axes of the slice: x: 2, y: 2, z: 4, core: 2. Of those that a mesh axis runs over, the one named last changes fastest.
Arguments:
- inputs: bfloat16 [2, 4096, 1120], P(None, ('dp', 'tensor')), may hold values from -6 to 6
- segments: int32 [2, 4096], P(None, ('dp', 'tensor')), may hold values from -1 to 4, as said below
- norm1_gain: float32 [1120], replicated, may hold values from 0.1 to 1.9
- norm1_bias: float32 [1120], replicated, may hold values from -1.75 to 1.75
- qkv_weight: bfloat16 [3, 1120, 1120], P(None, None, 'tensor'), may hold values from -0.1875 to 0.1875
- out_weight: bfloat16 [1120, 1120], P('tensor'), may hold values from -1.5 to 1.5
- norm2_gain: float32 [1120], replicated, may hold values from 0.1 to 1.9
- norm2_bias: float32 [1120], replicated, may hold values from -1.75 to 1.75
- up_weight: bfloat16 [1120, 4480], P(None, 'tensor'), may hold values from -0.1875 to 0.1875
- down_weight: bfloat16 [4480, 1120], P('tensor'), may hold values from -0.09375 to 0.09375
- cotangent: bfloat16 [2, 4096, 1120], P(None, ('dp', 'tensor')), may hold values from -6 to 6
Outputs:
- output: bfloat16 [2, 4096, 1120], P(None, ('dp', 'tensor'))
- input_grad: float32 [2, 4096, 1120], P(None, ('dp', 'tensor'))
- norm1_gain_grad: float32 [1120], replicated
- norm1_bias_grad: float32 [1120], replicated
- qkv_grad: float32 [3, 1120, 1120], P(None, None, 'tensor')
- out_grad: float32 [1120, 1120], P('tensor')
- norm2_gain_grad: float32 [1120], replicated
- norm2_bias_grad: float32 [1120], replicated
- up_grad: float32 [1120, 4480], P(None, 'tensor')
- down_grad: float32 [4480, 1120], P('tensor')
The draws below stay inside these ranges and needn't reach their ends.
Inputs may be any that keep to these rules, and one draw needn't show every extreme that they name: `segments`: in each row, cell 0 starts at the row's first token and holds more than three quarters of the row; the row ends with one or more padding tokens (-1); between them cell numbers rise by one from cell to cell, each cell of consecutive tokens.
All inputs are finite; a program needn't handle non-finite values.
Results may differ from the reference program's by a relative error of at most 0.015.
Values may be sent and summed in bfloat16 or wider, within the bound.
A program may use at most 128 MiB of HBM per device.

```python
import jax
import jax.numpy as jnp
from jax import lax

D = 1120
HEADS = 20
HD = 56
FF = 4480
ROW = 512
MICRO = 2
TOKENS_MB = 4096


def draw_segments(key, part):
    key = jax.random.fold_in(key, 11)
    count_rows = MICRO * TOKENS_MB // ROW
    key_first, key_live, key_cell = jax.random.split(key, 3)
    first = jax.random.randint(key_first, (count_rows, 1), 3 * ROW // 4 + 1, 7 * ROW // 8 + 1)
    live_end = first + jax.random.randint(key_live, (count_rows, 1), 0, ROW // 8)
    cell_len = jax.random.randint(key_cell, (count_rows, 1), ROW // 32, ROW // 8 + 1)
    live_end = live_end.at[0, 0].set(first[0, 0] + ROW // 8 - 1)
    cell_len = cell_len.at[0, 0].set(ROW // 32)
    places = jnp.arange(ROW, dtype=jnp.int32)[None, :]
    labels = jnp.where(places < first, 0, jnp.where(places < live_end, 1 + (places - first) // cell_len, -1))
    return labels.astype(jnp.int32).reshape(MICRO, TOKENS_MB)


def block_scale(rng, extent, cuts, least, largest):
    def one(axis_at, parts):
        heights = jax.random.uniform(jax.random.fold_in(jax.random.fold_in(rng, 6), axis_at), (parts,), jnp.float32, least / len(cuts), largest / len(cuts))
        return jnp.repeat(jnp.exp(heights), extent[axis_at] // parts).reshape((-1,) + (1,) * (len(extent) - axis_at - 1))

    loudness = one(*cuts[0])
    for cut in cuts[1:]:
        loudness = loudness * one(*cut)
    return loudness


def gaussian(key, dims, width, limit, cuts=(), kind=jnp.bfloat16):
    array = jax.random.normal(key, dims, jnp.float32) * width
    if len(cuts) > 0:
        array = block_scale(key, dims, cuts, -0.22, 0.18) * array
    return jnp.clip(array, min=-limit, max=limit).astype(kind)


def setup_inputs(seed: int = 0) -> dict:
    arg_keys = jax.random.split(jax.random.key(seed), 12)
    inputs = gaussian(arg_keys[0], (MICRO, TOKENS_MB, D), 1.0, 6.0, ((1, 32),))
    segments = draw_segments(jax.random.fold_in(arg_keys[11], 71), 0)
    norm1_gain = jnp.clip(1.0 + 0.18 * jax.random.normal(arg_keys[2], (D,), jnp.float32), 0.1, 1.9)
    norm1_bias = gaussian(arg_keys[3], (D,), 0.3, 1.75, (), jnp.float32)
    qkv_weight = gaussian(arg_keys[4], (3, D, D), D ** -0.5, 0.1875, ((2, 4),))
    out_weight = gaussian(arg_keys[5], (D, D), (max(D // 64, 2)) ** -0.5, 1.5, ((0, 4),))
    norm2_gain = jnp.clip(1.0 + 0.18 * jax.random.normal(arg_keys[6], (D,), jnp.float32), 0.1, 1.9)
    norm2_bias = gaussian(arg_keys[7], (D,), 0.3, 1.75, (), jnp.float32)
    up_weight = gaussian(arg_keys[8], (D, FF), D ** -0.5, 0.1875, ((1, 4),))
    down_weight = gaussian(arg_keys[9], (FF, D), FF ** -0.5, 0.09375, ((0, 4),))
    cotangent = gaussian(arg_keys[10], (MICRO, TOKENS_MB, D), 1.0, 6.0, ((1, 32),))
    return dict(inputs=inputs, segments=segments, norm1_gain=norm1_gain, norm1_bias=norm1_bias, qkv_weight=qkv_weight, out_weight=out_weight, norm2_gain=norm2_gain, norm2_bias=norm2_bias, up_weight=up_weight, down_weight=down_weight, cotangent=cotangent)


@jax.custom_vjp
def low(v):
    return lax.optimization_barrier(v.astype(jnp.bfloat16)).astype(jnp.float32)

@jax.custom_vjp
def low_back(v):
    return v

def low_keep(v):
    return (low(v), None)

def low_pass(kept, grad):
    return (grad,)

def back_keep(v):
    return (v, None)

def back_low(kept, grad):
    return (low(grad),)
low.defvjp(low_keep, low_pass)
low_back.defvjp(back_keep, back_low)
highest = lax.Precision.HIGHEST

def layer_norm(values, gain, shift):
    center = values - lax.optimization_barrier(jnp.mean(values, axis=-1, keepdims=True))
    spread = lax.optimization_barrier(jnp.mean(center * center, axis=-1, keepdims=True))
    return center * lax.rsqrt(spread + 1e-05) * gain + shift

def gelu_tanh(values):
    return jax.nn.gelu(values, approximate=True)

def attend(packed):
    queries, keys, values, labels = packed
    scores = jnp.einsum('qhe,khe->hqk', queries, keys, precision=highest) * HD ** (-0.5)
    scores = low_back(scores)
    places = jnp.arange(ROW, dtype=jnp.int32)
    allowed = (places[:, None] >= places[None, :]) & (labels[:, None] == labels[None, :])
    masked = jnp.where(allowed[None], scores, -1e+30)
    probs = low(jax.nn.softmax(masked, axis=-1))
    mixed = jnp.einsum('hqk,khe->qhe', probs, values, precision=highest)
    return low(low_back(mixed.reshape(ROW, HEADS * HD)))

def forward(segments, inputs, norm1_gain, norm1_bias, qkv_weight, out_weight, norm2_gain, norm2_bias, up_weight, down_weight):
    row_inputs = inputs.reshape(-1, ROW, D)
    labels = segments.reshape(-1, ROW)
    count_rows = row_inputs.shape[0]
    norm_one = low(layer_norm(row_inputs, norm1_gain, norm1_bias))
    projected = low(low_back(jnp.einsum('rtd,cdf->crtf', norm_one, qkv_weight, precision=highest)))
    queries = projected[0].reshape(count_rows, ROW, HEADS, HD)
    keys = projected[1].reshape(count_rows, ROW, HEADS, HD)
    values = projected[2].reshape(count_rows, ROW, HEADS, HD)
    mixed = lax.map(jax.checkpoint(attend), (queries, keys, values, labels))
    attn = jnp.einsum('rtc,cd->rtd', mixed, out_weight, precision=highest)
    resid = row_inputs + low_back(attn)
    norm_two = low(layer_norm(resid, norm2_gain, norm2_bias))
    hidden_in = jnp.einsum('rtd,df->rtf', norm_two, up_weight, precision=highest)
    hidden = low(gelu_tanh(low_back(hidden_in)))
    branch = jnp.einsum('rtf,fd->rtd', hidden, down_weight, precision=highest)
    return (resid + low_back(branch)).reshape(inputs.shape)

def reference(inputs, segments, norm1_gain, norm1_bias, qkv_weight, out_weight, norm2_gain, norm2_bias, up_weight, down_weight, cotangent):
    live_mask = (segments >= 0)[..., None].astype(jnp.float32)
    grad_out = cotangent.astype(jnp.float32) * live_mask
    primals = (inputs.astype(jnp.float32), norm1_gain, norm1_bias, qkv_weight.astype(jnp.float32), out_weight.astype(jnp.float32), norm2_gain, norm2_bias, up_weight.astype(jnp.float32), down_weight.astype(jnp.float32))
    result, backward = jax.vjp(partial_forward(segments), *primals)
    grads = backward(grad_out)
    return (result.astype(jnp.bfloat16), grads[0], grads[1], grads[2], grads[3], grads[4], grads[5], grads[6], grads[7], grads[8])

def partial_forward(segments):

    def wrapped(*primals):
        return forward(segments, *primals)
    return wrapped
```

```python
import functools

import jax
import jax.numpy as jnp
from jax import lax
from jax.experimental import pallas as pl
from jax.experimental.pallas import tpu as pltpu
from jax.sharding import PartitionSpec as P


HD = 56
BF = jnp.bfloat16
F32 = jnp.float32
MESH = pl.DeviceIdType.MESH
NN = (((1,), (0,)), ((), ()))
NT = (((1,), (1,)), ((), ()))
TN = (((0,), (0,)), ((), ()))
COLS = 4
BITS = (1, 2)
NSEM = 256


def up_to(n, m):
    return -(-n // m) * m


def chunk_rows(rows):
    return up_to(-(-rows // COLS), 16)


def streams(ch):
    first = up_to(ch // 2, 16)
    return ((0, first, BITS, 0), (first, ch - first, BITS[::-1], 1))


def dg(a, b, dims):
    return lax.dot_general(a, b, dims, preferred_element_type=F32)


def normed(v):
    center = v - jnp.mean(v, axis=-1, keepdims=True)
    rstd = lax.rsqrt(jnp.mean(center * center, axis=-1, keepdims=True) + 1e-05)
    return center * rstd, rstd


def kernel(
    x_hbm, seg_ref, n1g, n1b, wq_hbm, wo_hbm, n2g, n2b, wu_hbm, wd_hbm, c_hbm,
    out_hbm, ig_hbm, gq_hbm, go_hbm, gu_hbm, gd_hbm, ng_ref,
    WQ, WO, WU, WD, GU, GD, RQ, RO, RU, RD, SQ, SO, SU, SD, KQ, KO, KU, KD,
    XS, CS, LAB, LT, BIAS, A1, QKV, PB0, PB1, O, HS, A2, Z, GP, GB, DHB, DO, DH, U,
    T2, S1, S2, SZ, R1, R2, RZ, OB, NG, NR,
    ssem, rsem, lsem,
):
    d = lax.axis_index("dp")
    z = lax.axis_index("tensor")
    c = lax.rem(d, 2)
    q = lax.rem(d // 2, COLS)
    zl = lax.rem(z, 2)
    zh = z // 2
    b = zl + 2 * c
    sw = zh != c
    dc = d + 1 - 2 * c
    z1 = z + 1 - 2 * zl
    z2 = z + 2 - 4 * zh
    core = (dc, z)
    zpeer = (d, z1)
    sigma = (dc, z2)

    def col(bit):
        on = lax.rem(q // bit, 2)
        return (d + 2 * bit * (1 - 2 * on), z)

    def flip(owner, bit):
        on = lax.rem(owner // bit, 2)
        return owner + bit * (1 - 2 * on)

    xpeer, ypeer = col(1), col(2)
    micro, tok, width = XS.shape
    row = 4 * tok
    heads = O.shape[1] // HD
    scale = HD ** (-0.5)
    counts = dict(r=0, l=0)
    pending = []

    def rcopy(src, dst, peer):
        i = counts["r"]
        counts["r"] = i + 1
        assert i < NSEM
        return pltpu.make_async_remote_copy(
            src_ref=src, dst_ref=dst, send_sem=ssem.at[i], recv_sem=rsem.at[i], device_id=peer, device_id_type=MESH
        )

    def lcopy(src, dst):
        i = counts["l"]
        counts["l"] = i + 1
        return pltpu.make_async_copy(src, dst, lsem.at[i])

    def rows(start, size, step=16):
        return pl.ds(pl.multiple_of(start, step), size)

    def blk(m, j):
        return pl.ds(pl.multiple_of(m * row + j * tok, tok), tok)

    def swapped(f):
        pl.when(sw)(f)

    def kept(f):
        pl.when(jnp.logical_not(sw))(f)

    barrier = pltpu.get_barrier_semaphore()
    peers = (core, zpeer, sigma, xpeer, ypeer)
    for p in peers:
        pl.semaphore_signal(barrier, 1, device_id=p, device_id_type=MESH)
    pl.semaphore_wait(barrier, len(peers))

    class Gather:
        def __init__(self, view):
            self.view = view
            self.cz = rcopy(view(b), view(b), zpeer)
            self.cc = rcopy(view(b), view(b), core)
            far = 1 - zl + 2 * c
            self.cf = rcopy(view(far), view(far), core)

        def start(self):
            self.cz.start()
            self.cc.start()

        def forward(self):
            self.cz.wait_recv()
            self.cf.start()

        def finish(self):
            self.cc.wait_recv()
            self.cf.wait_recv()
            pending.extend([self.cz, self.cc, self.cf])

    def gather_rows(ref, m):
        return Gather(lambda j: ref.at[blk(m, j)])

    class Scatter:
        def __init__(self, s):
            self.s = s
            self.c1 = rcopy(S1.at[s], R1.at[s], core)
            self.c2 = rcopy(S2.at[s], R2.at[s], core)
            self.cz = rcopy(SZ.at[s], RZ.at[s], zpeer)

        def start(self, term):
            s = self.s
            away = 1 - zl
            part = term(away + 2 * (1 - c), away + 2 * c)
            S1[s] = part[:tok].astype(BF)
            self.c1.start()
            keep = part[tok:]
            part = term(zl + 2 * (1 - c), zl + 2 * c)
            S2[s] = part[:tok].astype(BF)
            T2[s] = part[tok:]
            self.c2.start()
            self.c1.wait_recv()
            SZ[s] = (keep + R1[s].astype(F32)).astype(BF)
            self.cz.start()

        def finish(self):
            s = self.s
            self.c2.wait_recv()
            self.cz.wait_recv()
            total = T2[s] + R2[s].astype(F32) + RZ[s].astype(F32)
            for cp in (self.c1, self.c2, self.cz):
                cp.wait_send()
            return total

    class Weight:
        def __init__(self, hbm, ref):
            self.hbm, self.ref = hbm, ref
            have, total = hbm.shape[0], ref.shape[0]
            self.ch = ch = total // COLS
            self.local = lcopy(hbm, ref.at[0:have])
            self.hops = []
            for off, size, order, _ in streams(ch):
                i = counts["r"]
                counts["r"] = i + 1
                first = []
                for short in (False, True):
                    lost = max(0, total - have)
                    n = size - min(lost, size) if short and off else size
                    at = rows(q * ch + off, n)
                    cp = pltpu.make_async_remote_copy(
                        src_ref=hbm.at[at], dst_ref=ref.at[at], send_sem=ssem.at[i], recv_sem=rsem.at[i],
                        device_id=sigma, device_id_type=MESH,
                    )
                    first.append((n, cp))
                steps, done = [], [0]
                for bit in order:
                    copies = []
                    for s in done:
                        owner = q
                        for k in BITS:
                            if s & k:
                                owner = flip(owner, k)
                        at = rows(owner * ch + off, size)
                        copies.append(rcopy(ref.at[at], ref.at[at], col(bit)))
                    steps.append(copies)
                    done = done + [s | bit for s in done]
                self.hops.append((size, first, steps))

        def each_first(self, act):
            for size, ((_, whole), (n, part)) in [(h[0], h[1]) for h in self.hops]:
                if n == size:
                    act(whole)
                else:
                    pl.when(q < COLS - 1)(functools.partial(act, whole))
                    pl.when(q == COLS - 1)(functools.partial(act, part))

        def send(self):
            swapped(lambda: self.each_first(lambda cp: cp.start()))

        def load(self):
            kept(self.local.start)

        def stage(self, j):
            def go():
                if j == 0:
                    self.each_first(lambda cp: cp.wait_recv())
                else:
                    for _, _, steps in self.hops:
                        for cp in steps[j - 1]:
                            cp.wait_recv()
                for _, _, steps in self.hops:
                    for cp in steps[j]:
                        cp.start()

            swapped(go)

        def finish(self):
            def go():
                for _, _, steps in self.hops:
                    for cp in steps[-1]:
                        cp.wait_recv()
                self.each_first(lambda cp: cp.wait_send())
                for _, _, steps in self.hops:
                    for copies in steps:
                        for cp in copies:
                            cp.wait_send()

            swapped(go)
            kept(self.local.wait)

    class Grad:
        def __init__(self, ref, lanes, recv, far, near, hbm):
            self.ref, self.lanes, self.recv, self.far, self.near, self.hbm = ref, lanes, recv, far, near, hbm
            self.ch = ch = recv.shape[1]
            self.parts = []
            for off, size, order, fin in streams(ch):
                part = dict(off=off, size=size, order=order, fin=fin)
                base, steps = 0, []
                for j, bit in enumerate(order):
                    rest = [0]
                    for k in order[j + 1 :]:
                        rest = rest + [s | k for s in rest]
                    copies = []
                    for i, s in enumerate(rest):
                        mine = q
                        for k in BITS:
                            if s & k:
                                mine = flip(mine, k)
                        theirs = flip(mine, bit)
                        slot = recv.at[base + i, off : off + size]
                        copies.append((mine, base + i, rcopy(self.at(theirs, off, size), slot, col(bit))))
                    base += len(rest)
                    steps.append(copies)
                part["rs"] = steps
                part["sigma"] = rcopy(self.at(q, off, size), far.at[off : off + size], sigma)
                part["near"] = rcopy(self.at(q, off, size), near.at[0:size], core)
                part["own"] = lcopy(self.at(q, off, size), self.out(q, off, size))
                part["own_core"] = rcopy(self.at(q, off, size), self.out(q, off, size), core)
                done, spread = [0], []
                for bit in order:
                    copies = []
                    for s in done:
                        owner = q
                        for k in BITS:
                            if s & k:
                                owner = flip(owner, k)
                        src = self.at(q, off, size) if s == 0 else self.out(owner, off, size)
                        got = flip(owner, bit)
                        copies.append(
                            (
                                rcopy(src, self.out(owner, off, size), col(bit)),
                                rcopy(self.out(got, off, size), self.out(got, off, size), core),
                            )
                        )
                    spread.append(copies)
                    done = done + [s | bit for s in done]
                part["spread"] = spread
                self.parts.append(part)

        def at(self, owner, off, size):
            return self.ref.at[rows(owner * self.ch + off, size), 0 : self.lanes]

        def out(self, owner, off, size):
            return self.hbm.at[rows(owner * self.ch + off, size)]

        def reduce_send(self, j):
            for p in self.parts:
                for _, _, cp in p["rs"][j]:
                    cp.start()

        def reduce_add(self, j):
            for p in self.parts:
                off, size = p["off"], p["size"]
                for mine, slot, cp in p["rs"][j]:
                    cp.wait_recv()
                    r = rows(mine * self.ch + off, size)
                    total = self.ref[r, 0 : self.lanes].astype(F32) + self.recv[slot, off : off + size].astype(F32)
                    self.ref[r, 0 : self.lanes] = total.astype(BF)
                    pending.append(cp)

        def sigma_send(self):
            swapped(lambda: [p["sigma"].start() for p in self.parts] and None)

        def sigma_take(self):
            def go():
                for p in self.parts:
                    off, size = p["off"], p["size"]
                    p["sigma"].wait()
                    self.ref[rows(q * self.ch + off, size), 0 : self.lanes] = self.far[off : off + size]

            swapped(go)

        def near_send(self):
            for p in self.parts:
                pl.when(c != p["fin"])(p["near"].start)

        def near_add(self):
            for p in self.parts:

                def give(p=p):
                    p["near"].wait_send()

                def take(p=p):
                    p["near"].wait_recv()
                    r = rows(q * self.ch + p["off"], p["size"])
                    total = self.ref[r, 0 : self.lanes].astype(F32) + self.near[0 : p["size"]].astype(F32)
                    self.ref[r, 0 : self.lanes] = total.astype(BF)
                    for cp, _ in p["spread"][0]:
                        cp.start()
                    p["own_core"].start()
                    p["own"].start()

                pl.when(c != p["fin"])(give)
                pl.when(c == p["fin"])(take)

        def spread(self, j):
            for p in self.parts:

                def go(p=p):
                    for cp, _ in p["spread"][j]:
                        cp.wait_recv()
                    if j + 1 < len(p["spread"]):
                        for cp, _ in p["spread"][j + 1]:
                            cp.start()
                    for _, cp in p["spread"][j]:
                        cp.start()

                pl.when(c == p["fin"])(go)

        def finish(self):
            for p in self.parts:

                def owner(p=p):
                    p["own"].wait()
                    p["own_core"].wait_send()
                    for copies in p["spread"]:
                        for a, f in copies:
                            a.wait_send()
                            f.wait_send()

                def other(p=p):
                    p["own_core"].wait_recv()
                    for copies in p["spread"]:
                        for _, f in copies:
                            f.wait_recv()

                pl.when(c == p["fin"])(owner)
                pl.when(c != p["fin"])(other)

    wq, wo, wu, wd = Weight(wq_hbm, WQ), Weight(wo_hbm, WO), Weight(wu_hbm, WU), Weight(wd_hbm, WD)
    other_b = zl + 2 * (1 - c)
    x_swap = [rcopy(x_hbm.at[m], XS.at[m], sigma) for m in range(micro)]
    x_load = [lcopy(x_hbm.at[m], XS.at[m]) for m in range(micro)]
    c_swap = rcopy(c_hbm, CS, sigma)
    c_load = lcopy(c_hbm, CS)
    lab_swap = rcopy(seg_ref, LAB.at[other_b], sigma)
    lab_gather = Gather(lambda j: LAB.at[j])
    a1_gather = [gather_rows(A1, m) for m in range(micro)]
    gb_gather = [gather_rows(GB, m) for m in range(micro)]
    a2_gather = [gather_rows(A2, m) for m in range(micro)]
    dhb_gather = [gather_rows(DHB, m) for m in range(micro)]

    def first_norm(m):
        swapped(x_swap[m].wait_recv)
        kept(x_load[m].wait)
        xhat, _ = normed(XS[m].astype(F32))
        A1[blk(m, b), :] = (xhat * n1g[...] + n1b[...]).astype(BF)
        a1_gather[m].start()

    def labels_wide():
        for m in range(micro):
            for j in range(4):
                lab = LAB[j, m : m + 1, :].astype(F32)
                LT[m, j * tok : (j + 1) * tok, :] = jnp.transpose(jnp.broadcast_to(lab, (tok, tok)))

    def loss_grad():
        swapped(c_swap.wait_recv)
        kept(c_load.wait)
        for m in range(micro):
            live = (LT[m, pl.ds(pl.multiple_of(b * tok, tok), tok), 0:1] >= 0.0).astype(F32)
            GB[blk(m, b), :] = (CS[m].astype(F32) * live).astype(BF)
            gb_gather[m].start()

    def make_bias(m):
        for j in range(4):
            lab = LAB[j, m : m + 1, :].astype(F32)
            place_q = lax.broadcasted_iota(jnp.int32, (row, tok), 0)
            place_k = lax.broadcasted_iota(jnp.int32, (row, tok), 1) + j * tok
            ok = (LT[m] == lab) & (place_k <= place_q)
            BIAS[:, j * tok : (j + 1) * tok] = jnp.where(ok, 0.0, -1e30)

    half = row // 2
    local_width = O.shape[1]

    def qkv_slices(m, h, qb):
        nk = (qb + 1) * half
        at = m * row
        q0 = at + qb * half
        e0, e1, e2 = h * HD, local_width + h * HD, 2 * local_width + h * HD
        return (
            slice(q0, q0 + half),
            slice(at, at + nk),
            slice(e0, e0 + HD),
            slice(e1, e1 + HD),
            slice(e2, e2 + HD),
        )

    def project(m):
        at = slice(m * row, (m + 1) * row)
        QKV[at, :] = dg(A1[at, :], WQ[0:width, :], NN).astype(BF)

    def attend(m):
        for h in range(heads):
            for qb, PB in ((0, PB0), (1, PB1)):
                rq, rk, eq, ek, ev = qkv_slices(m, h, qb)
                s = dg(QKV[rq, eq], QKV[rk, ek], NT) * scale
                s = s + BIAS[qb * half : (qb + 1) * half, 0 : (qb + 1) * half]
                e = jnp.exp(s - jnp.max(s, axis=-1, keepdims=True))
                p = (e * (1.0 / jnp.sum(e, axis=-1, keepdims=True))).astype(BF)
                PB[m, h] = p
                O[rq, eq] = dg(p, QKV[rk, ev], NN).astype(BF)

    def attend_back(m):
        for h in range(heads):
            for qb, PB in ((1, PB1), (0, PB0)):
                rq, rk, eq, ek, ev = qkv_slices(m, h, qb)
                qv, do, pb = QKV[rq, eq], DO[rq, eq], PB[m, h]
                kv = QKV[rk, ek]
                dp = dg(do, QKV[rk, ev], NT)
                p = pb.astype(F32)
                pdp = p * dp
                ds = (pdp - p * jnp.sum(pdp, axis=-1, keepdims=True)).astype(BF)
                dq = (dg(ds, kv, NN) * scale).astype(BF)
                dk, dv = dg(ds, qv, TN), dg(pb, do, TN)
                if qb == 1:
                    dq1, dk1, dv1, rq1 = dq, dk, dv, rq
                else:
                    QKV[rq, eq] = dq
                    QKV[rq1, eq] = dq1
                    QKV[rq, ek] = ((dk1[:half] + dk) * scale).astype(BF)
                    QKV[rq1, ek] = (dk1[half:] * scale).astype(BF)
                    QKV[rq, ev] = (dv1[:half] + dv).astype(BF)
                    QKV[rq1, ev] = dv1[half:].astype(BF)

    def pair(ref, m, i, j):
        return jnp.concatenate([ref[blk(m, i), :], ref[blk(m, j), :]], axis=0)

    def second_norm(m, total):
        h = XS[m].astype(F32) + total
        HS[m] = h
        xhat, _ = normed(h)
        A2[blk(m, b), :] = (xhat * n2g[...] + n2b[...]).astype(BF)
        a2_gather[m].start()

    def up(m):
        for part in range(2):
            up_half(m * row + part * half)

    def up_half(at):
        U[...] = dg(A2[at : at + half, :], WU[0:width, :], NN)
        c0 = 0.7978845608028654
        step = 32

        def body(i, carry):
            r = rows(i * step, step, step)
            w = rows(at + i * step, step, step)
            u = U[r, :]
            u2 = u * u
            t = jnp.tanh(c0 * u * (1.0 + 0.044715 * u2))
            hp = 0.5 * (1.0 + t)
            Z[w, :] = (u * hp).astype(BF)
            GP[w, :] = (hp + (0.5 * c0) * u * (1.0 - t * t) * (1.0 + (3 * 0.044715) * u2)).astype(BF)
            return carry

        lax.fori_loop(0, half // step, body, 0)

    def down_back(m):
        at = slice(m * row, (m + 1) * row)
        dz = dg(GB[at, :], WD[0 : Z.shape[1], :], NT)
        GP[at, :] = (dz * GP[at, :].astype(F32)).astype(BF)

    def norm_back(v, gain, grad):
        xhat, rstd = normed(v)
        gains = jnp.sum(grad * xhat, axis=0, keepdims=True)
        shifts = jnp.sum(grad, axis=0, keepdims=True)
        dn = grad * gain
        dv = rstd * (
            dn - jnp.mean(dn, axis=-1, keepdims=True) - xhat * jnp.mean(dn * xhat, axis=-1, keepdims=True)
        )
        return dv, gains, shifts

    def second_norm_back(m, total):
        dv, gains, shifts = norm_back(HS[m], n2g[...], total)
        NG[2:3, :] += gains
        NG[3:4, :] += shifts
        dh = GB[blk(m, b), :].astype(F32) + dv
        DH[m] = dh
        DHB[blk(m, b), :] = dh.astype(BF)
        dhb_gather[m].start()

    def first_norm_back(m, total):
        dv, gains, shifts = norm_back(XS[m].astype(F32), n1g[...], total)
        NG[0:1, :] += gains
        NG[1:2, :] += shifts
        return DH[m] + dv

    NG[...] = jnp.zeros_like(NG)
    wq.send()
    swapped(lambda: (lab_swap.start(), x_swap[0].start(), x_swap[1].start()) and None)
    kept(lambda: (x_load[0].start(), x_load[1].start(), c_load.start()) and None)
    for w in (wq, wo, wu, wd):
        w.load()

    @pl.when(jnp.logical_not(sw))
    def _():
        LAB[b] = seg_ref[...]

    swapped(lab_swap.wait_recv)
    lab_gather.start()
    first_norm(0)
    wq.stage(0)
    first_norm(1)
    swapped(c_swap.start)
    wo.send()
    lab_gather.forward()
    a1_gather[0].forward()
    lab_gather.finish()
    labels_wide()
    make_bias(0)
    wq.stage(1)
    wu.send()
    a1_gather[1].forward()
    wo.stage(0)
    a1_gather[0].finish()
    wq.finish()

    attn_sum = [Scatter(2 * m) for m in range(micro)]
    mid_sum = [Scatter(2 * m) for m in range(micro)]
    y_sum = [Scatter(2 * m + 1) for m in range(micro)]
    in_sum = [Scatter(2 * m) for m in range(micro)]

    def out_term(m):
        return lambda i, j: dg(pair(O, m, i, j), WO[0:local_width, :], NN)

    def y_term(m):
        return lambda i, j: dg(pair(Z, m, i, j), WD[0 : Z.shape[1], :], NN)

    def mid_term(m):
        return lambda i, j: dg(pair(GP, m, i, j), WU[0:width, :], NT)

    def in_term(m):
        return lambda i, j: dg(pair(QKV, m, i, j), WQ[0:width, :], NT)

    project(0)
    loss_grad()
    wo.stage(1)
    wd.send()
    attend(0)
    wu.stage(0)
    wo.finish()
    attn_sum[0].start(out_term(0))
    for m in range(micro):
        gb_gather[m].forward()
    a1_gather[1].finish()
    make_bias(1)
    project(1)
    wu.stage(1)
    attend(1)
    wd.stage(0)
    attn_sum[1].start(out_term(1))
    second_norm(0, attn_sum[0].finish())
    wd.stage(1)
    second_norm(1, attn_sum[1].finish())
    a2_gather[0].forward()
    wu.finish()
    a2_gather[0].finish()
    up(0)
    a2_gather[1].forward()
    wd.finish()
    gb_gather[0].finish()
    down_back(0)
    mid_sum[0].start(mid_term(0))
    a2_gather[1].finish()
    up(1)
    gb_gather[1].finish()
    down_back(1)
    mid_sum[1].start(mid_term(1))
    second_norm_back(0, mid_sum[0].finish())
    y_sum[0].start(y_term(0))
    second_norm_back(1, mid_sum[1].finish())
    y_sum[1].start(y_term(1))
    dhb_gather[0].forward()

    gq = Grad(WU, gq_hbm.shape[1], RQ, SQ, KQ, gq_hbm)
    go = Grad(WD, width, RO, SO, KO, go_hbm)
    gu = Grad(GU, gu_hbm.shape[1], RU, SU, KU, gu_hbm)
    gd = Grad(GD, width, RD, SD, KD, gd_hbm)
    ff = Z.shape[1]
    GD[0:ff, :] = dg(Z[...], GB[...], TN).astype(BF)
    GD[ff:, :] = jnp.zeros((GD.shape[0] - ff, width), BF)
    gd.reduce_send(0)
    dhb_gather[1].forward()
    GU[0:width, :] = dg(A2[...], GP[...], TN).astype(BF)
    GU[width:, :] = jnp.zeros((GU.shape[0] - width, ff), BF)
    dhb_gather[0].finish()

    def heads_back(m):
        at = slice(m * row, (m + 1) * row)
        DO[at, :] = dg(DHB[at, :], WO[0:local_width, :], NT).astype(BF)
        attend_back(m)

    heads_back(0)
    gd.reduce_add(0)
    gd.reduce_send(1)
    gu.reduce_send(0)
    in_sum[0].start(in_term(0))
    dhb_gather[1].finish()
    WD[0:local_width, :] = dg(O[...], DHB[...], TN).astype(BF)
    gd.reduce_add(1)
    gd.sigma_send()
    heads_back(1)
    gu.reduce_add(0)
    gu.reduce_send(1)
    in_sum[1].start(in_term(1))
    WU[0:width, 0 : 3 * local_width] = dg(A1[...], QKV[...], TN).astype(BF)
    gq.reduce_send(0)
    go.reduce_send(0)
    gd.sigma_take()
    gd.near_send()
    gu.reduce_add(1)
    gu.sigma_send()
    gd.near_add()

    out_swap = [rcopy(OB.at[m], out_hbm.at[m], sigma) for m in range(micro)]
    out_keep = [lcopy(OB.at[m], out_hbm.at[m]) for m in range(micro)]
    ig_swap = [rcopy(XS.at[m], CS.at[m], sigma) for m in range(micro)]
    ig_keep = [lcopy(DH.at[m], ig_hbm.at[m]) for m in range(micro)]
    for m in range(micro):
        OB[m] = (HS[m] + y_sum[m].finish()).astype(BF)
        swapped(out_swap[m].start)
        kept(out_keep[m].start)
    gq.reduce_add(0)
    gq.reduce_send(1)
    go.reduce_add(0)
    go.reduce_send(1)
    gu.sigma_take()
    gu.near_send()
    for m in range(micro):
        dx = first_norm_back(m, in_sum[m].finish())
        DH[m] = dx

        @pl.when(sw)
        def _():
            XS[m] = dx.astype(BF)
            ig_swap[m].start()

        kept(ig_keep[m].start)
    gu.near_add()
    gd.spread(0)
    gq.reduce_add(1)
    gq.sigma_send()
    go.reduce_add(1)
    go.sigma_send()
    sums = iter([rcopy(NG, NR.at[i], p) for i, p in enumerate((core, zpeer, sigma, xpeer, ypeer))])

    def sum_send():
        cp = next(sums)
        cp.start()
        return cp

    def sum_add(i, cp):
        cp.wait()
        NG[...] = NG[...] + NR[i]

    cp = sum_send()
    gu.spread(0)
    gd.spread(1)
    sum_add(0, cp)
    cp = sum_send()
    gu.spread(1)
    sum_add(1, cp)
    cp = sum_send()
    gq.sigma_take()
    gq.near_send()
    go.sigma_take()
    go.near_send()
    gq.near_add()
    go.near_add()
    sum_add(2, cp)
    cp = sum_send()
    gq.spread(0)
    go.spread(0)
    sum_add(3, cp)
    cp = sum_send()
    gq.spread(1)
    go.spread(1)
    sum_add(4, cp)
    ng_ref[...] = NG[...]
    for m in range(micro):

        @pl.when(sw)
        def _():
            ig_swap[m].wait()
            DH[m] = CS[m].astype(F32)
            ig_keep[m].start()
            out_swap[m].wait()
            c_in = x_swap[m]
            c_in.wait_send()

        ig_keep[m].wait()
        kept(out_keep[m].wait)
    swapped(lambda: (c_swap.wait_send(), lab_swap.wait_send()) and None)
    lab_gather_sends = []
    for cp in pending + lab_gather_sends:
        cp.wait_send()
    for g in (gd, gu, gq, go):
        g.finish()


def layer(
    inputs, segments, norm1_gain, norm1_bias, qkv_weight, out_weight, norm2_gain, norm2_bias, up_weight, down_weight,
    cotangent,
):
    micro, tok, width = inputs.shape
    local_width = qkv_weight.shape[2]
    ff = up_weight.shape[1]
    row = 4 * tok
    heads = local_width // HD
    three = 3 * local_width
    wide = up_to(three, 128)
    half = row // 2
    cq, co, cu, cd = chunk_rows(width), chunk_rows(local_width), chunk_rows(width), chunk_rows(ff)
    wq = jnp.transpose(qkv_weight, (1, 0, 2)).reshape(width, three)
    wq = jnp.pad(wq, ((0, COLS * cq - width), (0, 0)))
    wo = jnp.pad(out_weight, ((0, COLS * co - local_width), (0, 0)))

    def v(shape, dtype=BF):
        return pltpu.VMEM(shape, dtype)

    def recv(ch, lanes):
        return v((COLS - 1, ch, lanes))

    def near(ch, lanes):
        return v((max(size for _, size, _, _ in streams(ch)), lanes))

    any_spec = pl.BlockSpec(memory_space=pl.ANY)
    vmem = pl.BlockSpec(memory_space=pltpu.VMEM)
    scratch = [
        v((COLS * cq, three)), v((COLS * co, width)), v((COLS * cu, ff)), v((COLS * cd, width)),
        v((COLS * cu, ff)), v((COLS * cd, width)),
        recv(cq, wide), recv(co, width), recv(cu, ff), recv(cd, width),
        v((cq, wide)), v((co, width)), v((cu, ff)), v((cd, width)),
        near(cq, wide), near(co, width), near(cu, ff), near(cd, width),
        v((micro, tok, width)), v((micro, tok, width)), v((4, micro, tok), jnp.int32), v((micro, row, tok), F32),
        v((row, row), F32),
        v((micro * row, width)), v((micro * row, three)),
        v((micro, heads, half, half)), v((micro, heads, half, row)), v((micro * row, local_width)),
        v((micro, tok, width), F32),
        v((micro * row, width)), v((micro * row, ff)), v((micro * row, ff)), v((micro * row, width)),
        v((micro * row, width)), v((micro * row, local_width)), v((micro, tok, width), F32), v((half, ff), F32),
        v((2 * micro, tok, width), F32),
        v((2 * micro, tok, width)), v((2 * micro, tok, width)), v((2 * micro, tok, width)),
        v((2 * micro, tok, width)), v((2 * micro, tok, width)), v((2 * micro, tok, width)),
        v((micro, tok, width)),
        v((8, width), F32), v((5, 8, width), F32),
        pltpu.SemaphoreType.DMA((NSEM,)), pltpu.SemaphoreType.DMA((NSEM,)), pltpu.SemaphoreType.DMA((32,)),
    ]
    out, input_grad, gq, go, gu, gd, ng = pl.pallas_call(
        kernel,
        out_shape=[
            jax.ShapeDtypeStruct((micro, tok, width), BF),
            jax.ShapeDtypeStruct((micro, tok, width), F32),
            jax.ShapeDtypeStruct((COLS * cq, wide), BF),
            jax.ShapeDtypeStruct((COLS * co, width), BF),
            jax.ShapeDtypeStruct((COLS * cu, ff), BF),
            jax.ShapeDtypeStruct((COLS * cd, width), BF),
            jax.ShapeDtypeStruct((8, width), F32),
        ],
        in_specs=[any_spec, vmem, vmem, vmem, any_spec, any_spec, vmem, vmem, any_spec, any_spec, any_spec],
        out_specs=[any_spec] * 6 + [vmem],
        scratch_shapes=scratch,
        compiler_params=pltpu.CompilerParams(
            collective_id=0, has_side_effects=True, vmem_limit_bytes=64 * 1024 * 1024
        ),
    )(
        inputs, segments, norm1_gain[None], norm1_bias[None], wq, wo, norm2_gain[None], norm2_bias[None], up_weight,
        down_weight, cotangent,
    )
    grads = (
        jnp.transpose(gq[:width, :three].reshape(width, 3, local_width), (1, 0, 2)).astype(F32),
        go[:local_width].astype(F32),
        gu[:width].astype(F32),
        gd[:ff].astype(F32),
    )
    extent = lax.axis_size("dp")
    block = 2 * COLS
    if extent > block:
        groups = [[r + block * j for j in range(extent // block)] for r in range(block)]
        grads = lax.psum(grads, "dp", axis_index_groups=groups)
        ng = lax.psum(ng, "dp", axis_index_groups=groups)
    gq, go, gu, gd = grads
    return out, input_grad, ng[0], ng[1], gq, go, ng[2], ng[3], gu, gd


def solution(mesh):
    tokens = P(None, ("dp", "tensor"), None)
    weights = (P(None, None, "tensor"), P("tensor", None))
    mlp = (P(None, "tensor"), P("tensor", None))
    return jax.shard_map(
        layer,
        mesh=mesh,
        in_specs=(tokens, P(None, ("dp", "tensor")), P(), P(), *weights, P(), P(), *mlp, tokens),
        out_specs=(tokens, tokens, P(), P(), *weights, P(), P(), *mlp),
        check_vma=False,
    )
```

```python
import functools

import jax
import jax.numpy as jnp
from jax import lax
from jax.experimental import pallas as pl
from jax.experimental.pallas import tpu as pltpu
from jax.sharding import PartitionSpec as P


HD = 56
BF = jnp.bfloat16
F32 = jnp.float32
MESH = pl.DeviceIdType.MESH
NN = (((1,), (0,)), ((), ()))
NT = (((1,), (1,)), ((), ()))
TN = (((0,), (0,)), ((), ()))
COLS = 4
BITS = (1, 2)
NSEM = 384


def up_to(n, m):
    return -(-n // m) * m


def chunk_rows(rows):
    return up_to(-(-rows // COLS), 16)


def parts_of(ch, n):
    out, off = [], 0
    for i in range(n):
        size = up_to(-(-(ch - off) // (n - i)), 16)
        out.append((off, size, BITS if i % 2 == 0 else BITS[::-1], i % 2))
        off += size
    return out


def dg(a, b, dims):
    return lax.dot_general(a, b, dims, preferred_element_type=F32)


def normed(v):
    center = v - jnp.mean(v, axis=0, keepdims=True)
    rstd = lax.rsqrt(jnp.mean(center * center, axis=0, keepdims=True) + 1e-05)
    return center * rstd, rstd


def kernel(
    x_hbm, seg_ref, n1g, n1b, wq_hbm, wo_hbm, ends, n2g, n2b, wu_hbm, wd_hbm, c_hbm,
    out_hbm, ig_hbm, gq_hbm, go_hbm, gu_hbm, gd_hbm, ng_ref,
    WQ, WO, WU, WD, GU, GD, RQ, RO, RU, RD, SQ, SO, SU, SD, KQ, KO, KU, KD,
    XS, CS, LAB, LT, BIAS, NW, A1, QKV, PB0, PB1, O, HS, A2, Z, GP, GB, DHB, DO, DH, U,
    T2, S1, S2, SZ, R1, R2, RZ, OB, NG, NR,
    ssem, rsem, lsem,
):
    d = lax.axis_index("dp")
    z = lax.axis_index("tensor")
    c = lax.rem(d, 2)
    q = lax.rem(d // 2, COLS)
    zl = lax.rem(z, 2)
    zh = z // 2
    b = zl + 2 * c
    sw = zh != c
    dc = d + 1 - 2 * c
    z1 = z + 1 - 2 * zl
    z2 = z + 2 - 4 * zh
    core = (dc, z)
    zpeer = (d, z1)
    sigma = (dc, z2)

    def flip(owner, bit):
        on = lax.rem(owner // bit, 2)
        return owner + bit * (1 - 2 * on)

    def col(bit):
        return (d + 2 * (flip(q, bit) - q), z)

    def masked(owner, s):
        for k in BITS:
            if s & k:
                owner = flip(owner, k)
        return owner

    xpeer, ypeer = col(1), col(2)
    micro, width, tok = XS.shape
    row = 4 * tok
    half = row // 2
    local_width = O.shape[1]
    ff = Z.shape[1]
    heads = local_width // HD
    scale = HD ** (-0.5)
    counts = dict(r=0, l=0)
    pending = []

    def rcopy(src, dst, peer):
        i = counts["r"]
        counts["r"] = i + 1
        assert i < NSEM
        return pltpu.make_async_remote_copy(
            src_ref=src, dst_ref=dst, send_sem=ssem.at[i], recv_sem=rsem.at[i], device_id=peer, device_id_type=MESH
        )

    def lcopy(src, dst):
        i = counts["l"]
        counts["l"] = i + 1
        return pltpu.make_async_copy(src, dst, lsem.at[i])

    def rows(start, size, step=16):
        return pl.ds(pl.multiple_of(start, step), size)

    def cols(j):
        return pl.ds(pl.multiple_of(j * tok, tok), tok)

    def swapped(*fs):
        @pl.when(sw)
        def _():
            for f in fs:
                f()

    def kept(*fs):
        @pl.when(jnp.logical_not(sw))
        def _():
            for f in fs:
                f()

    barrier = pltpu.get_barrier_semaphore()
    peers = (core, zpeer, sigma, xpeer, ypeer)
    for p in peers:
        pl.semaphore_signal(barrier, 1, device_id=p, device_id_type=MESH)
    pl.semaphore_wait(barrier, len(peers))

    class Gather:
        def __init__(self, view):
            self.own = view(b)
            self.cz = rcopy(view(b), view(b), zpeer)
            self.cc = rcopy(view(b), view(b), core)
            far = 1 - zl + 2 * c
            self.cf = rcopy(view(far), view(far), core)

        def start(self):
            self.cz.start()
            self.cc.start()

        def forward(self):
            self.cz.wait_recv()
            self.cf.start()

        def finish(self):
            self.cc.wait_recv()
            self.cf.wait_recv()
            pending.extend([self.cz, self.cc, self.cf])

    def gather_rows(ref, m):
        return Gather(lambda j: ref.at[m * 4 + j])

    class Scatter:
        def __init__(self, s):
            self.s = s
            self.c1 = rcopy(S1.at[s], R1.at[s], core)
            self.c2 = rcopy(S2.at[s], R2.at[s], core)
            self.cz = rcopy(SZ.at[s], RZ.at[s], zpeer)

        def start(self, term):
            s = self.s
            away = 1 - zl
            part = term(away + 2 * (1 - c), away + 2 * c)
            S1[s] = part[:, :tok].astype(BF)
            self.c1.start()
            keep = part[:, tok:]
            part = term(zl + 2 * (1 - c), zl + 2 * c)
            S2[s] = part[:, :tok].astype(BF)
            T2[s] = part[:, tok:]
            self.c2.start()
            self.c1.wait_recv()
            SZ[s] = (keep + R1[s].astype(F32)).astype(BF)
            self.cz.start()

        def finish(self):
            s = self.s
            self.c2.wait_recv()
            self.cz.wait_recv()
            total = T2[s] + R2[s].astype(F32) + RZ[s].astype(F32)
            for cp in (self.c1, self.c2, self.cz):
                cp.wait_send()
            return total

    class Weight:
        def __init__(self, hbm, end, ref, n):
            self.ref = ref
            self.ch = ch = ref.shape[0] // COLS
            self.whole = hbm.shape[0] if end is None else (COLS - 1) * ch
            self.locals = [lcopy(hbm.at[0 : self.whole], ref.at[0 : self.whole])]
            if end is not None:
                self.locals.append(lcopy(end, ref.at[self.whole : self.whole + ch]))
            self.hops = []
            for off, size, order, _ in parts_of(ch, n):
                i = counts["r"]
                counts["r"] = i + 1

                def first(src, at, i=i):
                    return pltpu.make_async_remote_copy(
                        src_ref=src, dst_ref=ref.at[at], send_sem=ssem.at[i], recv_sem=rsem.at[i],
                        device_id=sigma, device_id_type=MESH,
                    )

                at = rows(q * ch + off, size)
                usual = first(hbm.at[at], at)
                if end is None:
                    last_at = (COLS - 1) * ch + off
                    last_size = max(0, min(size, self.whole - last_at))
                    at = slice(last_at, last_at + last_size)
                    last = first(hbm.at[at], at) if last_size else None
                else:
                    at = slice(self.whole + off, self.whole + off + size)
                    last = first(end.at[off : off + size], at)
                steps, done = [], [0]
                for bit in order:
                    copies = []
                    for s in done:
                        at = rows(masked(q, s) * ch + off, size)
                        copies.append(rcopy(ref.at[at], ref.at[at], col(bit)))
                    steps.append(copies)
                    done = done + [s | bit for s in done]
                self.hops.append(((usual, last), steps))

        def first(self, hop, act):
            usual, last = hop[0]
            pl.when(q < COLS - 1)(lambda: act(usual))
            if last is not None:
                pl.when(q == COLS - 1)(lambda: act(last))

        def load(self):
            kept(*[cp.start for cp in self.locals])

        def pass_on(self, h, j):
            if j == 0:
                self.first(h, lambda cp: cp.wait_recv())
            else:
                for cp in h[1][j - 1]:
                    cp.wait_recv()
            for cp in h[1][j]:
                cp.start()

        def finish(self):
            def go():
                for h in self.hops:
                    for cp in h[1][-1]:
                        cp.wait_recv()

            swapped(go)
            kept(*[cp.wait for cp in self.locals])

        def sent(self):
            def go():
                for h in self.hops:
                    self.first(h, lambda cp: cp.wait_send())
                    for copies in h[1]:
                        for cp in copies:
                            cp.wait_send()

            swapped(go)

    class Piece:
        def __init__(self, ref, recv, far, near, hbm, off, size, order, fin):
            self.ref, self.recv, self.far, self.near, self.hbm = ref, recv, far, near, hbm
            self.off, self.size, self.fin = off, size, fin
            self.ch = recv.shape[1]
            self.place = slice(off, off + size)
            base, self.sums = 0, []
            for j, bit in enumerate(order):
                rest = [0]
                for k in order[j + 1 :]:
                    rest = rest + [s | k for s in rest]
                copies = []
                for i, s in enumerate(rest):
                    mine = masked(q, s)
                    slot = recv.at[base + i, self.place]
                    copies.append((mine, base + i, rcopy(ref.at[self.at(flip(mine, bit))], slot, col(bit))))
                base += len(rest)
                self.sums.append(copies)
            own, out = ref.at[self.at(q)], hbm.at[self.at(q)]
            self.trade = rcopy(own, far.at[self.place], sigma)
            self.join = rcopy(own, near.at[self.place], core)
            self.own = lcopy(own, out)
            self.own_core = rcopy(own, out, core)
            done, self.spreads = [0], []
            for bit in order:
                copies = []
                for s in done:
                    owner = masked(q, s)
                    src = own if s == 0 else hbm.at[self.at(owner)]
                    got = hbm.at[self.at(flip(owner, bit))]
                    copies.append((rcopy(src, hbm.at[self.at(owner)], col(bit)), rcopy(got, got, core)))
                self.spreads.append(copies)
                done = done + [s | bit for s in done]
            self.steps = [self.send_first, self.add_send, self.add_trade, self.take_join, self.join_spread]
            self.steps += [functools.partial(self.spread, j) for j in range(len(self.spreads))]
            self.done = 0

        def at(self, owner):
            return rows(owner * self.ch + self.off, self.size)

        def run(self, upto):
            while self.done < min(upto, len(self.steps)):
                self.steps[self.done]()
                self.done += 1

        def add(self, j):
            for mine, slot, cp in self.sums[j]:
                cp.wait_recv()
                r = self.at(mine)
                total = self.ref[r, :].astype(F32) + self.recv[slot, self.place].astype(F32)
                self.ref[r, :] = total.astype(BF)
                pending.append(cp)

        def send_first(self):
            for _, _, cp in self.sums[0]:
                cp.start()

        def add_send(self):
            self.add(0)
            for _, _, cp in self.sums[1]:
                cp.start()

        def add_trade(self):
            self.add(1)
            swapped(self.trade.start)

        def take_join(self):
            def go():
                self.trade.wait()
                self.ref[self.at(q), :] = self.far[self.place]

            swapped(go)
            pl.when(c != self.fin)(self.join.start)

        def join_spread(self):
            def take():
                self.join.wait_recv()
                r = self.at(q)
                total = self.ref[r, :].astype(F32) + self.near[self.place].astype(F32)
                self.ref[r, :] = total.astype(BF)
                for cp, _ in self.spreads[0]:
                    cp.start()
                self.own_core.start()
                self.own.start()

            pl.when(c == self.fin)(take)

        def spread(self, j):
            def go():
                for cp, _ in self.spreads[j]:
                    cp.wait_recv()
                if j + 1 < len(self.spreads):
                    for cp, _ in self.spreads[j + 1]:
                        cp.start()
                for _, cp in self.spreads[j]:
                    cp.start()

            pl.when(c == self.fin)(go)

        def finish(self):
            def owner():
                self.own.wait()
                self.own_core.wait_send()
                for copies in self.spreads:
                    for a, f in copies:
                        a.wait_send()
                        f.wait_send()

            def other():
                self.join.wait_send()
                self.own_core.wait_recv()
                for copies in self.spreads:
                    for _, f in copies:
                        f.wait_recv()

            pl.when(c == self.fin)(owner)
            pl.when(c != self.fin)(other)

    def pieces(ref, recv, far, near, hbm, n):
        return [Piece(ref, recv, far, near, hbm, *p) for p in parts_of(recv.shape[1], n)]

    def wave(group, last):
        first = min(p.done for p in group)
        for t in range(first, last + len(group)):
            for i, p in enumerate(group):
                p.run(min(last, t - i + 1))

    tail_q, tail_o = WQ.shape[0] // COLS, WO.shape[0] // COLS
    wq = Weight(wq_hbm, ends.at[0:tail_q], WQ, 4)
    wo = Weight(wo_hbm, ends.at[tail_q : tail_q + tail_o], WO, 2)
    wu, wd = Weight(wu_hbm, None, WU, 4), Weight(wd_hbm, None, WD, 4)
    other_b = zl + 2 * (1 - c)
    x_swap = [rcopy(x_hbm.at[m], XS.at[m], sigma) for m in range(micro)]
    x_load = [lcopy(x_hbm.at[m], XS.at[m]) for m in range(micro)]
    c_swap = [rcopy(c_hbm.at[m], CS.at[m], sigma) for m in range(micro)]
    c_load = [lcopy(c_hbm.at[m], CS.at[m]) for m in range(micro)]
    lab_swap = rcopy(seg_ref, LAB.at[other_b], sigma)
    lab_gather = Gather(lambda j: LAB.at[j])
    a1_gather = [gather_rows(A1, m) for m in range(micro)]
    gb_gather = [gather_rows(GB, m) for m in range(micro)]
    a2_gather = [gather_rows(A2, m) for m in range(micro)]
    dhb_gather = [gather_rows(DHB, m) for m in range(micro)]
    attn_sum = [Scatter(2 * m) for m in range(micro)]
    mid_sum = [Scatter(2 * m) for m in range(micro)]
    y_sum = [Scatter(2 * m + 1) for m in range(micro)]
    in_sum = [Scatter(2 * m) for m in range(micro)]
    gd = pieces(GD, RD, SD, KD, gd_hbm, 2)
    gu = pieces(GU, RU, SU, KU, gu_hbm, 2)
    gq = pieces(WU, RQ, SQ, KQ, gq_hbm, 4)
    go = pieces(WD, RO, SO, KO, go_hbm, 2)
    out_swap = [rcopy(OB.at[m], out_hbm.at[m], sigma) for m in range(micro)]
    out_keep = [lcopy(OB.at[m], out_hbm.at[m]) for m in range(micro)]
    ig_swap = [rcopy(XS.at[m], CS.at[m], sigma) for m in range(micro)]
    ig_keep = [lcopy(DH.at[m], ig_hbm.at[m]) for m in range(micro)]
    sum_copies = [rcopy(NG, NR.at[i], p) for i, p in enumerate(peers)]

    def widen():
        for i, ref in enumerate((n1g, n1b, n2g, n2b)):
            NW[i] = jnp.transpose(jnp.broadcast_to(ref[...].reshape(1, width), (tok, width)))

    def first_norm(m):
        swapped(x_swap[m].wait_recv)
        kept(x_load[m].wait)
        xhat, _ = normed(XS[m].astype(F32))
        A1[m * 4 + b] = (xhat * NW[0] + NW[1]).astype(BF)
        a1_gather[m].start()

    def loss_grad(m):
        swapped(c_swap[m].wait_recv)
        kept(c_load[m].wait)
        labels = LAB[b]
        live = (labels[m : m + 1, :] >= 0).astype(F32)
        GB[m * 4 + b] = (CS[m].astype(F32) * live).astype(BF)
        gb_gather[m].start()

    def labels_wide():
        for m in range(micro):
            for j in range(4):
                lab = LAB[j, m : m + 1, :].astype(F32)
                LT[m, j * tok : (j + 1) * tok, :] = jnp.transpose(jnp.broadcast_to(lab, (tok, tok)))

    def make_bias(m):
        for j in range(4):
            lab = LAB[j, m : m + 1, :].astype(F32)
            place_k = lax.broadcasted_iota(jnp.int32, (row, tok), 0)
            place_q = lax.broadcasted_iota(jnp.int32, (row, tok), 1) + j * tok
            ok = (LT[m] == lab) & (place_k <= place_q)
            BIAS[:, j * tok : (j + 1) * tok] = jnp.where(ok, 0.0, -1e30)

    def whole(ref, m):
        return jnp.concatenate([ref[m * 4 + j] for j in range(4)], axis=1)

    def both(ref):
        return jnp.concatenate([ref[j] for j in range(ref.shape[0])], axis=1)

    def pair(ref, m, i, j):
        return jnp.concatenate([ref[m, :, cols(i)], ref[m, :, cols(j)]], axis=1)

    def project(m):
        QKV[m] = dg(WQ[0 : 3 * local_width, :], whole(A1, m), NN).astype(BF)

    def head_slices(h, qb):
        e = [slice(i * local_width + h * HD, i * local_width + (h + 1) * HD) for i in range(3)]
        return slice(qb * half, (qb + 1) * half), slice(0, (qb + 1) * half), *e

    def attend(m):
        for h in range(heads):
            for qb, PB in ((0, PB0), (1, PB1)):
                at, upto, eq, ek, ev = head_slices(h, qb)
                s = dg(QKV[m, ek, upto], QKV[m, eq, at], TN) * scale + BIAS[upto, at]
                e = jnp.exp(s - jnp.max(s, axis=0, keepdims=True))
                p = (e * (1.0 / jnp.sum(e, axis=0, keepdims=True))).astype(BF)
                PB[m, h] = p
                O[m, eq, at] = dg(QKV[m, ev, upto], p, NN).astype(BF)

    def heads_back(m):
        DO[m] = dg(WO[0:local_width, :], whole(DHB, m), NN).astype(BF)
        for h in range(heads):
            for qb, PB in ((1, PB1), (0, PB0)):
                at, upto, eq, ek, ev = head_slices(h, qb)
                qv, do, pb, kv = QKV[m, eq, at], DO[m, eq, at], PB[m, h], QKV[m, ek, upto]
                p = pb.astype(F32)
                pdp = p * dg(QKV[m, ev, upto], do, TN)
                ds = (pdp - p * jnp.sum(pdp, axis=0, keepdims=True)).astype(BF)
                dq = (dg(kv, ds, NN) * scale).astype(BF)
                dk, dv = dg(qv, ds, NT), dg(do, pb, NT)
                if qb == 1:
                    dq1, dk1, dv1, at1 = dq, dk, dv, at
                else:
                    QKV[m, eq, at] = dq
                    QKV[m, eq, at1] = dq1
                    QKV[m, ek, at] = ((dk1[:, :half] + dk) * scale).astype(BF)
                    QKV[m, ek, at1] = (dk1[:, half:] * scale).astype(BF)
                    QKV[m, ev, at] = (dv1[:, :half] + dv).astype(BF)
                    QKV[m, ev, at1] = dv1[:, half:].astype(BF)

    def second_norm(m, total):
        h = XS[m].astype(F32) + total
        HS[m] = h
        xhat, _ = normed(h)
        A2[m * 4 + b] = (xhat * NW[2] + NW[3]).astype(BF)
        a2_gather[m].start()

    def up(m):
        U[...] = dg(WU[0:width, :], whole(A2, m), TN)
        c0 = 0.7978845608028654
        step = 32

        def body(i, carry):
            r = rows(i * step, step, step)
            u = U[r, :]
            u2 = u * u
            t = jnp.tanh(c0 * u * (1.0 + 0.044715 * u2))
            hp = 0.5 * (1.0 + t)
            Z[m, r, :] = (u * hp).astype(BF)
            GP[m, r, :] = (hp + (0.5 * c0) * u * (1.0 - t * t) * (1.0 + (3 * 0.044715) * u2)).astype(BF)
            return carry

        lax.fori_loop(0, ff // step, body, 0)

    def down_back(m):
        dz = dg(WD[0:ff, :], whole(GB, m), NN)
        GP[m] = (dz * GP[m].astype(F32)).astype(BF)

    def over_tokens(v):
        ones = jnp.ones((8, tok), BF)
        high = v.astype(BF)
        low = (v - high.astype(F32)).astype(BF)
        return (dg(ones, high, NT) + dg(ones, low, NT))[0:1, :]

    def norm_back(v, gain, grad, i):
        xhat, rstd = normed(v)
        dn = grad * gain
        dv = rstd * (
            dn - jnp.mean(dn, axis=0, keepdims=True) - xhat * jnp.mean(dn * xhat, axis=0, keepdims=True)
        )
        return dv, grad * xhat

    def second_norm_back(m, total):
        dv, gains = norm_back(HS[m], NW[2], total, 2)
        dh = GB[m * 4 + b].astype(F32) + dv
        DH[m] = dh
        DHB[m * 4 + b] = dh.astype(BF)
        dhb_gather[m].start()
        NG[2:3, :] += over_tokens(gains)
        NG[3:4, :] += over_tokens(total)

    def first_norm_back(m, total):
        dv, gains = norm_back(XS[m].astype(F32), NW[0], total, 0)
        dx = DH[m] + dv
        DH[m] = dx

        @pl.when(sw)
        def _():
            XS[m] = dx.astype(BF)
            ig_swap[m].start()

        kept(ig_keep[m].start)
        NG[0:1, :] += over_tokens(gains)
        NG[1:2, :] += over_tokens(total)

    def out_term(m):
        return lambda i, j: dg(WO[0:local_width, :], pair(O, m, i, j), TN)

    def y_term(m):
        return lambda i, j: dg(WD[0:ff, :], pair(Z, m, i, j), TN)

    def mid_term(m):
        return lambda i, j: dg(WU[0:width, :], pair(GP, m, i, j), NN)

    def in_term(m):
        return lambda i, j: dg(WQ[0 : 3 * local_width, :], pair(QKV, m, i, j), TN)

    def give_output(m):
        OB[m] = (HS[m] + y_sum[m].finish()).astype(BF)
        swapped(out_swap[m].start)
        kept(out_keep[m].start)

    def sum_add(i):
        sum_copies[i].wait()
        NG[...] = NG[...] + NR[i]

    def begin(w, i):
        swapped(lambda: w.first(w.hops[i], lambda cp: cp.start()))

    def hop(w, i, j):
        swapped(lambda: w.pass_on(w.hops[i], j))

    swapped(lab_swap.start, x_swap[0].start)
    begin(wq, 0)
    begin(wq, 1)
    kept(*[cp.start for cp in x_load])
    for w in (wq, wo, wu, wd):
        w.load()
    kept(*[cp.start for cp in c_load])

    @pl.when(jnp.logical_not(sw))
    def _():
        LAB[b] = seg_ref[...]

    NG[...] = jnp.zeros_like(NG)
    widen()
    swapped(lab_swap.wait_recv)
    lab_gather.start()
    first_norm(0)
    begin(wq, 2)
    kept(lambda: first_norm(1))
    lab_gather.forward()
    hop(wq, 0, 0)
    begin(wq, 3)
    a1_gather[0].forward()
    hop(wq, 1, 0)
    begin(wo, 0)
    hop(wq, 0, 1)
    lab_gather.finish()
    labels_wide()
    make_bias(0)
    hop(wq, 2, 0)
    begin(wo, 1)
    hop(wq, 1, 1)
    hop(wq, 3, 0)
    swapped(x_swap[1].start)
    hop(wq, 2, 1)
    hop(wo, 0, 0)
    begin(wu, 0)
    hop(wq, 3, 1)
    hop(wo, 1, 0)
    begin(wu, 1)
    a1_gather[0].finish()
    kept(lambda: loss_grad(0), lambda: loss_grad(1))
    wq.finish()

    project(0)
    hop(wo, 0, 1)
    hop(wo, 1, 1)
    attend(0)
    swapped(lambda: first_norm(1))
    begin(wu, 2)
    wo.finish()
    attn_sum[0].start(out_term(0))
    hop(wu, 0, 0)
    begin(wu, 3)
    a1_gather[1].forward()
    hop(wu, 1, 0)
    swapped(c_swap[0].start)
    hop(wu, 0, 1)
    make_bias(1)
    a1_gather[1].finish()
    project(1)
    hop(wu, 2, 0)
    swapped(c_swap[1].start)
    hop(wu, 1, 1)
    attend(1)
    attn_sum[1].start(out_term(1))
    hop(wu, 3, 0)
    begin(wd, 0)
    hop(wu, 2, 1)
    second_norm(0, attn_sum[0].finish())
    swapped(lambda: loss_grad(0))
    begin(wd, 1)
    hop(wu, 3, 1)
    second_norm(1, attn_sum[1].finish())
    a2_gather[0].forward()
    swapped(lambda: loss_grad(1))
    begin(wd, 2)
    wu.finish()
    a2_gather[0].finish()
    up(0)
    hop(wd, 0, 0)
    begin(wd, 3)
    a2_gather[1].forward()
    hop(wd, 1, 0)
    hop(wd, 0, 1)
    a2_gather[1].finish()
    up(1)
    gb_gather[0].forward()
    hop(wd, 2, 0)
    hop(wd, 1, 1)
    gb_gather[1].forward()
    hop(wd, 3, 0)
    hop(wd, 2, 1)
    gb_gather[0].finish()
    gb_gather[1].finish()
    hop(wd, 3, 1)
    GD[0:ff, :] = dg(jnp.concatenate([Z[m] for m in range(micro)], axis=1), both(GB), NT).astype(BF)
    GD[ff:, :] = jnp.zeros((GD.shape[0] - ff, width), BF)
    wd.finish()
    wave(gd, 1)

    down_back(0)
    mid_sum[0].start(mid_term(0))
    down_back(1)
    mid_sum[1].start(mid_term(1))
    GU[0:width, :] = dg(both(A2), jnp.concatenate([GP[m] for m in range(micro)], axis=1), NT).astype(BF)
    GU[width:, :] = jnp.zeros((GU.shape[0] - width, ff), BF)
    second_norm_back(0, mid_sum[0].finish())
    wave(gd, 2)
    wave(gu, 1)
    second_norm_back(1, mid_sum[1].finish())
    for w in (wq, wo, wu, wd):
        w.sent()
    dhb_gather[0].forward()
    wave(gd, 3)
    dhb_gather[0].finish()
    heads_back(0)
    dhb_gather[1].forward()
    in_sum[0].start(in_term(0))
    wave(gu, 2)
    dhb_gather[1].finish()
    heads_back(1)
    in_sum[1].start(in_term(1))
    three = 3 * local_width
    WU[0:three, :] = dg(jnp.concatenate([QKV[m] for m in range(micro)], axis=1), both(A1), NT).astype(BF)
    WU[three : gq[0].ch * COLS, :] = jnp.zeros((gq[0].ch * COLS - three, width), BF)
    wave(gq, 1)
    wave(gu, 3)
    y_sum[0].start(y_term(0))
    y_sum[1].start(y_term(1))
    WD[0:local_width, :] = dg(jnp.concatenate([O[m] for m in range(micro)], axis=1), both(DHB), NT).astype(BF)
    WD[local_width : go[0].ch * COLS, :] = jnp.zeros((go[0].ch * COLS - local_width, width), BF)
    wave(go, 1)
    wave(gd, 4)
    first_norm_back(0, in_sum[0].finish())
    wave(gd, 5)
    first_norm_back(1, in_sum[1].finish())
    sum_copies[0].start()
    wave(gq, 2)
    wave(go, 2)
    wave(gd, 6)
    for m in range(micro):
        give_output(m)
    wave(go, 3)
    sum_add(0)
    sum_copies[1].start()
    wave(gu, 4)
    wave(gd, 7)
    wave(gq, 3)
    wave(gu, 5)
    sum_add(1)
    sum_copies[2].start()
    wave(go, 5)
    wave(gu, 6)
    wave(gq, 5)
    sum_add(2)
    sum_copies[3].start()
    wave(go, 6)
    wave(gu, 7)
    wave(gq, 6)
    sum_add(3)
    sum_copies[4].start()
    wave(go, 7)
    wave(gq, 7)
    sum_add(4)
    ng_ref[...] = NG[...]
    for m in range(micro):

        @pl.when(sw)
        def _():
            ig_swap[m].wait()
            DH[m] = CS[m].astype(F32)
            ig_keep[m].start()
            out_swap[m].wait()
            x_swap[m].wait_send()
            c_swap[m].wait_send()

        ig_keep[m].wait()
        kept(out_keep[m].wait)
    swapped(lab_swap.wait_send)
    for cp in pending:
        cp.wait_send()
    for p in gd + gu + gq + go:
        p.finish()


def layer(
    inputs, segments, norm1_gain, norm1_bias, qkv_weight, out_weight, norm2_gain, norm2_bias, up_weight, down_weight,
    cotangent,
):
    micro, tok, width = inputs.shape
    local_width = qkv_weight.shape[2]
    ff = up_weight.shape[1]
    row = 4 * tok
    heads = local_width // HD
    three = 3 * local_width
    half = row // 2
    cq, co, cu, cd = chunk_rows(three), chunk_rows(local_width), chunk_rows(width), chunk_rows(ff)
    wq = jnp.transpose(qkv_weight, (0, 2, 1)).reshape(three, width)

    def tail(w, ch):
        rest = w[(COLS - 1) * ch :]
        return [rest, jnp.zeros((ch - rest.shape[0], width), BF)]

    ends = jnp.concatenate(tail(wq, cq) + tail(out_weight, co), axis=0)

    def v(shape, dtype=BF):
        return pltpu.VMEM(shape, dtype)

    def recv(ch, lanes):
        return v((COLS - 1, ch, lanes))

    any_spec = pl.BlockSpec(memory_space=pl.ANY)
    vmem = pl.BlockSpec(memory_space=pltpu.VMEM)
    block = (width, tok)
    scratch = [
        v((COLS * cq, width)), v((COLS * co, width)), v((COLS * cu, ff)), v((COLS * cd, width)),
        v((COLS * cu, ff)), v((COLS * cd, width)),
        recv(cq, width), recv(co, width), recv(cu, ff), recv(cd, width),
        v((cq, width)), v((co, width)), v((cu, ff)), v((cd, width)),
        v((cq, width)), v((co, width)), v((cu, ff)), v((cd, width)),
        v((micro, *block)), v((micro, *block)), v((4, micro, tok), jnp.int32), v((micro, row, tok), F32),
        v((row, row), F32), v((4, *block), F32),
        v((4 * micro, *block)), v((micro, three, row)),
        v((micro, heads, half, half)), v((micro, heads, row, half)), v((micro, local_width, row)),
        v((micro, *block), F32),
        v((4 * micro, *block)), v((micro, ff, row)), v((micro, ff, row)), v((4 * micro, *block)),
        v((4 * micro, *block)), v((micro, local_width, row)), v((micro, *block), F32), v((ff, row), F32),
        v((2 * micro, *block), F32),
        *[v((2 * micro, *block)) for _ in range(6)],
        v((micro, *block)),
        v((8, width), F32), v((5, 8, width), F32),
        pltpu.SemaphoreType.DMA((NSEM,)), pltpu.SemaphoreType.DMA((NSEM,)), pltpu.SemaphoreType.DMA((40,)),
    ]
    out, input_grad, gq, go, gu, gd, ng = pl.pallas_call(
        kernel,
        out_shape=[
            jax.ShapeDtypeStruct((micro, *block), BF),
            jax.ShapeDtypeStruct((micro, *block), F32),
            jax.ShapeDtypeStruct((COLS * cq, width), BF),
            jax.ShapeDtypeStruct((COLS * co, width), BF),
            jax.ShapeDtypeStruct((COLS * cu, ff), BF),
            jax.ShapeDtypeStruct((COLS * cd, width), BF),
            jax.ShapeDtypeStruct((8, width), F32),
        ],
        in_specs=[any_spec, vmem, vmem, vmem] + [any_spec] * 3 + [vmem, vmem] + [any_spec] * 3,
        out_specs=[any_spec] * 6 + [vmem],
        scratch_shapes=scratch,
        compiler_params=pltpu.CompilerParams(
            collective_id=0, has_side_effects=True, vmem_limit_bytes=64 * 1024 * 1024
        ),
    )(
        jnp.transpose(inputs, (0, 2, 1)), segments, norm1_gain, norm1_bias,
        wq, out_weight, ends, norm2_gain, norm2_bias, up_weight, down_weight,
        jnp.transpose(cotangent, (0, 2, 1)),
    )
    grads = (
        jnp.transpose(gq[:three].astype(F32).reshape(3, local_width, width), (0, 2, 1)),
        go[:local_width].astype(F32),
        gu[:width].astype(F32),
        gd[:ff].astype(F32),
    )
    extent = lax.axis_size("dp")
    block = 2 * COLS
    if extent > block:
        groups = [[r + block * j for j in range(extent // block)] for r in range(block)]
        grads = lax.psum(grads, "dp", axis_index_groups=groups)
        ng = lax.psum(ng, "dp", axis_index_groups=groups)
    gq, go, gu, gd = grads
    out, input_grad = jnp.transpose(out, (0, 2, 1)), jnp.transpose(input_grad, (0, 2, 1))
    return out, input_grad, ng[0], ng[1], gq, go, ng[2], ng[3], gu, gd


def solution(mesh):
    tokens = P(None, ("dp", "tensor"), None)
    weights = (P(None, None, "tensor"), P("tensor", None))
    mlp = (P(None, "tensor"), P("tensor", None))
    return jax.shard_map(
        layer,
        mesh=mesh,
        in_specs=(tokens, P(None, ("dp", "tensor")), P(), P(), *weights, P(), P(), *mlp, tokens),
        out_specs=(tokens, tokens, P(), P(), *weights, P(), P(), *mlp),
        check_vma=False,
    )
```

```python
import functools

import jax
import jax.numpy as jnp
from jax import lax
from jax.experimental import pallas as pl
from jax.experimental.pallas import tpu as pltpu
from jax.sharding import PartitionSpec as P


HD = 56
BF = jnp.bfloat16
F32 = jnp.float32
MESH = pl.DeviceIdType.MESH
NN = (((1,), (0,)), ((), ()))
NT = (((1,), (1,)), ((), ()))
TN = (((0,), (0,)), ((), ()))
COLS = 4
BITS = (1, 2)
NSEM = 241


def up_to(n, m):
    return -(-n // m) * m


def chunk_rows(rows):
    return up_to(-(-rows // COLS), 16)


def parts_of(ch, n):
    out, off = [], 0
    for i in range(n):
        size = up_to(-(-(ch - off) // (n - i)), 16)
        out.append((off, size, BITS if i % 2 == 0 else BITS[::-1], i % 2))
        off += size
    return out


def dg(a, b, dims):
    return lax.dot_general(a, b, dims, preferred_element_type=F32)


def normed(v):
    center = v - jnp.mean(v, axis=0, keepdims=True)
    rstd = lax.rsqrt(jnp.mean(center * center, axis=0, keepdims=True) + 1e-05)
    return center * rstd, rstd


def kernel(
    x_hbm, seg_ref, n1g, n1b, wq_hbm, wq_end, wo_hbm, n2g, n2b, wu_hbm, wd_hbm, c_hbm,
    out_hbm, ig_hbm, gq_hbm, go_hbm, gu_hbm, gd_hbm, ng_ref,
    WQ, WO, WU, WD, GU, GD, RQ, RO, RU, RD, SQ, SO, SU, SD, KQ, KO, KU, KD,
    XS, CS, LAB, LT, BIAS, NW, A1, QKV, PB0, PB1, O, HS, A2, Z, GP, GB, DHB, DO, DH, U,
    T2, S1, SZ, R1, RZ, OB, NG, NR,
    ssem, rsem, lsem,
):
    d = lax.axis_index("dp")
    z = lax.axis_index("tensor")
    c = lax.rem(d, 2)
    q = lax.rem(d // 2, COLS)
    zl = lax.rem(z, 2)
    zh = z // 2
    b = zl + 2 * c
    sw = zh != c
    dc = d + 1 - 2 * c
    z1 = z + 1 - 2 * zl
    z2 = z + 2 - 4 * zh
    core = (dc, z)
    zpeer = (d, z1)
    sigma = (dc, z2)

    def flip(owner, bit):
        on = lax.rem(owner // bit, 2)
        return owner + bit * (1 - 2 * on)

    def col(bit):
        return (d + 2 * (flip(q, bit) - q), z)

    def masked(owner, s):
        for k in BITS:
            if s & k:
                owner = flip(owner, k)
        return owner

    xpeer, ypeer = col(1), col(2)
    micro, width, tok = XS.shape
    row = 4 * tok
    half = row // 2
    local_width = O.shape[1]
    ff = Z.shape[1]
    heads = local_width // HD
    scale = HD ** (-0.5)
    counts = dict(r=0, l=0)
    pending = []

    def rcopy(src, dst, peer):
        i = counts["r"]
        counts["r"] = i + 1
        assert i < NSEM
        return pltpu.make_async_remote_copy(
            src_ref=src, dst_ref=dst, send_sem=ssem.at[i], recv_sem=rsem.at[i], device_id=peer, device_id_type=MESH
        )

    def lcopy(src, dst):
        i = counts["l"]
        counts["l"] = i + 1
        return pltpu.make_async_copy(src, dst, lsem.at[i])

    def rows(start, size, step=16):
        return pl.ds(pl.multiple_of(start, step), size)

    def cols(j):
        return pl.ds(pl.multiple_of(j * tok, tok), tok)

    def swapped(*fs):
        @pl.when(sw)
        def _():
            for f in fs:
                f()

    def kept(*fs):
        @pl.when(jnp.logical_not(sw))
        def _():
            for f in fs:
                f()

    barrier = pltpu.get_barrier_semaphore()
    peers = (core, zpeer, sigma, xpeer, ypeer)
    for p in peers:
        pl.semaphore_signal(barrier, 1, device_id=p, device_id_type=MESH)
    pl.semaphore_wait(barrier, len(peers))

    class Gather:
        def __init__(self, view):
            self.own = view(b)
            self.cz = rcopy(view(b), view(b), zpeer)
            self.cc = rcopy(view(b), view(b), core)
            far = 1 - zl + 2 * c
            self.cf = rcopy(view(far), view(far), core)

        def start(self):
            self.cz.start()
            self.cc.start()

        def forward(self):
            self.cz.wait_recv()
            self.cf.start()

        def finish(self):
            self.cc.wait_recv()
            self.cf.wait_recv()
            pending.extend([self.cz, self.cc, self.cf])

    def gather_rows(ref, m):
        return Gather(lambda j: ref.at[m * 4 + j])

    class Scatter:
        def __init__(self, s):
            self.s = s
            self.idx = counts["r"]
            counts["r"] += 2
            self.cz = rcopy(SZ.at[s], RZ.at[s], zpeer)

        def give(self, i):
            return pltpu.make_async_remote_copy(
                src_ref=S1.at[self.s, i], dst_ref=R1.at[self.s, i], send_sem=ssem.at[self.idx + i],
                recv_sem=rsem.at[self.idx + i], device_id=core, device_id_type=MESH,
            )

        def start(self, term):
            s = self.s

            def body(i, carry):
                side = lax.rem(1 - zl + i, 2)
                part = term(side + 2 * (1 - c), side + 2 * c)
                S1[s, i] = part[:, :tok].astype(BF)
                T2[s * i + 2 * micro * (1 - i)] = part[:, tok:]
                self.give(i).start()
                return carry

            lax.fori_loop(0, 2, body, 0)
            self.give(0).wait_recv()
            SZ[s] = (T2[2 * micro] + R1[s, 0].astype(F32)).astype(BF)
            self.cz.start()

        def finish(self):
            s = self.s
            self.give(1).wait_recv()
            self.cz.wait_recv()
            total = T2[s] + R1[s, 1].astype(F32) + RZ[s].astype(F32)
            self.give(0).wait_send()
            self.give(1).wait_send()
            self.cz.wait_send()
            return total

    class Weight:
        def __init__(self, hbm, ref, n, end=None):
            ch = ref.shape[0] // COLS
            whole = hbm.shape[0] if end is None else (COLS - 1) * ch
            self.locals = [lcopy(hbm.at[0:whole], ref.at[0:whole])]
            if end is not None:
                self.locals.append(lcopy(end, ref.at[whole : whole + ch]))
            self.hops = []
            for off, size, order, _ in parts_of(ch, n):
                i = counts["r"]
                counts["r"] = i + 1

                def first(src, at, i=i):
                    return pltpu.make_async_remote_copy(
                        src_ref=src, dst_ref=ref.at[at], send_sem=ssem.at[i], recv_sem=rsem.at[i],
                        device_id=sigma, device_id_type=MESH,
                    )

                at = rows(q * ch + off, size)
                usual = first(hbm.at[at], at)
                last_at = (COLS - 1) * ch + off
                last_size = max(0, min(size, whole - last_at))
                at = slice(last_at, last_at + last_size)
                last = usual if last_size == size else first(hbm.at[at], at) if last_size else None
                if end is not None:
                    last = first(end.at[off : off + size], slice(last_at, last_at + size))
                steps, done = [], [0]
                for bit in order:
                    copies = []
                    for s in done:
                        at = rows(masked(q, s) * ch + off, size)
                        copies.append(rcopy(ref.at[at], ref.at[at], col(bit)))
                    steps.append(copies)
                    done = done + [s | bit for s in done]
                self.hops.append(((usual, last), steps))

        def first(self, hop, act):
            usual, last = hop[0]
            if last is usual:
                act(usual)
                return
            pl.when(q < COLS - 1)(lambda: act(usual))
            if last is not None:
                pl.when(q == COLS - 1)(lambda: act(last))

        def load(self):
            kept(*[cp.start for cp in self.locals])

        def pass_on(self, h, j):
            if j == 0:
                self.first(h, lambda cp: cp.wait_recv())
            else:
                for cp in h[1][j - 1]:
                    cp.wait_recv()
            for cp in h[1][j]:
                cp.start()

        def finish(self):
            def go():
                for h in self.hops:
                    for cp in h[1][-1]:
                        cp.wait_recv()

            swapped(go)
            kept(*[cp.wait for cp in self.locals])

        def sent(self):
            def go():
                for h in self.hops:
                    self.first(h, lambda cp: cp.wait_send())
                    for copies in h[1]:
                        for cp in copies:
                            cp.wait_send()

            swapped(go)

    class Piece:
        def __init__(self, ref, recv, far, near, hbm, off, size, order, fin):
            self.ref, self.recv, self.far, self.near, self.hbm = ref, recv, far, near, hbm
            self.off, self.size, self.fin = off, size, fin
            self.ch = recv.shape[1]
            self.place = slice(off, off + size)
            base, self.sums = 0, []
            for j, bit in enumerate(order):
                rest = [0]
                for k in order[j + 1 :]:
                    rest = rest + [s | k for s in rest]
                copies = []
                for i, s in enumerate(rest):
                    mine = masked(q, s)
                    slot = recv.at[base + i, self.place]
                    copies.append((mine, base + i, rcopy(ref.at[self.at(flip(mine, bit))], slot, col(bit))))
                base += len(rest)
                self.sums.append(copies)
            own, out = ref.at[self.at(q)], hbm.at[self.at(q)]
            self.trade = rcopy(own, far.at[self.place], sigma)
            self.join = rcopy(own, near.at[self.place], core)
            self.own = lcopy(own, out)
            self.own_core = rcopy(own, out, core)
            done, self.spreads = [0], []
            for bit in order:
                copies = []
                for s in done:
                    owner = masked(q, s)
                    src = own if s == 0 else hbm.at[self.at(owner)]
                    got = hbm.at[self.at(flip(owner, bit))]
                    copies.append((rcopy(src, hbm.at[self.at(owner)], col(bit)), rcopy(got, got, core)))
                self.spreads.append(copies)
                done = done + [s | bit for s in done]
            self.steps = [self.send_first, self.add_send, self.add_trade, self.take_join, self.join_spread]
            self.steps += [functools.partial(self.spread, j) for j in range(len(self.spreads))]
            self.done = 0

        def at(self, owner):
            return rows(owner * self.ch + self.off, self.size)

        def run(self, upto):
            while self.done < min(upto, len(self.steps)):
                self.steps[self.done]()
                self.done += 1

        def by_rows(self, owner, more, plain=False):
            base = owner * self.ch + self.off

            def body(i, carry):
                r = rows(base + i * 16, 16)
                other = more[rows(self.off + i * 16, 16), :]
                if not plain:
                    other = (self.ref[r, :].astype(F32) + other.astype(F32)).astype(BF)
                self.ref[r, :] = other
                return carry

            lax.fori_loop(0, self.size // 16, body, 0)

        def add(self, j):
            for mine, slot, cp in self.sums[j]:
                cp.wait_recv()
                self.by_rows(mine, self.recv.at[slot])
                pending.append(cp)

        def send_first(self):
            for _, _, cp in self.sums[0]:
                cp.start()

        def add_send(self):
            self.add(0)
            for _, _, cp in self.sums[1]:
                cp.start()

        def add_trade(self):
            self.add(1)
            swapped(self.trade.start)

        def take_join(self):
            def go():
                self.trade.wait()
                self.by_rows(q, self.far, plain=True)

            swapped(go)
            pl.when(c != self.fin)(self.join.start)

        def join_spread(self):
            def take():
                self.join.wait_recv()
                self.by_rows(q, self.near)
                for cp, _ in self.spreads[0]:
                    cp.start()
                self.own_core.start()
                self.own.start()

            pl.when(c == self.fin)(take)

        def spread(self, j):
            def go():
                for cp, _ in self.spreads[j]:
                    cp.wait_recv()
                if j + 1 < len(self.spreads):
                    for cp, _ in self.spreads[j + 1]:
                        cp.start()
                for _, cp in self.spreads[j]:
                    cp.start()

            pl.when(c == self.fin)(go)

        def finish(self):
            def owner():
                self.own.wait()
                self.own_core.wait_send()
                for copies in self.spreads:
                    for a, f in copies:
                        a.wait_send()
                        f.wait_send()

            def other():
                self.join.wait_send()
                self.own_core.wait_recv()
                for copies in self.spreads:
                    for _, f in copies:
                        f.wait_recv()

            pl.when(c == self.fin)(owner)
            pl.when(c != self.fin)(other)

    def pieces(ref, recv, far, near, hbm, n):
        return [Piece(ref, recv, far, near, hbm, *p) for p in parts_of(recv.shape[1], n)]

    def wave(group, last):
        first = min(p.done for p in group)
        for t in range(first, last + len(group)):
            for i, p in enumerate(group):
                p.run(min(last, t - i + 1))

    wq, wo = Weight(wq_hbm, WQ, 4, wq_end), Weight(wo_hbm, WO, 2)
    wu, wd = Weight(wu_hbm, WU, 4), Weight(wd_hbm, WD, 4)
    other_b = zl + 2 * (1 - c)
    x_swap = [rcopy(x_hbm.at[m], XS.at[m], sigma) for m in range(micro)]
    x_load = [lcopy(x_hbm.at[m], XS.at[m]) for m in range(micro)]
    c_swap = [rcopy(c_hbm.at[m], CS.at[m], sigma) for m in range(micro)]
    c_load = [lcopy(c_hbm.at[m], CS.at[m]) for m in range(micro)]
    lab_swap = rcopy(seg_ref, LAB.at[other_b], sigma)
    lab_gather = Gather(lambda j: LAB.at[j])
    a1_gather = [gather_rows(A1, m) for m in range(micro)]
    gb_gather = [gather_rows(GB, m) for m in range(micro)]
    a2_gather = [gather_rows(A2, m) for m in range(micro)]
    dhb_gather = [gather_rows(DHB, m) for m in range(micro)]
    attn_sum = [Scatter(2 * m) for m in range(micro)]
    mid_sum = [Scatter(2 * m) for m in range(micro)]
    y_sum = [Scatter(2 * m + 1) for m in range(micro)]
    in_sum = [Scatter(2 * m) for m in range(micro)]
    gd = pieces(GD, RD, SD, KD, gd_hbm, 2)
    gu = pieces(GU, RU, SU, KU, gu_hbm, 2)
    gq = pieces(WU, RQ, SQ, KQ, gq_hbm, 4)
    go = pieces(WD, RO, SO, KO, go_hbm, 2)
    out_swap = [rcopy(OB.at[m], out_hbm.at[m], sigma) for m in range(micro)]
    out_keep = [lcopy(OB.at[m], out_hbm.at[m]) for m in range(micro)]
    ig_swap = [rcopy(XS.at[m], CS.at[m], sigma) for m in range(micro)]
    ig_keep = [lcopy(DH.at[m], ig_hbm.at[m]) for m in range(micro)]
    sum_copies = [rcopy(NG, NR.at[i], p) for i, p in enumerate((sigma, xpeer, ypeer, zpeer, core))]

    def widen():
        for i, ref in enumerate((n1g, n1b, n2g, n2b)):
            NW[i] = jnp.transpose(jnp.broadcast_to(ref[...].reshape(1, width), (tok, width)))

    def first_norm(m):
        swapped(x_swap[m].wait_recv)
        kept(x_load[m].wait)
        xhat, _ = normed(XS[m].astype(F32))
        A1[m * 4 + b] = (xhat * NW[0] + NW[1]).astype(BF)
        a1_gather[m].start()

    def loss_grad(m):
        swapped(c_swap[m].wait_recv)
        kept(c_load[m].wait)
        labels = LAB[b]
        live = (labels[m : m + 1, :] >= 0).astype(F32)
        GB[m * 4 + b] = (CS[m].astype(F32) * live).astype(BF)
        gb_gather[m].start()

    def labels_wide():
        for m in range(micro):
            for j in range(4):
                lab = LAB[j, m : m + 1, :].astype(F32)
                LT[m, j * tok : (j + 1) * tok, :] = jnp.transpose(jnp.broadcast_to(lab, (tok, tok)))

    def make_bias(m):
        for j in range(4):
            lab = LAB[j, m : m + 1, :].astype(F32)
            place_k = lax.broadcasted_iota(jnp.int32, (row, tok), 0)
            place_q = lax.broadcasted_iota(jnp.int32, (row, tok), 1) + j * tok
            ok = (LT[m] == lab) & (place_k <= place_q)
            BIAS[:, j * tok : (j + 1) * tok] = jnp.where(ok, 0.0, -1e30)

    def whole(ref, m):
        return jnp.concatenate([ref[m * 4 + j] for j in range(4)], axis=1)

    def both(ref):
        return jnp.concatenate([ref[j] for j in range(ref.shape[0])], axis=1)

    def pair(ref, m, i, j):
        return jnp.concatenate([ref[m, :, cols(i)], ref[m, :, cols(j)]], axis=1)

    def project(m):
        QKV[m] = dg(WQ[0 : 3 * local_width, :], whole(A1, m), NN).astype(BF)

    def head_slices(h, qb):
        e = [slice(i * local_width + h * HD, i * local_width + (h + 1) * HD) for i in range(3)]
        return slice(qb * half, (qb + 1) * half), slice(0, (qb + 1) * half), *e

    def attend(m):
        for h in range(heads):
            for qb, PB in ((0, PB0), (1, PB1)):
                at, upto, eq, ek, ev = head_slices(h, qb)
                s = dg(QKV[m, ek, upto], QKV[m, eq, at], TN) * scale + BIAS[upto, at]
                e = jnp.exp(s - jnp.max(s, axis=0, keepdims=True))
                p = (e * (1.0 / jnp.sum(e, axis=0, keepdims=True))).astype(BF)
                PB[m, h] = p
                O[m, eq, at] = dg(QKV[m, ev, upto], p, NN).astype(BF)

    def heads_back(m):
        DO[m] = dg(WO[0:local_width, :], whole(DHB, m), NN).astype(BF)
        for h in range(heads):
            for qb, PB in ((1, PB1), (0, PB0)):
                at, upto, eq, ek, ev = head_slices(h, qb)
                qv, do, pb, kv = QKV[m, eq, at], DO[m, eq, at], PB[m, h], QKV[m, ek, upto]
                p = pb.astype(F32)
                pdp = p * dg(QKV[m, ev, upto], do, TN)
                ds = (pdp - p * jnp.sum(pdp, axis=0, keepdims=True)).astype(BF)
                dq = (dg(kv, ds, NN) * scale).astype(BF)
                dk, dv = dg(qv, ds, NT), dg(do, pb, NT)
                if qb == 1:
                    dq1, dk1, dv1, at1 = dq, dk, dv, at
                else:
                    QKV[m, eq, at] = dq
                    QKV[m, eq, at1] = dq1
                    QKV[m, ek, at] = ((dk1[:, :half] + dk) * scale).astype(BF)
                    QKV[m, ek, at1] = (dk1[:, half:] * scale).astype(BF)
                    QKV[m, ev, at] = (dv1[:, :half] + dv).astype(BF)
                    QKV[m, ev, at1] = dv1[:, half:].astype(BF)

    def second_norm(m, total):
        h = XS[m].astype(F32) + total
        HS[m] = h
        xhat, _ = normed(h)
        A2[m * 4 + b] = (xhat * NW[2] + NW[3]).astype(BF)
        a2_gather[m].start()

    def up(m):
        c0 = 0.7978845608028654
        step = 32

        def side(j, carry):
            blocks = jnp.concatenate([A2[m * 4 + 2 * j], A2[m * 4 + 2 * j + 1]], axis=1)
            U[...] = dg(WU[0:width, :], blocks, TN)
            at = pl.ds(pl.multiple_of(j * half, half), half)

            def body(i, carry):
                r = rows(i * step, step, step)
                u = U[r, :]
                u2 = u * u
                t = jnp.tanh(c0 * u * (1.0 + 0.044715 * u2))
                hp = 0.5 * (1.0 + t)
                Z[m, r, at] = (u * hp).astype(BF)
                GP[m, r, at] = (hp + (0.5 * c0) * u * (1.0 - t * t) * (1.0 + (3 * 0.044715) * u2)).astype(BF)
                return carry

            return lax.fori_loop(0, ff // step, body, carry)

        lax.fori_loop(0, 2, side, 0)

    def down_back(m):
        dz = dg(WD[0:ff, :], whole(GB, m), NN)
        GP[m] = (dz * GP[m].astype(F32)).astype(BF)

    def over_tokens(v):
        ones = jnp.ones((8, tok), BF)
        high = v.astype(BF)
        low = (v - high.astype(F32)).astype(BF)
        return (dg(ones, high, NT) + dg(ones, low, NT))[0:1, :]

    def norm_back(v, gain, grad, i):
        xhat, rstd = normed(v)
        dn = grad * gain
        dv = rstd * (
            dn - jnp.mean(dn, axis=0, keepdims=True) - xhat * jnp.mean(dn * xhat, axis=0, keepdims=True)
        )
        return dv, grad * xhat

    def second_norm_back(m, total):
        dv, gains = norm_back(HS[m], NW[2], total, 2)
        dh = GB[m * 4 + b].astype(F32) + dv
        DH[m] = dh
        DHB[m * 4 + b] = dh.astype(BF)
        dhb_gather[m].start()
        NG[2:3, :] += over_tokens(gains)
        NG[3:4, :] += over_tokens(total)

    def first_norm_back(m, total):
        dv, gains = norm_back(XS[m].astype(F32), NW[0], total, 0)
        DH[m] = DH[m] + dv
        NG[0:1, :] += over_tokens(gains)
        NG[1:2, :] += over_tokens(total)

    def give_input_grad(m):
        @pl.when(sw)
        def _():
            XS[m] = DH[m].astype(BF)
            ig_swap[m].start()

        kept(ig_keep[m].start)

    def out_term(m):
        return lambda i, j: dg(WO[0:local_width, :], pair(O, m, i, j), TN)

    def y_term(m):
        return lambda i, j: dg(WD[0:ff, :], pair(Z, m, i, j), TN)

    def mid_term(m):
        return lambda i, j: dg(WU[0:width, :], pair(GP, m, i, j), NN)

    def in_term(m):
        return lambda i, j: dg(WQ[0 : 3 * local_width, :], pair(QKV, m, i, j), TN)

    def give_output(m):
        OB[m] = (HS[m] + y_sum[m].finish()).astype(BF)
        swapped(out_swap[m].start)
        kept(out_keep[m].start)

    def sum_add(i):
        sum_copies[i].wait()
        NG[...] = NG[...] + NR[i]

    def place(ref, height, value):
        n, m = value.shape
        ref[0:n, 0:m] = value.astype(BF)
        ref[n:height, :] = jnp.zeros((height - n, ref.shape[1]), BF)
        if m < ref.shape[1]:
            ref[0:n, m:] = jnp.zeros((n, ref.shape[1] - m), BF)

    def micros(ref):
        return jnp.concatenate([ref[m] for m in range(micro)], axis=1)

    def begin(w, i):
        swapped(lambda: w.first(w.hops[i], lambda cp: cp.start()))

    def hop(w, i, j):
        swapped(lambda: w.pass_on(w.hops[i], j))

    swapped(lab_swap.start, x_swap[0].start)
    begin(wq, 0)
    begin(wq, 1)
    kept(*[cp.start for cp in x_load])
    for w in (wq, wo, wu, wd):
        w.load()
    kept(*[cp.start for cp in c_load])

    @pl.when(jnp.logical_not(sw))
    def _():
        LAB[b] = seg_ref[...]

    NG[...] = jnp.zeros_like(NG)
    widen()
    swapped(lab_swap.wait_recv)
    lab_gather.start()
    first_norm(0)
    begin(wq, 2)
    kept(lambda: first_norm(1))
    lab_gather.forward()
    hop(wq, 0, 0)
    begin(wq, 3)
    a1_gather[0].forward()
    hop(wq, 1, 0)
    begin(wo, 0)
    hop(wq, 0, 1)
    lab_gather.finish()
    labels_wide()
    make_bias(0)
    hop(wq, 2, 0)
    begin(wo, 1)
    hop(wq, 1, 1)
    hop(wq, 3, 0)
    swapped(x_swap[1].start)
    hop(wq, 2, 1)
    hop(wo, 0, 0)
    begin(wu, 0)
    hop(wq, 3, 1)
    hop(wo, 1, 0)
    begin(wu, 1)
    a1_gather[0].finish()
    kept(lambda: loss_grad(0), lambda: loss_grad(1))
    wq.finish()

    project(0)
    hop(wo, 0, 1)
    hop(wo, 1, 1)
    attend(0)
    swapped(lambda: first_norm(1))
    begin(wu, 2)
    wo.finish()
    attn_sum[0].start(out_term(0))
    hop(wu, 0, 0)
    begin(wu, 3)
    a1_gather[1].forward()
    hop(wu, 1, 0)
    swapped(c_swap[0].start)
    hop(wu, 0, 1)
    make_bias(1)
    a1_gather[1].finish()
    project(1)
    hop(wu, 2, 0)
    swapped(c_swap[1].start)
    hop(wu, 1, 1)
    attend(1)
    attn_sum[1].start(out_term(1))
    hop(wu, 3, 0)
    begin(wd, 0)
    hop(wu, 2, 1)
    second_norm(0, attn_sum[0].finish())
    swapped(lambda: loss_grad(0))
    begin(wd, 1)
    hop(wu, 3, 1)
    second_norm(1, attn_sum[1].finish())
    a2_gather[0].forward()
    swapped(lambda: loss_grad(1))
    begin(wd, 2)
    wu.finish()
    a2_gather[0].finish()
    up(0)
    hop(wd, 0, 0)
    begin(wd, 3)
    a2_gather[1].forward()
    hop(wd, 1, 0)
    hop(wd, 0, 1)
    a2_gather[1].finish()
    up(1)
    gb_gather[0].forward()
    hop(wd, 2, 0)
    hop(wd, 1, 1)
    gb_gather[1].forward()
    hop(wd, 3, 0)
    hop(wd, 2, 1)
    gb_gather[0].finish()
    gb_gather[1].finish()
    hop(wd, 3, 1)
    place(GD, GD.shape[0], dg(micros(Z), both(GB), NT))
    wd.finish()
    wave(gd, 1)

    down_back(0)
    mid_sum[0].start(mid_term(0))
    down_back(1)
    mid_sum[1].start(mid_term(1))
    place(GU, GU.shape[0], dg(both(A2), micros(GP), NT))
    second_norm_back(0, mid_sum[0].finish())
    wave(gd, 2)
    wave(gu, 1)
    second_norm_back(1, mid_sum[1].finish())
    for w in (wq, wo, wu, wd):
        w.sent()
    y_sum[0].start(y_term(0))
    dhb_gather[0].forward()
    dhb_gather[0].finish()
    heads_back(0)
    wave(gd, 3)
    y_sum[1].start(y_term(1))
    dhb_gather[1].forward()
    in_sum[0].start(in_term(0))
    dhb_gather[1].finish()
    heads_back(1)
    wave(gu, 2)
    in_sum[1].start(in_term(1))
    place(WU, gq[0].ch * COLS, dg(micros(QKV), both(A1), NT))
    wave(gq[:2], 1)
    wave(gq[2:], 1)
    give_output(0)
    place(WD, go[0].ch * COLS, dg(micros(O), both(DHB), NT))
    wave(go, 1)
    wave(gu, 3)
    wave(gd, 4)
    wave(gq[:2], 2)
    wave(gq[2:], 2)
    wave(go, 2)
    wave(gd, 5)
    wave(gq[:2], 3)
    wave(gq[2:], 3)
    wave(go, 3)
    give_output(1)
    wave(gu, 5)
    wave(gd, 6)
    first_norm_back(0, in_sum[0].finish())
    first_norm_back(1, in_sum[1].finish())
    sum_copies[0].start()
    give_input_grad(0)
    give_input_grad(1)
    wave(gd, 7)
    wave(gu, 6)
    sum_add(0)
    sum_copies[1].start()
    wave(gq[:2], 5)
    wave(gq[2:], 5)
    wave(go, 5)
    wave(gu, 7)
    sum_add(1)
    sum_copies[2].start()
    wave(gq[:2], 6)
    wave(gq[2:], 6)
    sum_add(2)
    sum_copies[3].start()
    wave(go, 6)
    wave(gq[:2], 7)
    sum_add(3)
    sum_copies[4].start()
    wave(gq[2:], 7)
    wave(go, 7)
    sum_add(4)
    ng_ref[...] = NG[...]
    for m in range(micro):

        @pl.when(sw)
        def _():
            ig_swap[m].wait()
            DH[m] = CS[m].astype(F32)
            ig_keep[m].start()
            out_swap[m].wait()
            x_swap[m].wait_send()
            c_swap[m].wait_send()

        ig_keep[m].wait()
        kept(out_keep[m].wait)
    swapped(lab_swap.wait_send)
    for cp in pending:
        cp.wait_send()
    for p in gd + gu + gq + go:
        p.finish()


def layer(
    inputs, segments, norm1_gain, norm1_bias, qkv_weight, out_weight, norm2_gain, norm2_bias, up_weight, down_weight,
    cotangent,
):
    micro, tok, width = inputs.shape
    local_width = qkv_weight.shape[2]
    ff = up_weight.shape[1]
    row = 4 * tok
    heads = local_width // HD
    three = 3 * local_width
    lw, lf = up_to(width, 128), up_to(ff, 128)
    half = row // 2
    cq, co, cu, cd = chunk_rows(three), chunk_rows(local_width), chunk_rows(width), chunk_rows(ff)
    wq = jnp.transpose(qkv_weight, (0, 2, 1)).reshape(three, width)

    def tall(w, height):
        return jnp.pad(w, ((0, height - w.shape[0]), (0, 0)))

    def v(shape, dtype=BF):
        return pltpu.VMEM(shape, dtype)

    def recv(ch, lanes):
        return v((COLS - 1, ch, lanes))

    any_spec = pl.BlockSpec(memory_space=pl.ANY)
    vmem = pl.BlockSpec(memory_space=pltpu.VMEM)
    block = (width, tok)
    scratch = [
        v((COLS * cq, width)), v((COLS * co, width)), v((COLS * cu, ff)), v((COLS * cd, width)),
        v((COLS * cu, lf)), v((COLS * cd, lw)),
        recv(cq, width), recv(co, width), recv(cu, lf), recv(cd, lw),
        v((cq, width)), v((co, width)), v((cu, lf)), v((cd, lw)),
        v((cq, width)), v((co, width)), v((cu, lf)), v((cd, lw)),
        v((micro, *block)), v((micro, *block)), v((4, micro, tok), jnp.int32), v((micro, row, tok), F32),
        v((row, row), F32), v((4, *block), F32),
        v((4 * micro, *block)), v((micro, three, row)),
        v((micro, heads, half, half)), v((micro, heads, row, half)), v((micro, local_width, row)),
        v((micro, *block), F32),
        v((4 * micro, *block)), v((micro, ff, row)), v((micro, ff, row)), v((4 * micro, *block)),
        v((4 * micro, *block)), v((micro, local_width, row)), v((micro, *block), F32), v((ff, half), F32),
        v((2 * micro + 1, *block), F32),
        v((2 * micro, 2, *block)), v((2 * micro, *block)), v((2 * micro, 2, *block)), v((2 * micro, *block)),
        v((micro, *block)),
        v((8, width), F32), v((5, 8, width), F32),
        pltpu.SemaphoreType.DMA((NSEM,)), pltpu.SemaphoreType.DMA((NSEM,)), pltpu.SemaphoreType.DMA((23,)),
    ]
    out, input_grad, gq, go, gu, gd, ng = pl.pallas_call(
        kernel,
        out_shape=[
            jax.ShapeDtypeStruct((micro, *block), BF),
            jax.ShapeDtypeStruct((micro, *block), F32),
            jax.ShapeDtypeStruct((COLS * cq, width), BF),
            jax.ShapeDtypeStruct((COLS * co, width), BF),
            jax.ShapeDtypeStruct((COLS * cu, lf), BF),
            jax.ShapeDtypeStruct((COLS * cd, lw), BF),
            jax.ShapeDtypeStruct((8, width), F32),
        ],
        in_specs=[any_spec, vmem, vmem, vmem] + [any_spec] * 3 + [vmem, vmem] + [any_spec] * 3,
        out_specs=[any_spec] * 6 + [vmem],
        scratch_shapes=scratch,
        compiler_params=pltpu.CompilerParams(
            collective_id=0, has_side_effects=True, vmem_limit_bytes=64 * 1024 * 1024
        ),
    )(
        jnp.transpose(inputs, (0, 2, 1)), segments, norm1_gain, norm1_bias,
        wq, tall(wq[(COLS - 1) * cq :], cq), tall(out_weight, COLS * co), norm2_gain, norm2_bias, up_weight, down_weight,
        jnp.transpose(cotangent, (0, 2, 1)),
    )
    grads = (
        jnp.transpose(gq[:three].astype(F32).reshape(3, local_width, width), (0, 2, 1)),
        go[:local_width].astype(F32),
        gu[:width, :ff].astype(F32),
        gd[:ff, :width].astype(F32),
    )
    extent = lax.axis_size("dp")
    block = 2 * COLS
    if extent > block:
        groups = [[r + block * j for j in range(extent // block)] for r in range(block)]
        grads = lax.psum(grads, "dp", axis_index_groups=groups)
        ng = lax.psum(ng, "dp", axis_index_groups=groups)
    gq, go, gu, gd = grads
    out, input_grad = jnp.transpose(out, (0, 2, 1)), jnp.transpose(input_grad, (0, 2, 1))
    return out, input_grad, ng[0], ng[1], gq, go, ng[2], ng[3], gu, gd


def solution(mesh):
    tokens = P(None, ("dp", "tensor"), None)
    weights = (P(None, None, "tensor"), P("tensor", None))
    mlp = (P(None, "tensor"), P("tensor", None))
    return jax.shard_map(
        layer,
        mesh=mesh,
        in_specs=(tokens, P(None, ("dp", "tensor")), P(), P(), *weights, P(), P(), *mlp, tokens),
        out_specs=(tokens, tokens, P(), P(), *weights, P(), P(), *mlp),
        check_vma=False,
    )
```

```python
import functools

import jax
import jax.numpy as jnp
from jax import lax
from jax.experimental import pallas as pl
from jax.experimental.pallas import tpu as pltpu
from jax.sharding import PartitionSpec as P


HD = 56
BF = jnp.bfloat16
F32 = jnp.float32
MESH = pl.DeviceIdType.MESH
NN = (((1,), (0,)), ((), ()))
NT = (((1,), (1,)), ((), ()))
TN = (((0,), (0,)), ((), ()))
COLS = 4
BITS = (1, 2)
NSEM = 217


def up_to(n, m):
    return -(-n // m) * m


def chunk_rows(rows):
    return up_to(-(-rows // COLS), 16)


def parts_of(ch, n):
    out, off = [], 0
    for i in range(n):
        size = up_to(-(-(ch - off) // (n - i)), 16)
        out.append((off, size, BITS if i % 2 == 0 else BITS[::-1], i % 2))
        off += size
    return out


def dg(a, b, dims):
    return lax.dot_general(a, b, dims, preferred_element_type=F32)


def normed(v):
    center = v - jnp.mean(v, axis=0, keepdims=True)
    rstd = lax.rsqrt(jnp.mean(center * center, axis=0, keepdims=True) + 1e-05)
    return center * rstd, rstd


def kernel(
    x_hbm, seg_ref, n1g, n1b, wq_hbm, wq_end, wo_hbm, n2g, n2b, wu_hbm, wd_hbm, c_hbm,
    out_hbm, ig_hbm, gq_hbm, go_hbm, gu_hbm, gd_hbm, ng_ref,
    WQ, WO, WU, WD, GU, GD, RQ, RO, RU, RD, SQ, SO, SU, SD, KQ, KO, KU, KD,
    XS, CS, LAB, LT, BIAS, NW, A1, QKV, PB0, PB1, O, HS, A2, Z, GP, GB, DHB, DO, DH, U,
    T2, S1, SZ, R1, RZ, OB, NG, NR,
    ssem, rsem, lsem,
):
    d = lax.axis_index("dp")
    z = lax.axis_index("tensor")
    c = lax.rem(d, 2)
    q = lax.rem(d // 2, COLS)
    zl = lax.rem(z, 2)
    zh = z // 2
    b = zl + 2 * c
    sw = zh != c
    dc = d + 1 - 2 * c
    z1 = z + 1 - 2 * zl
    z2 = z + 2 - 4 * zh
    core = (dc, z)
    zpeer = (d, z1)
    sigma = (dc, z2)

    def flip(owner, bit):
        on = lax.rem(owner // bit, 2)
        return owner + bit * (1 - 2 * on)

    def col(bit):
        return (d + 2 * (flip(q, bit) - q), z)

    def masked(owner, s):
        for k in BITS:
            if s & k:
                owner = flip(owner, k)
        return owner

    xpeer, ypeer = col(1), col(2)
    micro, width, tok = XS.shape
    row = 4 * tok
    half = row // 2
    local_width = O.shape[1]
    ff = Z.shape[1]
    heads = local_width // HD
    scale = HD ** (-0.5)
    counts = dict(r=0, l=0)
    pending = []

    def rcopy(src, dst, peer):
        i = counts["r"]
        counts["r"] = i + 1
        assert i < NSEM
        return pltpu.make_async_remote_copy(
            src_ref=src, dst_ref=dst, send_sem=ssem.at[i], recv_sem=rsem.at[i], device_id=peer, device_id_type=MESH
        )

    def lcopy(src, dst):
        i = counts["l"]
        counts["l"] = i + 1
        return pltpu.make_async_copy(src, dst, lsem.at[i])

    def rows(start, size, step=16):
        return pl.ds(pl.multiple_of(start, step), size)

    def cols(j):
        return pl.ds(pl.multiple_of(j * tok, tok), tok)

    def swapped(*fs):
        @pl.when(sw)
        def _():
            for f in fs:
                f()

    def kept(*fs):
        @pl.when(jnp.logical_not(sw))
        def _():
            for f in fs:
                f()

    barrier = pltpu.get_barrier_semaphore()
    peers = (core, zpeer, sigma, xpeer, ypeer)
    for p in peers:
        pl.semaphore_signal(barrier, 1, device_id=p, device_id_type=MESH)
    pl.semaphore_wait(barrier, len(peers))

    class Gather:
        def __init__(self, view):
            self.own = view(b)
            self.cz = rcopy(view(b), view(b), zpeer)
            self.cc = rcopy(view(b), view(b), core)
            far = 1 - zl + 2 * c
            self.cf = rcopy(view(far), view(far), core)

        def start(self):
            self.cz.start()
            self.cc.start()

        def forward(self):
            self.cz.wait_recv()
            self.cf.start()

        def finish(self):
            self.cc.wait_recv()
            self.cf.wait_recv()
            pending.extend([self.cz, self.cc, self.cf])

    def gather_rows(ref, m):
        return Gather(lambda j: ref.at[m * 4 + j])

    class Scatter:
        def __init__(self, s):
            self.s = s
            self.idx = counts["r"]
            counts["r"] += 2
            self.cz = rcopy(SZ.at[s], RZ.at[s], zpeer)

        def give(self, i):
            return pltpu.make_async_remote_copy(
                src_ref=S1.at[self.s, i], dst_ref=R1.at[self.s, i], send_sem=ssem.at[self.idx + i],
                recv_sem=rsem.at[self.idx + i], device_id=core, device_id_type=MESH,
            )

        def start(self, term):
            s = self.s

            def body(i, carry):
                side = lax.rem(1 - zl + i, 2)
                part = term(side + 2 * (1 - c), side + 2 * c)
                S1[s, i] = part[:, :tok].astype(BF)
                T2[s * i + 2 * micro * (1 - i)] = part[:, tok:]
                self.give(i).start()
                return carry

            lax.fori_loop(0, 2, body, 0)
            self.give(0).wait_recv()
            SZ[s] = (T2[2 * micro] + R1[s, 0].astype(F32)).astype(BF)
            self.cz.start()

        def finish(self):
            s = self.s
            self.give(1).wait_recv()
            self.cz.wait_recv()
            total = T2[s] + R1[s, 1].astype(F32) + RZ[s].astype(F32)
            self.give(0).wait_send()
            self.give(1).wait_send()
            self.cz.wait_send()
            return total

    class Weight:
        def __init__(self, hbm, ref, n, end=None):
            ch = ref.shape[0] // COLS
            whole = hbm.shape[0] if end is None else (COLS - 1) * ch
            self.locals = [lcopy(hbm.at[0:whole], ref.at[0:whole])]
            if end is not None:
                self.locals.append(lcopy(end, ref.at[whole : whole + ch]))
            self.hops = []
            for off, size, order, _ in parts_of(ch, n):
                i = counts["r"]
                counts["r"] = i + 1

                def first(src, at, i=i):
                    return pltpu.make_async_remote_copy(
                        src_ref=src, dst_ref=ref.at[at], send_sem=ssem.at[i], recv_sem=rsem.at[i],
                        device_id=sigma, device_id_type=MESH,
                    )

                at = rows(q * ch + off, size)
                usual = first(hbm.at[at], at)
                last_at = (COLS - 1) * ch + off
                last_size = max(0, min(size, whole - last_at))
                at = slice(last_at, last_at + last_size)
                last = usual if last_size == size else first(hbm.at[at], at) if last_size else None
                if end is not None:
                    last = first(end.at[off : off + size], slice(last_at, last_at + size))
                steps, done = [], [0]
                for bit in order:
                    copies = []
                    for s in done:
                        at = rows(masked(q, s) * ch + off, size)
                        copies.append(rcopy(ref.at[at], ref.at[at], col(bit)))
                    steps.append(copies)
                    done = done + [s | bit for s in done]
                self.hops.append(((usual, last), steps))

        def first(self, hop, act):
            usual, last = hop[0]
            if last is usual:
                act(usual)
                return
            pl.when(q < COLS - 1)(lambda: act(usual))
            if last is not None:
                pl.when(q == COLS - 1)(lambda: act(last))

        def load(self):
            kept(*[cp.start for cp in self.locals])

        def pass_on(self, h, j):
            if j == 0:
                self.first(h, lambda cp: cp.wait_recv())
            else:
                for cp in h[1][j - 1]:
                    cp.wait_recv()
            for cp in h[1][j]:
                cp.start()

        def finish(self):
            def go():
                for h in self.hops:
                    for cp in h[1][-1]:
                        cp.wait_recv()

            swapped(go)
            kept(*[cp.wait for cp in self.locals])

        def sent(self):
            def go():
                for h in self.hops:
                    self.first(h, lambda cp: cp.wait_send())
                    for copies in h[1]:
                        for cp in copies:
                            cp.wait_send()

            swapped(go)

    class Piece:
        def __init__(self, ref, recv, far, near, hbm, off, size, order, fin):
            self.ref, self.recv, self.far, self.near, self.hbm = ref, recv, far, near, hbm
            self.off, self.size, self.fin = off, size, fin
            self.ch = recv.shape[1]
            self.place = slice(off, off + size)
            base, self.sums = 0, []
            for j, bit in enumerate(order):
                rest = [0]
                for k in order[j + 1 :]:
                    rest = rest + [s | k for s in rest]
                copies = []
                for i, s in enumerate(rest):
                    mine = masked(q, s)
                    slot = recv.at[base + i, self.place]
                    copies.append((mine, base + i, rcopy(ref.at[self.at(flip(mine, bit))], slot, col(bit))))
                base += len(rest)
                self.sums.append(copies)
            own, out = ref.at[self.at(q)], hbm.at[self.at(q)]
            self.trade = rcopy(own, far.at[self.place], sigma)
            self.join = rcopy(own, near.at[self.place], core)
            self.own = lcopy(own, out)
            self.own_core = rcopy(own, out, core)
            done, self.spreads = [0], []
            for bit in order:
                copies = []
                for s in done:
                    owner = masked(q, s)
                    src = own if s == 0 else hbm.at[self.at(owner)]
                    got = hbm.at[self.at(flip(owner, bit))]
                    copies.append((rcopy(src, hbm.at[self.at(owner)], col(bit)), rcopy(got, got, core)))
                self.spreads.append(copies)
                done = done + [s | bit for s in done]
            self.steps = [self.send_first, self.add_send, self.add_trade, self.take_join, self.join_spread]
            self.steps += [functools.partial(self.spread, j) for j in range(len(self.spreads))]
            self.done = 0

        def at(self, owner):
            return rows(owner * self.ch + self.off, self.size)

        def run(self, upto):
            while self.done < min(upto, len(self.steps)):
                self.steps[self.done]()
                self.done += 1

        def by_rows(self, owner, more, plain=False):
            base = owner * self.ch + self.off

            def body(i, carry):
                r = rows(base + i * 16, 16)
                other = more[rows(self.off + i * 16, 16), :]
                if not plain:
                    other = (self.ref[r, :].astype(F32) + other.astype(F32)).astype(BF)
                self.ref[r, :] = other
                return carry

            lax.fori_loop(0, self.size // 16, body, 0)

        def add(self, j):
            for mine, slot, cp in self.sums[j]:
                cp.wait_recv()
                self.by_rows(mine, self.recv.at[slot])
                pending.append(cp)

        def send_first(self):
            for _, _, cp in self.sums[0]:
                cp.start()

        def add_send(self):
            self.add(0)
            for _, _, cp in self.sums[1]:
                cp.start()

        def add_trade(self):
            self.add(1)
            swapped(self.trade.start)

        def take_join(self):
            def go():
                self.trade.wait()
                self.by_rows(q, self.far, plain=True)

            swapped(go)
            pl.when(c != self.fin)(self.join.start)

        def join_spread(self):
            def take():
                self.join.wait_recv()
                self.by_rows(q, self.near)
                for cp, _ in self.spreads[0]:
                    cp.start()
                self.own_core.start()
                self.own.start()

            pl.when(c == self.fin)(take)

        def spread(self, j):
            def go():
                for cp, _ in self.spreads[j]:
                    cp.wait_recv()
                if j + 1 < len(self.spreads):
                    for cp, _ in self.spreads[j + 1]:
                        cp.start()
                for _, cp in self.spreads[j]:
                    cp.start()

            pl.when(c == self.fin)(go)

        def finish(self):
            def owner():
                self.own.wait()
                self.own_core.wait_send()
                for copies in self.spreads:
                    for a, f in copies:
                        a.wait_send()
                        f.wait_send()

            def other():
                self.join.wait_send()
                self.own_core.wait_recv()
                for copies in self.spreads:
                    for _, f in copies:
                        f.wait_recv()

            pl.when(c == self.fin)(owner)
            pl.when(c != self.fin)(other)

    def pieces(ref, recv, far, near, hbm, n):
        return [Piece(ref, recv, far, near, hbm, *p) for p in parts_of(recv.shape[1], n)]

    def wave(group, last):
        first = min(p.done for p in group)
        for t in range(first, last + len(group)):
            for i, p in enumerate(group):
                p.run(min(last, t - i + 1))

    def sweep(group, last):
        for t in range(min(p.done for p in group), last):
            for p in group:
                p.run(t + 1)

    wq, wo = Weight(wq_hbm, WQ, 4, wq_end), Weight(wo_hbm, WO, 2)
    wu, wd = Weight(wu_hbm, WU, 4), Weight(wd_hbm, WD, 4)
    other_b = zl + 2 * (1 - c)
    x_swap = [rcopy(x_hbm.at[m], XS.at[m], sigma) for m in range(micro)]
    x_load = [lcopy(x_hbm.at[m], XS.at[m]) for m in range(micro)]
    c_swap = [rcopy(c_hbm.at[m], CS.at[m], sigma) for m in range(micro)]
    c_load = [lcopy(c_hbm.at[m], CS.at[m]) for m in range(micro)]
    lab_swap = rcopy(seg_ref, LAB.at[other_b], sigma)
    lab_gather = Gather(lambda j: LAB.at[j])
    a1_gather = [gather_rows(A1, m) for m in range(micro)]
    gb_gather = [gather_rows(GB, m) for m in range(micro)]
    a2_gather = [gather_rows(A2, m) for m in range(micro)]
    dhb_gather = [gather_rows(DHB, m) for m in range(micro)]
    attn_sum = [Scatter(2 * m) for m in range(micro)]
    mid_sum = [Scatter(2 * m) for m in range(micro)]
    y_sum = [Scatter(2 * m + 1) for m in range(micro)]
    in_sum = [Scatter(2 * m) for m in range(micro)]
    gd = pieces(GD, RD, SD, KD, gd_hbm, 2)
    gu = pieces(GU, RU, SU, KU, gu_hbm, 2)
    gq = pieces(WU, RQ, SQ, KQ, gq_hbm, 2)
    go = pieces(WD, RO, SO, KO, go_hbm, 2)
    out_swap = [rcopy(OB.at[m], out_hbm.at[m], sigma) for m in range(micro)]
    out_keep = [lcopy(OB.at[m], out_hbm.at[m]) for m in range(micro)]
    ig_swap = [rcopy(XS.at[m], CS.at[m], sigma) for m in range(micro)]
    ig_keep = [lcopy(DH.at[m], ig_hbm.at[m]) for m in range(micro)]
    sum_copies = [rcopy(NG, NR.at[i], p) for i, p in enumerate((sigma, xpeer, ypeer, zpeer, core))]

    def widen():
        for i, ref in enumerate((n1g, n1b, n2g, n2b)):
            NW[i] = jnp.transpose(jnp.broadcast_to(ref[...].reshape(1, width), (tok, width)))

    def first_norm(m):
        swapped(x_swap[m].wait_recv)
        kept(x_load[m].wait)
        xhat, _ = normed(XS[m].astype(F32))
        A1[m * 4 + b] = (xhat * NW[0] + NW[1]).astype(BF)
        a1_gather[m].start()

    def loss_grad(m):
        swapped(c_swap[m].wait_recv)
        kept(c_load[m].wait)
        labels = LAB[b]
        live = (labels[m : m + 1, :] >= 0).astype(F32)
        GB[m * 4 + b] = (CS[m].astype(F32) * live).astype(BF)
        gb_gather[m].start()

    def labels_wide():
        for m in range(micro):
            for j in range(4):
                lab = LAB[j, m : m + 1, :].astype(F32)
                LT[m, j * tok : (j + 1) * tok, :] = jnp.transpose(jnp.broadcast_to(lab, (tok, tok)))

    def make_bias(m):
        for j in range(4):
            lab = LAB[j, m : m + 1, :].astype(F32)
            place_k = lax.broadcasted_iota(jnp.int32, (row, tok), 0)
            place_q = lax.broadcasted_iota(jnp.int32, (row, tok), 1) + j * tok
            ok = (LT[m] == lab) & (place_k <= place_q)
            BIAS[:, j * tok : (j + 1) * tok] = jnp.where(ok, 0.0, -1e30)

    def whole(ref, m):
        return jnp.concatenate([ref[m * 4 + j] for j in range(4)], axis=1)

    def both(ref):
        return jnp.concatenate([ref[j] for j in range(ref.shape[0])], axis=1)

    def pair(ref, m, i, j):
        return jnp.concatenate([ref[m, :, cols(i)], ref[m, :, cols(j)]], axis=1)

    def project(m):
        QKV[m] = dg(WQ[0 : 3 * local_width, :], whole(A1, m), NN).astype(BF)

    def head_slices(h, qb):
        e = [slice(i * local_width + h * HD, i * local_width + (h + 1) * HD) for i in range(3)]
        return slice(qb * half, (qb + 1) * half), slice(0, (qb + 1) * half), *e

    def attend(m):
        for h in range(heads):
            for qb, PB in ((0, PB0), (1, PB1)):
                at, upto, eq, ek, ev = head_slices(h, qb)
                s = dg(QKV[m, ek, upto], QKV[m, eq, at], TN) * scale + BIAS[upto, at]
                e = jnp.exp(s - jnp.max(s, axis=0, keepdims=True))
                p = (e * (1.0 / jnp.sum(e, axis=0, keepdims=True))).astype(BF)
                PB[m, h] = p
                O[m, eq, at] = dg(QKV[m, ev, upto], p, NN).astype(BF)

    def heads_back(m):
        DO[m] = dg(WO[0:local_width, :], whole(DHB, m), NN).astype(BF)
        for h in range(heads):
            for qb, PB in ((1, PB1), (0, PB0)):
                at, upto, eq, ek, ev = head_slices(h, qb)
                qv, do, pb, kv = QKV[m, eq, at], DO[m, eq, at], PB[m, h], QKV[m, ek, upto]
                p = pb.astype(F32)
                pdp = p * dg(QKV[m, ev, upto], do, TN)
                ds = (pdp - p * jnp.sum(pdp, axis=0, keepdims=True)).astype(BF)
                dq = (dg(kv, ds, NN) * scale).astype(BF)
                dk, dv = dg(qv, ds, NT), dg(do, pb, NT)
                if qb == 1:
                    dq1, dk1, dv1, at1 = dq, dk, dv, at
                else:
                    QKV[m, eq, at] = dq
                    QKV[m, eq, at1] = dq1
                    QKV[m, ek, at] = ((dk1[:, :half] + dk) * scale).astype(BF)
                    QKV[m, ek, at1] = (dk1[:, half:] * scale).astype(BF)
                    QKV[m, ev, at] = (dv1[:, :half] + dv).astype(BF)
                    QKV[m, ev, at1] = dv1[:, half:].astype(BF)

    def second_norm(m, total):
        h = XS[m].astype(F32) + total
        HS[m] = h
        xhat, _ = normed(h)
        A2[m * 4 + b] = (xhat * NW[2] + NW[3]).astype(BF)
        a2_gather[m].start()

    def up(m):
        c0 = 0.7978845608028654
        step = 32

        def side(j, carry):
            blocks = jnp.concatenate([A2[m * 4 + 2 * j], A2[m * 4 + 2 * j + 1]], axis=1)
            U[...] = dg(WU[0:width, :], blocks, TN)
            at = pl.ds(pl.multiple_of(j * half, half), half)

            def body(i, carry):
                r = rows(i * step, step, step)
                u = U[r, :]
                u2 = u * u
                t = jnp.tanh(c0 * u * (1.0 + 0.044715 * u2))
                hp = 0.5 * (1.0 + t)
                Z[m, r, at] = (u * hp).astype(BF)
                GP[m, r, at] = (hp + (0.5 * c0) * u * (1.0 - t * t) * (1.0 + (3 * 0.044715) * u2)).astype(BF)
                return carry

            return lax.fori_loop(0, ff // step, body, carry)

        lax.fori_loop(0, 2, side, 0)

    def down_back(m):
        dz = dg(WD[0:ff, :], whole(GB, m), NN)
        GP[m] = (dz * GP[m].astype(F32)).astype(BF)

    def over_tokens(v):
        ones = jnp.ones((8, tok), BF)
        high = v.astype(BF)
        low = (v - high.astype(F32)).astype(BF)
        return (dg(ones, high, NT) + dg(ones, low, NT))[0:1, :]

    def norm_back(v, gain, grad, i):
        xhat, rstd = normed(v)
        dn = grad * gain
        dv = rstd * (
            dn - jnp.mean(dn, axis=0, keepdims=True) - xhat * jnp.mean(dn * xhat, axis=0, keepdims=True)
        )
        return dv, grad * xhat

    def second_norm_back(m, total):
        dv, gains = norm_back(HS[m], NW[2], total, 2)
        dh = GB[m * 4 + b].astype(F32) + dv
        DH[m] = dh
        DHB[m * 4 + b] = dh.astype(BF)
        dhb_gather[m].start()
        NG[2:3, :] += over_tokens(gains)
        NG[3:4, :] += over_tokens(total)

    def first_norm_back(m, total):
        dv, gains = norm_back(XS[m].astype(F32), NW[0], total, 0)
        DH[m] = DH[m] + dv
        NG[0:1, :] += over_tokens(gains)
        NG[1:2, :] += over_tokens(total)

    def give_input_grad(m):
        @pl.when(sw)
        def _():
            XS[m] = DH[m].astype(BF)
            ig_swap[m].start()

        kept(ig_keep[m].start)

    def out_term(m):
        return lambda i, j: dg(WO[0:local_width, :], pair(O, m, i, j), TN)

    def y_term(m):
        return lambda i, j: dg(WD[0:ff, :], pair(Z, m, i, j), TN)

    def mid_term(m):
        return lambda i, j: dg(WU[0:width, :], pair(GP, m, i, j), NN)

    def in_term(m):
        return lambda i, j: dg(WQ[0 : 3 * local_width, :], pair(QKV, m, i, j), TN)

    def give_output(m):
        OB[m] = (HS[m] + y_sum[m].finish()).astype(BF)
        swapped(out_swap[m].start)
        kept(out_keep[m].start)

    def sum_add(i):
        sum_copies[i].wait()
        NG[...] = NG[...] + NR[i]

    def place(ref, height, value):
        n, m = value.shape
        ref[0:n, 0:m] = value.astype(BF)
        ref[n:height, :] = jnp.zeros((height - n, ref.shape[1]), BF)
        if m < ref.shape[1]:
            ref[0:n, m:] = jnp.zeros((n, ref.shape[1] - m), BF)

    def micros(ref):
        return jnp.concatenate([ref[m] for m in range(micro)], axis=1)

    def begin(w, i):
        swapped(lambda: w.first(w.hops[i], lambda cp: cp.start()))

    def hop(w, i, j):
        swapped(lambda: w.pass_on(w.hops[i], j))

    swapped(lab_swap.start, x_swap[0].start)
    begin(wq, 0)
    begin(wq, 1)
    kept(*[cp.start for cp in x_load])
    for w in (wq, wo, wu, wd):
        w.load()
    kept(*[cp.start for cp in c_load])

    @pl.when(jnp.logical_not(sw))
    def _():
        LAB[b] = seg_ref[...]

    NG[...] = jnp.zeros_like(NG)
    widen()
    swapped(lab_swap.wait_recv)
    lab_gather.start()
    first_norm(0)
    begin(wq, 2)
    kept(lambda: first_norm(1))
    lab_gather.forward()
    hop(wq, 0, 0)
    begin(wq, 3)
    a1_gather[0].forward()
    hop(wq, 1, 0)
    begin(wo, 0)
    hop(wq, 0, 1)
    lab_gather.finish()
    labels_wide()
    make_bias(0)
    hop(wq, 2, 0)
    begin(wo, 1)
    hop(wq, 1, 1)
    hop(wq, 3, 0)
    swapped(x_swap[1].start)
    hop(wq, 2, 1)
    hop(wo, 0, 0)
    begin(wu, 0)
    hop(wq, 3, 1)
    hop(wo, 1, 0)
    begin(wu, 1)
    a1_gather[0].finish()
    kept(lambda: loss_grad(0), lambda: loss_grad(1))
    wq.finish()

    project(0)
    hop(wo, 0, 1)
    hop(wo, 1, 1)
    attend(0)
    swapped(lambda: first_norm(1))
    begin(wu, 2)
    wo.finish()
    attn_sum[0].start(out_term(0))
    hop(wu, 0, 0)
    begin(wu, 3)
    a1_gather[1].forward()
    hop(wu, 1, 0)
    swapped(c_swap[0].start)
    hop(wu, 0, 1)
    make_bias(1)
    a1_gather[1].finish()
    project(1)
    hop(wu, 2, 0)
    swapped(c_swap[1].start)
    hop(wu, 1, 1)
    attend(1)
    attn_sum[1].start(out_term(1))
    hop(wu, 3, 0)
    begin(wd, 0)
    hop(wu, 2, 1)
    second_norm(0, attn_sum[0].finish())
    swapped(lambda: loss_grad(0))
    begin(wd, 1)
    hop(wu, 3, 1)
    second_norm(1, attn_sum[1].finish())
    a2_gather[0].forward()
    swapped(lambda: loss_grad(1))
    begin(wd, 2)
    wu.finish()
    a2_gather[0].finish()
    up(0)
    hop(wd, 0, 0)
    begin(wd, 3)
    a2_gather[1].forward()
    hop(wd, 1, 0)
    hop(wd, 0, 1)
    a2_gather[1].finish()
    up(1)
    gb_gather[0].forward()
    hop(wd, 2, 0)
    hop(wd, 1, 1)
    gb_gather[1].forward()
    hop(wd, 3, 0)
    hop(wd, 2, 1)
    gb_gather[0].finish()
    gb_gather[1].finish()
    hop(wd, 3, 1)
    place(GD, GD.shape[0], dg(micros(Z), both(GB), NT))
    wd.finish()
    wave(gd, 1)

    down_back(0)
    mid_sum[0].start(mid_term(0))
    down_back(1)
    mid_sum[1].start(mid_term(1))
    place(GU, GU.shape[0], dg(both(A2), micros(GP), NT))
    second_norm_back(0, mid_sum[0].finish())
    wave(gd, 2)
    wave(gu, 1)
    second_norm_back(1, mid_sum[1].finish())
    for w in (wq, wo, wu, wd):
        w.sent()
    y_sum[0].start(y_term(0))
    dhb_gather[0].forward()
    dhb_gather[0].finish()
    heads_back(0)
    wave(gd, 3)
    y_sum[1].start(y_term(1))
    dhb_gather[1].forward()
    in_sum[0].start(in_term(0))
    dhb_gather[1].finish()
    heads_back(1)
    wave(gu, 2)
    in_sum[1].start(in_term(1))
    place(WU, gq[0].ch * COLS, dg(micros(QKV), both(A1), NT))
    wave(gq, 1)
    give_output(0)
    place(WD, go[0].ch * COLS, dg(micros(O), both(DHB), NT))
    wave(go, 1)
    wave(gu, 3)
    wave(gd, 4)
    wave(gq, 2)
    wave(go, 2)
    wave(gd, 5)
    wave(gq, 3)
    wave(go, 3)
    give_output(1)
    wave(gu, 5)
    wave(gd, 6)
    first_norm_back(0, in_sum[0].finish())
    first_norm_back(1, in_sum[1].finish())
    sum_copies[0].start()
    give_input_grad(0)
    give_input_grad(1)
    wave(gd, 7)
    wave(gu, 6)
    sweep(gq + go, 4)
    sum_add(0)
    sum_copies[1].start()
    sweep(gq + go, 5)
    wave(gu, 7)
    sum_add(1)
    sum_copies[2].start()
    sweep(gq + go, 6)
    sum_add(2)
    sum_copies[3].start()
    sum_add(3)
    sum_copies[4].start()
    sweep(gq + go, 7)
    sum_add(4)
    ng_ref[...] = NG[...]
    for m in range(micro):

        @pl.when(sw)
        def _():
            ig_swap[m].wait()
            DH[m] = CS[m].astype(F32)
            ig_keep[m].start()
            out_swap[m].wait()
            x_swap[m].wait_send()
            c_swap[m].wait_send()

        ig_keep[m].wait()
        kept(out_keep[m].wait)
    swapped(lab_swap.wait_send)
    for cp in pending:
        cp.wait_send()
    for p in gd + gu + gq + go:
        p.finish()


def layer(
    inputs, segments, norm1_gain, norm1_bias, qkv_weight, out_weight, norm2_gain, norm2_bias, up_weight, down_weight,
    cotangent,
):
    micro, tok, width = inputs.shape
    local_width = qkv_weight.shape[2]
    ff = up_weight.shape[1]
    row = 4 * tok
    heads = local_width // HD
    three = 3 * local_width
    lw, lf = up_to(width, 128), up_to(ff, 128)
    half = row // 2
    cq, co, cu, cd = chunk_rows(three), chunk_rows(local_width), chunk_rows(width), chunk_rows(ff)
    wq = jnp.transpose(qkv_weight, (0, 2, 1)).reshape(three, width)

    def tall(w, height):
        return jnp.pad(w, ((0, height - w.shape[0]), (0, 0)))

    def v(shape, dtype=BF):
        return pltpu.VMEM(shape, dtype)

    def recv(ch, lanes):
        return v((COLS - 1, ch, lanes))

    any_spec = pl.BlockSpec(memory_space=pl.ANY)
    vmem = pl.BlockSpec(memory_space=pltpu.VMEM)
    block = (width, tok)
    scratch = [
        v((COLS * cq, width)), v((COLS * co, width)), v((COLS * cu, ff)), v((COLS * cd, width)),
        v((COLS * cu, lf)), v((COLS * cd, lw)),
        recv(cq, width), recv(co, width), recv(cu, lf), recv(cd, lw),
        v((cq, width)), v((co, width)), v((cu, lf)), v((cd, lw)),
        v((cq, width)), v((co, width)), v((cu, lf)), v((cd, lw)),
        v((micro, *block)), v((micro, *block)), v((4, micro, tok), jnp.int32), v((micro, row, tok), F32),
        v((row, row), F32), v((4, *block), F32),
        v((4 * micro, *block)), v((micro, three, row)),
        v((micro, heads, half, half)), v((micro, heads, row, half)), v((micro, local_width, row)),
        v((micro, *block), F32),
        v((4 * micro, *block)), v((micro, ff, row)), v((micro, ff, row)), v((4 * micro, *block)),
        v((4 * micro, *block)), v((micro, local_width, row)), v((micro, *block), F32), v((ff, half), F32),
        v((2 * micro + 1, *block), F32),
        v((2 * micro, 2, *block)), v((2 * micro, *block)), v((2 * micro, 2, *block)), v((2 * micro, *block)),
        v((micro, *block)),
        v((8, width), F32), v((5, 8, width), F32),
        pltpu.SemaphoreType.DMA((NSEM,)), pltpu.SemaphoreType.DMA((NSEM,)), pltpu.SemaphoreType.DMA((23,)),
    ]
    out, input_grad, gq, go, gu, gd, ng = pl.pallas_call(
        kernel,
        out_shape=[
            jax.ShapeDtypeStruct((micro, *block), BF),
            jax.ShapeDtypeStruct((micro, *block), F32),
            jax.ShapeDtypeStruct((COLS * cq, width), BF),
            jax.ShapeDtypeStruct((COLS * co, width), BF),
            jax.ShapeDtypeStruct((COLS * cu, lf), BF),
            jax.ShapeDtypeStruct((COLS * cd, lw), BF),
            jax.ShapeDtypeStruct((8, width), F32),
        ],
        in_specs=[any_spec, vmem, vmem, vmem] + [any_spec] * 3 + [vmem, vmem] + [any_spec] * 3,
        out_specs=[any_spec] * 6 + [vmem],
        scratch_shapes=scratch,
        compiler_params=pltpu.CompilerParams(
            collective_id=0, has_side_effects=True, vmem_limit_bytes=64 * 1024 * 1024
        ),
    )(
        jnp.transpose(inputs, (0, 2, 1)), segments, norm1_gain, norm1_bias,
        wq, tall(wq[(COLS - 1) * cq :], cq), tall(out_weight, COLS * co), norm2_gain, norm2_bias, up_weight, down_weight,
        jnp.transpose(cotangent, (0, 2, 1)),
    )
    grads = (
        jnp.transpose(gq[:three].astype(F32).reshape(3, local_width, width), (0, 2, 1)),
        go[:local_width].astype(F32),
        gu[:width, :ff].astype(F32),
        gd[:ff, :width].astype(F32),
    )
    extent = lax.axis_size("dp")
    block = 2 * COLS
    if extent > block:
        groups = [[r + block * j for j in range(extent // block)] for r in range(block)]
        grads = lax.psum(grads, "dp", axis_index_groups=groups)
        ng = lax.psum(ng, "dp", axis_index_groups=groups)
    gq, go, gu, gd = grads
    out, input_grad = jnp.transpose(out, (0, 2, 1)), jnp.transpose(input_grad, (0, 2, 1))
    return out, input_grad, ng[0], ng[1], gq, go, ng[2], ng[3], gu, gd


def solution(mesh):
    tokens = P(None, ("dp", "tensor"), None)
    weights = (P(None, None, "tensor"), P("tensor", None))
    mlp = (P(None, "tensor"), P("tensor", None))
    return jax.shard_map(
        layer,
        mesh=mesh,
        in_specs=(tokens, P(None, ("dp", "tensor")), P(), P(), *weights, P(), P(), *mlp, tokens),
        out_specs=(tokens, tokens, P(), P(), *weights, P(), P(), *mlp),
        check_vma=False,
    )
```

```python
import functools

import jax
import jax.numpy as jnp
from jax import lax
from jax.experimental import pallas as pl
from jax.experimental.pallas import tpu as pltpu
from jax.sharding import PartitionSpec as P


HD = 56
BF = jnp.bfloat16
F32 = jnp.float32
MESH = pl.DeviceIdType.MESH
NN = (((1,), (0,)), ((), ()))
NT = (((1,), (1,)), ((), ()))
TN = (((0,), (0,)), ((), ()))
COLS = 4
BITS = (1, 2)
NSEM = 217


def up_to(n, m):
    return -(-n // m) * m


def chunk_rows(rows):
    return up_to(-(-rows // COLS), 16)


def parts_of(ch, n):
    out, off = [], 0
    for i in range(n):
        size = up_to(-(-(ch - off) // (n - i)), 16)
        out.append((off, size, BITS if i % 2 == 0 else BITS[::-1], i % 2))
        off += size
    return out


def dg(a, b, dims):
    return lax.dot_general(a, b, dims, preferred_element_type=F32)


def normed(v):
    center = v - jnp.mean(v, axis=0, keepdims=True)
    rstd = lax.rsqrt(jnp.mean(center * center, axis=0, keepdims=True) + 1e-05)
    return center * rstd, rstd


def kernel(
    x_hbm, seg_ref, n1g, n1b, wq_hbm, wq_end, wo_hbm, n2g, n2b, wu_hbm, wd_hbm, c_hbm,
    out_hbm, ig_hbm, gq_hbm, go_hbm, gu_hbm, gd_hbm, ng_ref,
    WQ, WO, WU, WD, GU, GD, RQ, RO, RU, RD, SQ, SO, SU, SD, KQ, KO, KU, KD,
    XS, CS, LAB, LT, BIAS, NW, A1, QKV, PB0, PB1, O, HS, A2, Z, GP, GB, DHB, DO, DH, U,
    T2, S1, SZ, R1, RZ, OB, NG, NR,
    ssem, rsem, lsem,
):
    d = lax.axis_index("dp")
    z = lax.axis_index("tensor")
    c = lax.rem(d, 2)
    q = lax.rem(d // 2, COLS)
    zl = lax.rem(z, 2)
    zh = z // 2
    b = zl + 2 * c
    sw = zh != c
    dc = d + 1 - 2 * c
    z1 = z + 1 - 2 * zl
    z2 = z + 2 - 4 * zh
    core = (dc, z)
    zpeer = (d, z1)
    sigma = (dc, z2)

    def flip(owner, bit):
        on = lax.rem(owner // bit, 2)
        return owner + bit * (1 - 2 * on)

    def col(bit):
        return (d + 2 * (flip(q, bit) - q), z)

    def masked(owner, s):
        for k in BITS:
            if s & k:
                owner = flip(owner, k)
        return owner

    xpeer, ypeer = col(1), col(2)
    micro, width, tok = XS.shape
    row = 4 * tok
    half = row // 2
    local_width = O.shape[1]
    ff = Z.shape[1]
    heads = local_width // HD
    scale = HD ** (-0.5)
    counts = dict(r=0, l=0)
    pending = []

    def rcopy(src, dst, peer):
        i = counts["r"]
        counts["r"] = i + 1
        assert i < NSEM
        return pltpu.make_async_remote_copy(
            src_ref=src, dst_ref=dst, send_sem=ssem.at[i], recv_sem=rsem.at[i], device_id=peer, device_id_type=MESH
        )

    def lcopy(src, dst):
        i = counts["l"]
        counts["l"] = i + 1
        return pltpu.make_async_copy(src, dst, lsem.at[i])

    def rows(start, size, step=16):
        return pl.ds(pl.multiple_of(start, step), size)

    def cols(j):
        return pl.ds(pl.multiple_of(j * tok, tok), tok)

    def swapped(*fs):
        @pl.when(sw)
        def _():
            for f in fs:
                f()

    def kept(*fs):
        @pl.when(jnp.logical_not(sw))
        def _():
            for f in fs:
                f()

    barrier = pltpu.get_barrier_semaphore()
    peers = (core, zpeer, sigma, xpeer, ypeer)
    for p in peers:
        pl.semaphore_signal(barrier, 1, device_id=p, device_id_type=MESH)
    pl.semaphore_wait(barrier, len(peers))

    class Gather:
        def __init__(self, view):
            self.own = view(b)
            self.cz = rcopy(view(b), view(b), zpeer)
            self.cc = rcopy(view(b), view(b), core)
            far = 1 - zl + 2 * c
            self.cf = rcopy(view(far), view(far), core)

        def start(self):
            self.cz.start()
            self.cc.start()

        def forward(self):
            self.cz.wait_recv()
            self.cf.start()

        def finish(self):
            self.cc.wait_recv()
            self.cf.wait_recv()
            pending.extend([self.cz, self.cc, self.cf])

    def gather_rows(ref, m):
        return Gather(lambda j: ref.at[m * 4 + j])

    class Scatter:
        def __init__(self, s):
            self.s = s
            self.idx = counts["r"]
            counts["r"] += 2
            self.cz = rcopy(SZ.at[s], RZ.at[s], zpeer)

        def give(self, i):
            return pltpu.make_async_remote_copy(
                src_ref=S1.at[self.s, i], dst_ref=R1.at[self.s, i], send_sem=ssem.at[self.idx + i],
                recv_sem=rsem.at[self.idx + i], device_id=core, device_id_type=MESH,
            )

        def start(self, term):
            s = self.s

            def body(i, carry):
                side = lax.rem(1 - zl + i, 2)
                part = term(side + 2 * (1 - c), side + 2 * c)
                S1[s, i] = part[:, :tok].astype(BF)
                T2[s * i + 2 * micro * (1 - i)] = part[:, tok:]
                self.give(i).start()
                return carry

            lax.fori_loop(0, 2, body, 0)
            self.give(0).wait_recv()
            SZ[s] = (T2[2 * micro] + R1[s, 0].astype(F32)).astype(BF)
            self.cz.start()

        def finish(self):
            s = self.s
            self.give(1).wait_recv()
            self.cz.wait_recv()
            total = T2[s] + R1[s, 1].astype(F32) + RZ[s].astype(F32)
            self.give(0).wait_send()
            self.give(1).wait_send()
            self.cz.wait_send()
            return total

    class Weight:
        def __init__(self, hbm, ref, n, end=None):
            ch = ref.shape[0] // COLS
            whole = hbm.shape[0] if end is None else (COLS - 1) * ch
            self.locals = [lcopy(hbm.at[0:whole], ref.at[0:whole])]
            if end is not None:
                self.locals.append(lcopy(end, ref.at[whole : whole + ch]))
            self.hops = []
            for off, size, order, _ in parts_of(ch, n):
                i = counts["r"]
                counts["r"] = i + 1

                def first(src, at, i=i):
                    return pltpu.make_async_remote_copy(
                        src_ref=src, dst_ref=ref.at[at], send_sem=ssem.at[i], recv_sem=rsem.at[i],
                        device_id=sigma, device_id_type=MESH,
                    )

                at = rows(q * ch + off, size)
                usual = first(hbm.at[at], at)
                last_at = (COLS - 1) * ch + off
                last_size = max(0, min(size, whole - last_at))
                at = slice(last_at, last_at + last_size)
                last = usual if last_size == size else first(hbm.at[at], at) if last_size else None
                if end is not None:
                    last = first(end.at[off : off + size], slice(last_at, last_at + size))
                steps, done = [], [0]
                for bit in order:
                    copies = []
                    for s in done:
                        at = rows(masked(q, s) * ch + off, size)
                        copies.append(rcopy(ref.at[at], ref.at[at], col(bit)))
                    steps.append(copies)
                    done = done + [s | bit for s in done]
                self.hops.append(((usual, last), steps))

        def first(self, hop, act):
            usual, last = hop[0]
            if last is usual:
                act(usual)
                return
            pl.when(q < COLS - 1)(lambda: act(usual))
            if last is not None:
                pl.when(q == COLS - 1)(lambda: act(last))

        def load(self):
            kept(*[cp.start for cp in self.locals])

        def pass_on(self, h, j):
            if j == 0:
                self.first(h, lambda cp: cp.wait_recv())
            else:
                for cp in h[1][j - 1]:
                    cp.wait_recv()
            for cp in h[1][j]:
                cp.start()

        def finish(self):
            def go():
                for h in self.hops:
                    for cp in h[1][-1]:
                        cp.wait_recv()

            swapped(go)
            kept(*[cp.wait for cp in self.locals])

        def sent(self):
            def go():
                for h in self.hops:
                    self.first(h, lambda cp: cp.wait_send())
                    for copies in h[1]:
                        for cp in copies:
                            cp.wait_send()

            swapped(go)

    class Piece:
        def __init__(self, ref, recv, far, near, hbm, off, size, order, fin):
            self.ref, self.recv, self.far, self.near, self.hbm = ref, recv, far, near, hbm
            self.off, self.size, self.fin = off, size, fin
            self.ch = recv.shape[1]
            self.place = slice(off, off + size)
            base, self.sums = 0, []
            for j, bit in enumerate(order):
                rest = [0]
                for k in order[j + 1 :]:
                    rest = rest + [s | k for s in rest]
                copies = []
                for i, s in enumerate(rest):
                    mine = masked(q, s)
                    slot = recv.at[base + i, self.place]
                    copies.append((mine, base + i, rcopy(ref.at[self.at(flip(mine, bit))], slot, col(bit))))
                base += len(rest)
                self.sums.append(copies)
            own, out = ref.at[self.at(q)], hbm.at[self.at(q)]
            self.trade = rcopy(own, far.at[self.place], sigma)
            self.join = rcopy(own, near.at[self.place], core)
            self.own = lcopy(own, out)
            self.own_core = rcopy(own, out, core)
            done, self.spreads = [0], []
            for bit in order:
                copies = []
                for s in done:
                    owner = masked(q, s)
                    src = own if s == 0 else hbm.at[self.at(owner)]
                    got = hbm.at[self.at(flip(owner, bit))]
                    copies.append((rcopy(src, hbm.at[self.at(owner)], col(bit)), rcopy(got, got, core)))
                self.spreads.append(copies)
                done = done + [s | bit for s in done]
            self.steps = [self.send_first, self.add_send, self.add_trade, self.take_join, self.join_spread]
            self.steps += [functools.partial(self.spread, j) for j in range(len(self.spreads))]
            self.done = 0

        def at(self, owner):
            return rows(owner * self.ch + self.off, self.size)

        def run(self, upto):
            while self.done < min(upto, len(self.steps)):
                self.steps[self.done]()
                self.done += 1

        def by_rows(self, owner, more, plain=False):
            base = owner * self.ch + self.off

            def body(i, carry):
                r = rows(base + i * 16, 16)
                other = more[rows(self.off + i * 16, 16), :]
                if not plain:
                    other = (self.ref[r, :].astype(F32) + other.astype(F32)).astype(BF)
                self.ref[r, :] = other
                return carry

            lax.fori_loop(0, self.size // 16, body, 0)

        def add(self, j):
            for mine, slot, cp in self.sums[j]:
                cp.wait_recv()
                self.by_rows(mine, self.recv.at[slot])
                pending.append(cp)

        def send_first(self):
            for _, _, cp in self.sums[0]:
                cp.start()

        def add_send(self):
            self.add(0)
            for _, _, cp in self.sums[1]:
                cp.start()

        def add_trade(self):
            self.add(1)
            swapped(self.trade.start)

        def take_join(self):
            def go():
                self.trade.wait()
                self.by_rows(q, self.far, plain=True)

            swapped(go)
            pl.when(c != self.fin)(self.join.start)

        def join_spread(self):
            def take():
                self.join.wait_recv()
                self.by_rows(q, self.near)
                for cp, _ in self.spreads[0]:
                    cp.start()
                self.own_core.start()
                self.own.start()

            pl.when(c == self.fin)(take)

        def spread(self, j):
            def go():
                for cp, _ in self.spreads[j]:
                    cp.wait_recv()
                if j + 1 < len(self.spreads):
                    for cp, _ in self.spreads[j + 1]:
                        cp.start()
                for _, cp in self.spreads[j]:
                    cp.start()

            pl.when(c == self.fin)(go)

        def finish(self):
            def owner():
                self.own.wait()
                self.own_core.wait_send()
                for copies in self.spreads:
                    for a, f in copies:
                        a.wait_send()
                        f.wait_send()

            def other():
                self.join.wait_send()
                self.own_core.wait_recv()
                for copies in self.spreads:
                    for _, f in copies:
                        f.wait_recv()

            pl.when(c == self.fin)(owner)
            pl.when(c != self.fin)(other)

    def pieces(ref, recv, far, near, hbm, n):
        return [Piece(ref, recv, far, near, hbm, *p) for p in parts_of(recv.shape[1], n)]

    def wave(group, last):
        first = min(p.done for p in group)
        for t in range(first, last + len(group)):
            for i, p in enumerate(group):
                p.run(min(last, t - i + 1))

    def sweep(group, last):
        for t in range(min(p.done for p in group), last):
            for p in group:
                p.run(t + 1)

    wq, wo = Weight(wq_hbm, WQ, 4, wq_end), Weight(wo_hbm, WO, 2)
    wu, wd = Weight(wu_hbm, WU, 4), Weight(wd_hbm, WD, 4)
    other_b = zl + 2 * (1 - c)
    x_swap = [rcopy(x_hbm.at[m], XS.at[m], sigma) for m in range(micro)]
    x_load = [lcopy(x_hbm.at[m], XS.at[m]) for m in range(micro)]
    c_swap = [rcopy(c_hbm.at[m], CS.at[m], sigma) for m in range(micro)]
    c_load = [lcopy(c_hbm.at[m], CS.at[m]) for m in range(micro)]
    lab_swap = rcopy(seg_ref, LAB.at[other_b], sigma)
    lab_gather = Gather(lambda j: LAB.at[j])
    a1_gather = [gather_rows(A1, m) for m in range(micro)]
    gb_gather = [gather_rows(GB, m) for m in range(micro)]
    a2_gather = [gather_rows(A2, m) for m in range(micro)]
    dhb_gather = [gather_rows(DHB, m) for m in range(micro)]
    attn_sum = [Scatter(2 * m) for m in range(micro)]
    mid_sum = [Scatter(2 * m) for m in range(micro)]
    y_sum = [Scatter(2 * m + 1) for m in range(micro)]
    in_sum = [Scatter(2 * m) for m in range(micro)]
    gd = pieces(GD, RD, SD, KD, gd_hbm, 2)
    gu = pieces(GU, RU, SU, KU, gu_hbm, 2)
    gq = pieces(WU, RQ, SQ, KQ, gq_hbm, 2)
    go = pieces(WD, RO, SO, KO, go_hbm, 2)
    out_swap = [rcopy(OB.at[m], out_hbm.at[m], sigma) for m in range(micro)]
    out_keep = [lcopy(OB.at[m], out_hbm.at[m]) for m in range(micro)]
    ig_swap = [rcopy(XS.at[m], CS.at[m], sigma) for m in range(micro)]
    ig_keep = [lcopy(DH.at[m], ig_hbm.at[m]) for m in range(micro)]
    sum_copies = [rcopy(NG, NR.at[i], p) for i, p in enumerate((sigma, xpeer, ypeer, zpeer, core))]

    def widen():
        for i, ref in enumerate((n1g, n1b, n2g, n2b)):
            NW[i] = jnp.transpose(jnp.broadcast_to(ref[...].reshape(1, width), (tok, width)))

    def first_norm(m):
        swapped(x_swap[m].wait_recv)
        kept(x_load[m].wait)
        xhat, _ = normed(XS[m].astype(F32))
        A1[m * 4 + b] = (xhat * NW[0] + NW[1]).astype(BF)
        a1_gather[m].start()

    def loss_grad(m):
        swapped(c_swap[m].wait_recv)
        kept(c_load[m].wait)
        labels = LAB[b]
        live = (labels[m : m + 1, :] >= 0).astype(F32)
        GB[m * 4 + b] = (CS[m].astype(F32) * live).astype(BF)
        gb_gather[m].start()

    def labels_wide():
        for m in range(micro):
            for j in range(4):
                lab = LAB[j, m : m + 1, :].astype(F32)
                LT[m, j * tok : (j + 1) * tok, :] = jnp.transpose(jnp.broadcast_to(lab, (tok, tok)))

    def make_bias(m):
        for j in range(4):
            lab = LAB[j, m : m + 1, :].astype(F32)
            place_k = lax.broadcasted_iota(jnp.int32, (row, tok), 0)
            place_q = lax.broadcasted_iota(jnp.int32, (row, tok), 1) + j * tok
            ok = (LT[m] == lab) & (place_k <= place_q)
            BIAS[:, j * tok : (j + 1) * tok] = jnp.where(ok, 0.0, -1e30)

    def whole(ref, m):
        return jnp.concatenate([ref[m * 4 + j] for j in range(4)], axis=1)

    def both(ref):
        return jnp.concatenate([ref[j] for j in range(ref.shape[0])], axis=1)

    def pair(ref, m, i, j):
        return jnp.concatenate([ref[m, :, cols(i)], ref[m, :, cols(j)]], axis=1)

    def project(m):
        QKV[m] = dg(WQ[0 : 3 * local_width, :], whole(A1, m), NN).astype(BF)

    def head_slices(h, qb):
        e = [slice(i * local_width + h * HD, i * local_width + (h + 1) * HD) for i in range(3)]
        return slice(qb * half, (qb + 1) * half), slice(0, (qb + 1) * half), *e

    def attend(m):
        for h in range(heads):
            for qb, PB in ((0, PB0), (1, PB1)):
                at, upto, eq, ek, ev = head_slices(h, qb)
                s = dg(QKV[m, ek, upto], QKV[m, eq, at], TN) * scale + BIAS[upto, at]
                e = jnp.exp(s - jnp.max(s, axis=0, keepdims=True))
                p = (e * (1.0 / jnp.sum(e, axis=0, keepdims=True))).astype(BF)
                PB[m, h] = p
                O[m, eq, at] = dg(QKV[m, ev, upto], p, NN).astype(BF)

    def heads_back(m):
        DO[m] = dg(WO[0:local_width, :], whole(DHB, m), NN).astype(BF)
        for h in range(heads):
            for qb, PB in ((1, PB1), (0, PB0)):
                at, upto, eq, ek, ev = head_slices(h, qb)
                qv, do, pb, kv = QKV[m, eq, at], DO[m, eq, at], PB[m, h], QKV[m, ek, upto]
                p = pb.astype(F32)
                pdp = p * dg(QKV[m, ev, upto], do, TN)
                ds = (pdp - p * jnp.sum(pdp, axis=0, keepdims=True)).astype(BF)
                dq = (dg(kv, ds, NN) * scale).astype(BF)
                dk, dv = dg(qv, ds, NT), dg(do, pb, NT)
                if qb == 1:
                    dq1, dk1, dv1, at1 = dq, dk, dv, at
                else:
                    QKV[m, eq, at] = dq
                    QKV[m, eq, at1] = dq1
                    QKV[m, ek, at] = ((dk1[:, :half] + dk) * scale).astype(BF)
                    QKV[m, ek, at1] = (dk1[:, half:] * scale).astype(BF)
                    QKV[m, ev, at] = (dv1[:, :half] + dv).astype(BF)
                    QKV[m, ev, at1] = dv1[:, half:].astype(BF)

    def second_norm(m, total):
        h = XS[m].astype(F32) + total
        HS[m] = h
        xhat, _ = normed(h)
        A2[m * 4 + b] = (xhat * NW[2] + NW[3]).astype(BF)
        a2_gather[m].start()

    def up(m):
        c0 = 0.7978845608028654
        step = 32

        def side(j, carry):
            blocks = jnp.concatenate([A2[m * 4 + 2 * j], A2[m * 4 + 2 * j + 1]], axis=1)
            U[...] = dg(WU[0:width, :], blocks, TN)
            at = pl.ds(pl.multiple_of(j * half, half), half)

            def body(i, carry):
                r = rows(i * step, step, step)
                u = U[r, :]
                u2 = u * u
                t = jnp.tanh(c0 * u * (1.0 + 0.044715 * u2))
                hp = 0.5 * (1.0 + t)
                Z[m, r, at] = (u * hp).astype(BF)
                GP[m, r, at] = (hp + (0.5 * c0) * u * (1.0 - t * t) * (1.0 + (3 * 0.044715) * u2)).astype(BF)
                return carry

            return lax.fori_loop(0, ff // step, body, carry)

        lax.fori_loop(0, 2, side, 0)

    def down_back(m):
        dz = dg(WD[0:ff, :], whole(GB, m), NN)
        GP[m] = (dz * GP[m].astype(F32)).astype(BF)

    def over_tokens(v):
        ones = jnp.ones((8, tok), BF)
        high = v.astype(BF)
        low = (v - high.astype(F32)).astype(BF)
        return (dg(ones, high, NT) + dg(ones, low, NT))[0:1, :]

    def norm_back(v, gain, grad, i):
        xhat, rstd = normed(v)
        dn = grad * gain
        dv = rstd * (
            dn - jnp.mean(dn, axis=0, keepdims=True) - xhat * jnp.mean(dn * xhat, axis=0, keepdims=True)
        )
        return dv, grad * xhat

    def second_norm_back(m, total):
        dv, gains = norm_back(HS[m], NW[2], total, 2)
        dh = GB[m * 4 + b].astype(F32) + dv
        DH[m] = dh
        DHB[m * 4 + b] = dh.astype(BF)
        dhb_gather[m].start()
        NG[2:3, :] += over_tokens(gains)
        NG[3:4, :] += over_tokens(total)

    def first_norm_back(m, total):
        dv, gains = norm_back(XS[m].astype(F32), NW[0], total, 0)
        DH[m] = DH[m] + dv
        NG[0:1, :] += over_tokens(gains)
        NG[1:2, :] += over_tokens(total)

    def give_input_grad(m):
        @pl.when(sw)
        def _():
            XS[m] = DH[m].astype(BF)
            ig_swap[m].start()

        kept(ig_keep[m].start)

    def out_term(m):
        return lambda i, j: dg(WO[0:local_width, :], pair(O, m, i, j), TN)

    def y_term(m):
        return lambda i, j: dg(WD[0:ff, :], pair(Z, m, i, j), TN)

    def mid_term(m):
        return lambda i, j: dg(WU[0:width, :], pair(GP, m, i, j), NN)

    def in_term(m):
        return lambda i, j: dg(WQ[0 : 3 * local_width, :], pair(QKV, m, i, j), TN)

    def give_output(m):
        OB[m] = (HS[m] + y_sum[m].finish()).astype(BF)
        swapped(out_swap[m].start)
        kept(out_keep[m].start)

    def sum_add(i):
        sum_copies[i].wait()
        NG[...] = NG[...] + NR[i]

    def place(ref, height, value):
        n, m = value.shape
        ref[0:n, 0:m] = value.astype(BF)
        ref[n:height, :] = jnp.zeros((height - n, ref.shape[1]), BF)
        if m < ref.shape[1]:
            ref[0:n, m:] = jnp.zeros((n, ref.shape[1] - m), BF)

    def micros(ref):
        return jnp.concatenate([ref[m] for m in range(micro)], axis=1)

    def begin(w, i):
        swapped(lambda: w.first(w.hops[i], lambda cp: cp.start()))

    def hop(w, i, j):
        swapped(lambda: w.pass_on(w.hops[i], j))

    swapped(lab_swap.start, x_swap[0].start)
    begin(wq, 0)
    begin(wq, 1)
    kept(*[cp.start for cp in x_load])
    for w in (wq, wo, wu, wd):
        w.load()
    kept(*[cp.start for cp in c_load])

    @pl.when(jnp.logical_not(sw))
    def _():
        LAB[b] = seg_ref[...]

    NG[...] = jnp.zeros_like(NG)
    widen()
    swapped(lab_swap.wait_recv)
    lab_gather.start()
    first_norm(0)
    begin(wq, 2)
    kept(lambda: first_norm(1))
    lab_gather.forward()
    hop(wq, 0, 0)
    begin(wq, 3)
    a1_gather[0].forward()
    hop(wq, 1, 0)
    begin(wo, 0)
    hop(wq, 0, 1)
    lab_gather.finish()
    labels_wide()
    make_bias(0)
    hop(wq, 2, 0)
    begin(wo, 1)
    hop(wq, 1, 1)
    hop(wq, 3, 0)
    swapped(x_swap[1].start)
    hop(wq, 2, 1)
    hop(wo, 0, 0)
    begin(wu, 0)
    hop(wq, 3, 1)
    hop(wo, 1, 0)
    begin(wu, 1)
    a1_gather[0].finish()
    kept(lambda: loss_grad(0), lambda: loss_grad(1))
    wq.finish()

    project(0)
    hop(wo, 0, 1)
    hop(wo, 1, 1)
    attend(0)
    swapped(lambda: first_norm(1))
    begin(wu, 2)
    wo.finish()
    attn_sum[0].start(out_term(0))
    hop(wu, 0, 0)
    begin(wu, 3)
    a1_gather[1].forward()
    hop(wu, 1, 0)
    swapped(c_swap[0].start)
    hop(wu, 0, 1)
    make_bias(1)
    a1_gather[1].finish()
    project(1)
    hop(wu, 2, 0)
    swapped(c_swap[1].start)
    hop(wu, 1, 1)
    attend(1)
    attn_sum[1].start(out_term(1))
    hop(wu, 3, 0)
    begin(wd, 0)
    hop(wu, 2, 1)
    second_norm(0, attn_sum[0].finish())
    swapped(lambda: loss_grad(0))
    begin(wd, 1)
    hop(wu, 3, 1)
    second_norm(1, attn_sum[1].finish())
    a2_gather[0].forward()
    swapped(lambda: loss_grad(1))
    begin(wd, 2)
    wu.finish()
    a2_gather[0].finish()
    up(0)
    hop(wd, 0, 0)
    begin(wd, 3)
    a2_gather[1].forward()
    hop(wd, 1, 0)
    hop(wd, 0, 1)
    a2_gather[1].finish()
    up(1)
    gb_gather[0].forward()
    hop(wd, 2, 0)
    hop(wd, 1, 1)
    gb_gather[1].forward()
    hop(wd, 3, 0)
    hop(wd, 2, 1)
    gb_gather[0].finish()
    gb_gather[1].finish()
    hop(wd, 3, 1)
    place(GD, GD.shape[0], dg(micros(Z), both(GB), NT))
    wave(gd, 1)
    wd.finish()

    down_back(0)
    mid_sum[0].start(mid_term(0))
    down_back(1)
    mid_sum[1].start(mid_term(1))
    place(GU, GU.shape[0], dg(both(A2), micros(GP), NT))
    second_norm_back(0, mid_sum[0].finish())
    wave(gd, 2)
    wave(gu, 1)
    second_norm_back(1, mid_sum[1].finish())
    for w in (wq, wo, wu, wd):
        w.sent()
    y_sum[0].start(y_term(0))
    dhb_gather[0].forward()
    dhb_gather[0].finish()
    heads_back(0)
    wave(gd, 3)
    y_sum[1].start(y_term(1))
    dhb_gather[1].forward()
    in_sum[0].start(in_term(0))
    dhb_gather[1].finish()
    place(WD, go[0].ch * COLS, dg(micros(O), both(DHB), NT))
    wave(go, 1)
    heads_back(1)
    wave(gu, 2)
    in_sum[1].start(in_term(1))
    place(WU, gq[0].ch * COLS, dg(micros(QKV), both(A1), NT))
    wave(gq, 1)
    give_output(0)
    wave(go, 2)
    wave(gu, 3)
    wave(gd, 4)
    wave(go, 3)
    wave(gq, 2)
    wave(gd, 5)
    wave(gq, 3)
    give_output(1)
    wave(gu, 5)
    wave(gd, 6)
    first_norm_back(0, in_sum[0].finish())
    first_norm_back(1, in_sum[1].finish())
    sum_copies[0].start()
    give_input_grad(0)
    give_input_grad(1)
    wave(gd, 7)
    wave(gu, 6)
    sweep(gq + go, 4)
    sum_add(0)
    sum_copies[1].start()
    sweep(gq + go, 5)
    wave(gu, 7)
    sum_add(1)
    sum_copies[2].start()
    sweep(gq + go, 6)
    sum_add(2)
    sum_copies[3].start()
    sum_add(3)
    sum_copies[4].start()
    sweep(gq + go, 7)
    sum_add(4)
    ng_ref[...] = NG[...]
    for m in range(micro):

        @pl.when(sw)
        def _():
            ig_swap[m].wait()
            DH[m] = CS[m].astype(F32)
            ig_keep[m].start()
            out_swap[m].wait()
            x_swap[m].wait_send()
            c_swap[m].wait_send()

        ig_keep[m].wait()
        kept(out_keep[m].wait)
    swapped(lab_swap.wait_send)
    for cp in pending:
        cp.wait_send()
    for p in gd + gu + gq + go:
        p.finish()


def layer(
    inputs, segments, norm1_gain, norm1_bias, qkv_weight, out_weight, norm2_gain, norm2_bias, up_weight, down_weight,
    cotangent,
):
    micro, tok, width = inputs.shape
    local_width = qkv_weight.shape[2]
    ff = up_weight.shape[1]
    row = 4 * tok
    heads = local_width // HD
    three = 3 * local_width
    lw, lf = up_to(width, 128), up_to(ff, 128)
    half = row // 2
    cq, co, cu, cd = chunk_rows(three), chunk_rows(local_width), chunk_rows(width), chunk_rows(ff)
    wq = jnp.transpose(qkv_weight, (0, 2, 1)).reshape(three, width)

    def tall(w, height):
        return jnp.pad(w, ((0, height - w.shape[0]), (0, 0)))

    def v(shape, dtype=BF):
        return pltpu.VMEM(shape, dtype)

    def recv(ch, lanes):
        return v((COLS - 1, ch, lanes))

    any_spec = pl.BlockSpec(memory_space=pl.ANY)
    vmem = pl.BlockSpec(memory_space=pltpu.VMEM)
    block = (width, tok)
    scratch = [
        v((COLS * cq, width)), v((COLS * co, width)), v((COLS * cu, ff)), v((COLS * cd, width)),
        v((COLS * cu, lf)), v((COLS * cd, lw)),
        recv(cq, width), recv(co, width), recv(cu, lf), recv(cd, lw),
        v((cq, width)), v((co, width)), v((cu, lf)), v((cd, lw)),
        v((cq, width)), v((co, width)), v((cu, lf)), v((cd, lw)),
        v((micro, *block)), v((micro, *block)), v((4, micro, tok), jnp.int32), v((micro, row, tok), F32),
        v((row, row), F32), v((4, *block), F32),
        v((4 * micro, *block)), v((micro, three, row)),
        v((micro, heads, half, half)), v((micro, heads, row, half)), v((micro, local_width, row)),
        v((micro, *block), F32),
        v((4 * micro, *block)), v((micro, ff, row)), v((micro, ff, row)), v((4 * micro, *block)),
        v((4 * micro, *block)), v((micro, local_width, row)), v((micro, *block), F32), v((ff, half), F32),
        v((2 * micro + 1, *block), F32),
        v((2 * micro, 2, *block)), v((2 * micro, *block)), v((2 * micro, 2, *block)), v((2 * micro, *block)),
        v((micro, *block)),
        v((8, width), F32), v((5, 8, width), F32),
        pltpu.SemaphoreType.DMA((NSEM,)), pltpu.SemaphoreType.DMA((NSEM,)), pltpu.SemaphoreType.DMA((23,)),
    ]
    out, input_grad, gq, go, gu, gd, ng = pl.pallas_call(
        kernel,
        out_shape=[
            jax.ShapeDtypeStruct((micro, *block), BF),
            jax.ShapeDtypeStruct((micro, *block), F32),
            jax.ShapeDtypeStruct((COLS * cq, width), BF),
            jax.ShapeDtypeStruct((COLS * co, width), BF),
            jax.ShapeDtypeStruct((COLS * cu, lf), BF),
            jax.ShapeDtypeStruct((COLS * cd, lw), BF),
            jax.ShapeDtypeStruct((8, width), F32),
        ],
        in_specs=[any_spec, vmem, vmem, vmem] + [any_spec] * 3 + [vmem, vmem] + [any_spec] * 3,
        out_specs=[any_spec] * 6 + [vmem],
        scratch_shapes=scratch,
        compiler_params=pltpu.CompilerParams(
            collective_id=0, has_side_effects=True, vmem_limit_bytes=64 * 1024 * 1024
        ),
    )(
        jnp.transpose(inputs, (0, 2, 1)), segments, norm1_gain, norm1_bias,
        wq, tall(wq[(COLS - 1) * cq :], cq), tall(out_weight, COLS * co), norm2_gain, norm2_bias, up_weight, down_weight,
        jnp.transpose(cotangent, (0, 2, 1)),
    )
    grads = (
        jnp.transpose(gq[:three].astype(F32).reshape(3, local_width, width), (0, 2, 1)),
        go[:local_width].astype(F32),
        gu[:width, :ff].astype(F32),
        gd[:ff, :width].astype(F32),
    )
    extent = lax.axis_size("dp")
    block = 2 * COLS
    if extent > block:
        groups = [[r + block * j for j in range(extent // block)] for r in range(block)]
        grads = lax.psum(grads, "dp", axis_index_groups=groups)
        ng = lax.psum(ng, "dp", axis_index_groups=groups)
    gq, go, gu, gd = grads
    out, input_grad = jnp.transpose(out, (0, 2, 1)), jnp.transpose(input_grad, (0, 2, 1))
    return out, input_grad, ng[0], ng[1], gq, go, ng[2], ng[3], gu, gd


def solution(mesh):
    tokens = P(None, ("dp", "tensor"), None)
    weights = (P(None, None, "tensor"), P("tensor", None))
    mlp = (P(None, "tensor"), P("tensor", None))
    return jax.shard_map(
        layer,
        mesh=mesh,
        in_specs=(tokens, P(None, ("dp", "tensor")), P(), P(), *weights, P(), P(), *mlp, tokens),
        out_specs=(tokens, tokens, P(), P(), *weights, P(), P(), *mlp),
        check_vma=False,
    )
```

```python
import functools

import jax
import jax.numpy as jnp
from jax import lax
from jax.experimental import pallas as pl
from jax.experimental.pallas import tpu as pltpu
from jax.sharding import PartitionSpec as P


HD = 56
BF = jnp.bfloat16
F32 = jnp.float32
MESH = pl.DeviceIdType.MESH
NN = (((1,), (0,)), ((), ()))
NT = (((1,), (1,)), ((), ()))
TN = (((0,), (0,)), ((), ()))
COLS = 4
BITS = (1, 2)
NSEM = 217


def up_to(n, m):
    return -(-n // m) * m


def chunk_rows(rows):
    return up_to(-(-rows // COLS), 16)


def parts_of(ch, n):
    out, off = [], 0
    for i in range(n):
        size = up_to(-(-(ch - off) // (n - i)), 16)
        out.append((off, size, BITS if i % 2 == 0 else BITS[::-1], i % 2))
        off += size
    return out


def dg(a, b, dims):
    return lax.dot_general(a, b, dims, preferred_element_type=F32)


def normed(v):
    center = v - jnp.mean(v, axis=0, keepdims=True)
    rstd = lax.rsqrt(jnp.mean(center * center, axis=0, keepdims=True) + 1e-05)
    return center * rstd, rstd


def kernel(
    x_hbm, seg_ref, n1g, n1b, wq_hbm, ends, wo_hbm, n2g, n2b, wu_hbm, wd_hbm, c_hbm,
    out_hbm, ig_hbm, gq_hbm, go_hbm, gu_hbm, gd_hbm, ng_ref,
    WQ, WO, WU, WD, GU, GD, RQ, RO, RU, RD, SQ, SO, SU, SD, KQ, KO, KU, KD,
    XS, CS, LAB, LT, BIAS, NW, A1, QKV, PB0, PB1, O, HS, A2, Z, GP, GB, DHB, DO, DH, U,
    T2, S1, SZ, R1, RZ, OB, NG, NR,
    ssem, rsem, lsem,
):
    d = lax.axis_index("dp")
    z = lax.axis_index("tensor")
    c = lax.rem(d, 2)
    q = lax.rem(d // 2, COLS)
    zl = lax.rem(z, 2)
    zh = z // 2
    b = zl + 2 * c
    sw = zh != c
    dc = d + 1 - 2 * c
    z1 = z + 1 - 2 * zl
    z2 = z + 2 - 4 * zh
    core = (dc, z)
    zpeer = (d, z1)
    sigma = (dc, z2)

    def flip(owner, bit):
        on = lax.rem(owner // bit, 2)
        return owner + bit * (1 - 2 * on)

    def col(bit):
        return (d + 2 * (flip(q, bit) - q), z)

    def masked(owner, s):
        for k in BITS:
            if s & k:
                owner = flip(owner, k)
        return owner

    xpeer, ypeer = col(1), col(2)
    micro, width, tok = XS.shape
    row = 4 * tok
    half = row // 2
    local_width = O.shape[1]
    ff = Z.shape[1]
    heads = local_width // HD
    scale = HD ** (-0.5)
    counts = dict(r=0, l=0)
    pending = []

    def rcopy(src, dst, peer):
        i = counts["r"]
        counts["r"] = i + 1
        assert i < NSEM
        return pltpu.make_async_remote_copy(
            src_ref=src, dst_ref=dst, send_sem=ssem.at[i], recv_sem=rsem.at[i], device_id=peer, device_id_type=MESH
        )

    def lcopy(src, dst):
        i = counts["l"]
        counts["l"] = i + 1
        return pltpu.make_async_copy(src, dst, lsem.at[i])

    def rows(start, size, step=16):
        return pl.ds(pl.multiple_of(start, step), size)

    def cols(j):
        return pl.ds(pl.multiple_of(j * tok, tok), tok)

    def swapped(*fs):
        @pl.when(sw)
        def _():
            for f in fs:
                f()

    def kept(*fs):
        @pl.when(jnp.logical_not(sw))
        def _():
            for f in fs:
                f()

    barrier = pltpu.get_barrier_semaphore()
    peers = (core, zpeer, sigma, xpeer, ypeer)
    for p in peers:
        pl.semaphore_signal(barrier, 1, device_id=p, device_id_type=MESH)
    pl.semaphore_wait(barrier, len(peers))

    class Gather:
        def __init__(self, view):
            self.own = view(b)
            self.cz = rcopy(view(b), view(b), zpeer)
            self.cc = rcopy(view(b), view(b), core)
            far = 1 - zl + 2 * c
            self.cf = rcopy(view(far), view(far), core)

        def start(self):
            self.cz.start()
            self.cc.start()

        def forward(self):
            self.cz.wait_recv()
            self.cf.start()

        def finish(self):
            self.cc.wait_recv()
            self.cf.wait_recv()
            pending.extend([self.cz, self.cc, self.cf])

    def gather_rows(ref, m):
        return Gather(lambda j: ref.at[m * 4 + j])

    class Scatter:
        def __init__(self, s):
            self.s = s
            self.idx = counts["r"]
            counts["r"] += 2
            self.cz = rcopy(SZ.at[s], RZ.at[s], zpeer)

        def give(self, i):
            return pltpu.make_async_remote_copy(
                src_ref=S1.at[self.s, i], dst_ref=R1.at[self.s, i], send_sem=ssem.at[self.idx + i],
                recv_sem=rsem.at[self.idx + i], device_id=core, device_id_type=MESH,
            )

        def start(self, term):
            s = self.s

            def body(i, carry):
                side = lax.rem(1 - zl + i, 2)
                part = term(side + 2 * (1 - c), side + 2 * c)
                S1[s, i] = part[:, :tok].astype(BF)
                T2[s * i + 2 * micro * (1 - i)] = part[:, tok:]
                self.give(i).start()
                return carry

            lax.fori_loop(0, 2, body, 0)
            self.give(0).wait_recv()
            SZ[s] = (T2[2 * micro] + R1[s, 0].astype(F32)).astype(BF)
            self.cz.start()

        def finish(self):
            s = self.s
            self.give(1).wait_recv()
            self.cz.wait_recv()
            total = T2[s] + R1[s, 1].astype(F32) + RZ[s].astype(F32)
            self.give(0).wait_send()
            self.give(1).wait_send()
            self.cz.wait_send()
            return total

    class Weight:
        def __init__(self, hbm, ref, n, end=None):
            ch = ref.shape[0] // COLS
            whole = hbm.shape[0] if end is None else (COLS - 1) * ch
            self.locals = [lcopy(hbm.at[0:whole], ref.at[0:whole])]
            if end is not None:
                self.locals.append(lcopy(end, ref.at[whole : whole + ch]))
            self.hops = []
            for off, size, order, _ in parts_of(ch, n):
                i = counts["r"]
                counts["r"] = i + 1

                def first(src, at, i=i):
                    return pltpu.make_async_remote_copy(
                        src_ref=src, dst_ref=ref.at[at], send_sem=ssem.at[i], recv_sem=rsem.at[i],
                        device_id=sigma, device_id_type=MESH,
                    )

                at = rows(q * ch + off, size)
                usual = first(hbm.at[at], at)
                last_at = (COLS - 1) * ch + off
                last_size = max(0, min(size, whole - last_at))
                at = slice(last_at, last_at + last_size)
                last = usual if last_size == size else first(hbm.at[at], at) if last_size else None
                if end is not None:
                    last = first(end.at[off : off + size], slice(last_at, last_at + size))
                steps, done = [], [0]
                for bit in order:
                    copies = []
                    for s in done:
                        at = rows(masked(q, s) * ch + off, size)
                        copies.append(rcopy(ref.at[at], ref.at[at], col(bit)))
                    steps.append(copies)
                    done = done + [s | bit for s in done]
                self.hops.append(((usual, last), steps))

        def first(self, hop, act):
            usual, last = hop[0]
            if last is usual:
                act(usual)
                return
            pl.when(q < COLS - 1)(lambda: act(usual))
            if last is not None:
                pl.when(q == COLS - 1)(lambda: act(last))

        def load(self):
            kept(*[cp.start for cp in self.locals])

        def pass_on(self, h, j):
            if j == 0:
                self.first(h, lambda cp: cp.wait_recv())
            else:
                for cp in h[1][j - 1]:
                    cp.wait_recv()
            for cp in h[1][j]:
                cp.start()

        def finish(self):
            def go():
                for h in self.hops:
                    for cp in h[1][-1]:
                        cp.wait_recv()

            swapped(go)
            kept(*[cp.wait for cp in self.locals])

        def sent(self):
            def go():
                for h in self.hops:
                    self.first(h, lambda cp: cp.wait_send())
                    for copies in h[1]:
                        for cp in copies:
                            cp.wait_send()

            swapped(go)

    class Piece:
        def __init__(self, ref, recv, far, near, hbm, off, size, order, fin):
            self.ref, self.recv, self.far, self.near, self.hbm = ref, recv, far, near, hbm
            self.off, self.size, self.fin = off, size, fin
            self.ch = recv.shape[1]
            self.place = slice(off, off + size)
            base, self.sums = 0, []
            for j, bit in enumerate(order):
                rest = [0]
                for k in order[j + 1 :]:
                    rest = rest + [s | k for s in rest]
                copies = []
                for i, s in enumerate(rest):
                    mine = masked(q, s)
                    slot = recv.at[base + i, self.place]
                    copies.append((mine, base + i, rcopy(ref.at[self.at(flip(mine, bit))], slot, col(bit))))
                base += len(rest)
                self.sums.append(copies)
            own, out = ref.at[self.at(q)], hbm.at[self.at(q)]
            self.trade = rcopy(own, far.at[self.place], sigma)
            self.join = rcopy(own, near.at[self.place], core)
            self.own = lcopy(own, out)
            self.own_core = rcopy(own, out, core)
            done, self.spreads = [0], []
            for bit in order:
                copies = []
                for s in done:
                    owner = masked(q, s)
                    src = own if s == 0 else hbm.at[self.at(owner)]
                    got = hbm.at[self.at(flip(owner, bit))]
                    copies.append((rcopy(src, hbm.at[self.at(owner)], col(bit)), rcopy(got, got, core)))
                self.spreads.append(copies)
                done = done + [s | bit for s in done]
            self.steps = [self.send_first, self.add_send, self.add_trade, self.take_join, self.join_spread]
            self.steps += [functools.partial(self.spread, j) for j in range(len(self.spreads))]
            self.done = 0

        def at(self, owner):
            return rows(owner * self.ch + self.off, self.size)

        def run(self, upto):
            while self.done < min(upto, len(self.steps)):
                self.steps[self.done]()
                self.done += 1

        def by_rows(self, owner, more, plain=False):
            base = owner * self.ch + self.off

            def body(i, carry):
                r = rows(base + i * 16, 16)
                other = more[rows(self.off + i * 16, 16), :]
                if not plain:
                    other = (self.ref[r, :].astype(F32) + other.astype(F32)).astype(BF)
                self.ref[r, :] = other
                return carry

            lax.fori_loop(0, self.size // 16, body, 0)

        def add(self, j):
            for mine, slot, cp in self.sums[j]:
                cp.wait_recv()
                self.by_rows(mine, self.recv.at[slot])
                pending.append(cp)

        def send_first(self):
            for _, _, cp in self.sums[0]:
                cp.start()

        def add_send(self):
            self.add(0)
            for _, _, cp in self.sums[1]:
                cp.start()

        def add_trade(self):
            self.add(1)
            swapped(self.trade.start)

        def take_join(self):
            def go():
                self.trade.wait()
                self.by_rows(q, self.far, plain=True)

            swapped(go)
            pl.when(c != self.fin)(self.join.start)

        def join_spread(self):
            def take():
                self.join.wait_recv()
                self.by_rows(q, self.near)
                for cp, _ in self.spreads[0]:
                    cp.start()
                self.own_core.start()
                self.own.start()

            pl.when(c == self.fin)(take)

        def spread(self, j):
            def go():
                for cp, _ in self.spreads[j]:
                    cp.wait_recv()
                if j + 1 < len(self.spreads):
                    for cp, _ in self.spreads[j + 1]:
                        cp.start()
                for _, cp in self.spreads[j]:
                    cp.start()

            pl.when(c == self.fin)(go)

        def finish(self):
            def owner():
                self.own.wait()
                self.own_core.wait_send()
                for copies in self.spreads:
                    for a, f in copies:
                        a.wait_send()
                        f.wait_send()

            def other():
                self.join.wait_send()
                self.own_core.wait_recv()
                for copies in self.spreads:
                    for _, f in copies:
                        f.wait_recv()

            pl.when(c == self.fin)(owner)
            pl.when(c != self.fin)(other)

    def pieces(ref, recv, far, near, hbm, n):
        return [Piece(ref, recv, far, near, hbm, *p) for p in parts_of(recv.shape[1], n)]

    def wave(group, last):
        first = min(p.done for p in group)
        for t in range(first, last + len(group)):
            for i, p in enumerate(group):
                p.run(min(last, t - i + 1))

    def sweep(group, last):
        for t in range(min(p.done for p in group), last):
            for p in group:
                p.run(t + 1)

    wq = Weight(wq_hbm, WQ, 4, ends.at[0 : WQ.shape[0] // COLS])
    wo = Weight(wo_hbm, WO, 2, ends.at[WQ.shape[0] // COLS :])
    wu, wd = Weight(wu_hbm, WU, 4), Weight(wd_hbm, WD, 4)
    other_b = zl + 2 * (1 - c)
    x_swap = [rcopy(x_hbm.at[m], XS.at[m], sigma) for m in range(micro)]
    x_load = [lcopy(x_hbm.at[m], XS.at[m]) for m in range(micro)]
    c_swap = [rcopy(c_hbm.at[m], CS.at[m], sigma) for m in range(micro)]
    c_load = [lcopy(c_hbm.at[m], CS.at[m]) for m in range(micro)]
    lab_swap = rcopy(seg_ref, LAB.at[other_b], sigma)
    lab_gather = Gather(lambda j: LAB.at[j])
    a1_gather = [gather_rows(A1, m) for m in range(micro)]
    gb_gather = [gather_rows(GB, m) for m in range(micro)]
    a2_gather = [gather_rows(A2, m) for m in range(micro)]
    dhb_gather = [gather_rows(DHB, m) for m in range(micro)]
    attn_sum = [Scatter(2 * m) for m in range(micro)]
    mid_sum = [Scatter(2 * m) for m in range(micro)]
    y_sum = [Scatter(2 * m + 1) for m in range(micro)]
    in_sum = [Scatter(2 * m) for m in range(micro)]
    gd = pieces(GD, RD, SD, KD, gd_hbm, 2)
    gu = pieces(GU, RU, SU, KU, gu_hbm, 2)
    gq = pieces(WU, RQ, SQ, KQ, gq_hbm, 2)
    go = pieces(WD, RO, SO, KO, go_hbm, 2)
    out_swap = [rcopy(OB.at[m], out_hbm.at[m], sigma) for m in range(micro)]
    out_keep = [lcopy(OB.at[m], out_hbm.at[m]) for m in range(micro)]
    ig_swap = [rcopy(XS.at[m], CS.at[m], sigma) for m in range(micro)]
    ig_keep = [lcopy(DH.at[m], ig_hbm.at[m]) for m in range(micro)]
    sum_copies = [rcopy(NG, NR.at[i], p) for i, p in enumerate((sigma, xpeer, ypeer, zpeer, core))]

    def widen():
        for i, ref in enumerate((n1g, n1b, n2g, n2b)):
            NW[i] = jnp.transpose(jnp.broadcast_to(ref[...].reshape(1, width), (tok, width)))

    def first_norm(m):
        swapped(x_swap[m].wait_recv)
        kept(x_load[m].wait)
        xhat, _ = normed(XS[m].astype(F32))
        A1[m * 4 + b] = (xhat * NW[0] + NW[1]).astype(BF)
        a1_gather[m].start()

    def loss_grad(m):
        swapped(c_swap[m].wait_recv)
        kept(c_load[m].wait)
        labels = LAB[b]
        live = (labels[m : m + 1, :] >= 0).astype(F32)
        GB[m * 4 + b] = (CS[m].astype(F32) * live).astype(BF)
        gb_gather[m].start()

    def labels_wide():
        for m in range(micro):
            for j in range(4):
                lab = LAB[j, m : m + 1, :].astype(F32)
                LT[m, j * tok : (j + 1) * tok, :] = jnp.transpose(jnp.broadcast_to(lab, (tok, tok)))

    def make_bias(m):
        for j in range(4):
            lab = LAB[j, m : m + 1, :].astype(F32)
            place_k = lax.broadcasted_iota(jnp.int32, (row, tok), 0)
            place_q = lax.broadcasted_iota(jnp.int32, (row, tok), 1) + j * tok
            ok = (LT[m] == lab) & (place_k <= place_q)
            BIAS[:, j * tok : (j + 1) * tok] = jnp.where(ok, 0.0, -1e30)

    def whole(ref, m):
        return jnp.concatenate([ref[m * 4 + j] for j in range(4)], axis=1)

    def both(ref):
        return jnp.concatenate([ref[j] for j in range(ref.shape[0])], axis=1)

    def pair(ref, m, i, j):
        return jnp.concatenate([ref[m, :, cols(i)], ref[m, :, cols(j)]], axis=1)

    def project(m):
        QKV[m] = dg(WQ[0 : 3 * local_width, :], whole(A1, m), NN).astype(BF)

    def head_slices(h, qb):
        e = [slice(i * local_width + h * HD, i * local_width + (h + 1) * HD) for i in range(3)]
        return slice(qb * half, (qb + 1) * half), slice(0, (qb + 1) * half), *e

    def attend(m):
        for h in range(heads):
            for qb, PB in ((0, PB0), (1, PB1)):
                at, upto, eq, ek, ev = head_slices(h, qb)
                s = dg(QKV[m, ek, upto], QKV[m, eq, at], TN) * scale + BIAS[upto, at]
                e = jnp.exp(s - jnp.max(s, axis=0, keepdims=True))
                p = (e * (1.0 / jnp.sum(e, axis=0, keepdims=True))).astype(BF)
                PB[m, h] = p
                O[m, eq, at] = dg(QKV[m, ev, upto], p, NN).astype(BF)

    def heads_back(m):
        DO[m] = dg(WO[0:local_width, :], whole(DHB, m), NN).astype(BF)
        for h in range(heads):
            for qb, PB in ((1, PB1), (0, PB0)):
                at, upto, eq, ek, ev = head_slices(h, qb)
                qv, do, pb, kv = QKV[m, eq, at], DO[m, eq, at], PB[m, h], QKV[m, ek, upto]
                p = pb.astype(F32)
                pdp = p * dg(QKV[m, ev, upto], do, TN)
                ds = (pdp - p * jnp.sum(pdp, axis=0, keepdims=True)).astype(BF)
                dq = (dg(kv, ds, NN) * scale).astype(BF)
                dk, dv = dg(qv, ds, NT), dg(do, pb, NT)
                if qb == 1:
                    dq1, dk1, dv1, at1 = dq, dk, dv, at
                else:
                    QKV[m, eq, at] = dq
                    QKV[m, eq, at1] = dq1
                    QKV[m, ek, at] = ((dk1[:, :half] + dk) * scale).astype(BF)
                    QKV[m, ek, at1] = (dk1[:, half:] * scale).astype(BF)
                    QKV[m, ev, at] = (dv1[:, :half] + dv).astype(BF)
                    QKV[m, ev, at1] = dv1[:, half:].astype(BF)

    def second_norm(m, total):
        h = XS[m].astype(F32) + total
        HS[m] = h
        xhat, _ = normed(h)
        A2[m * 4 + b] = (xhat * NW[2] + NW[3]).astype(BF)
        a2_gather[m].start()

    def up(m):
        c0 = 0.7978845608028654
        step = 32

        def side(j, carry):
            blocks = jnp.concatenate([A2[m * 4 + 2 * j], A2[m * 4 + 2 * j + 1]], axis=1)
            U[...] = dg(WU[0:width, :], blocks, TN)
            at = pl.ds(pl.multiple_of(j * half, half), half)

            def body(i, carry):
                r = rows(i * step, step, step)
                u = U[r, :]
                u2 = u * u
                t = jnp.tanh(c0 * u * (1.0 + 0.044715 * u2))
                hp = 0.5 * (1.0 + t)
                Z[m, r, at] = (u * hp).astype(BF)
                GP[m, r, at] = (hp + (0.5 * c0) * u * (1.0 - t * t) * (1.0 + (3 * 0.044715) * u2)).astype(BF)
                return carry

            return lax.fori_loop(0, ff // step, body, carry)

        lax.fori_loop(0, 2, side, 0)

    def down_back(m):
        dz = dg(WD[0:ff, :], whole(GB, m), NN)
        GP[m] = (dz * GP[m].astype(F32)).astype(BF)

    def over_tokens(v):
        ones = jnp.ones((8, tok), BF)
        high = v.astype(BF)
        low = (v - high.astype(F32)).astype(BF)
        return (dg(ones, high, NT) + dg(ones, low, NT))[0:1, :]

    def norm_back(v, gain, grad, i):
        xhat, rstd = normed(v)
        dn = grad * gain
        dv = rstd * (
            dn - jnp.mean(dn, axis=0, keepdims=True) - xhat * jnp.mean(dn * xhat, axis=0, keepdims=True)
        )
        return dv, grad * xhat

    def second_norm_back(m, total):
        dv, gains = norm_back(HS[m], NW[2], total, 2)
        dh = GB[m * 4 + b].astype(F32) + dv
        DH[m] = dh
        DHB[m * 4 + b] = dh.astype(BF)
        dhb_gather[m].start()
        NG[2:3, :] += over_tokens(gains)
        NG[3:4, :] += over_tokens(total)

    def first_norm_back(m, total):
        dv, gains = norm_back(XS[m].astype(F32), NW[0], total, 0)
        DH[m] = DH[m] + dv
        NG[0:1, :] += over_tokens(gains)
        NG[1:2, :] += over_tokens(total)

    def give_input_grad(m):
        @pl.when(sw)
        def _():
            XS[m] = DH[m].astype(BF)
            ig_swap[m].start()

        kept(ig_keep[m].start)

    def out_term(m):
        return lambda i, j: dg(WO[0:local_width, :], pair(O, m, i, j), TN)

    def y_term(m):
        return lambda i, j: dg(WD[0:ff, :], pair(Z, m, i, j), TN)

    def mid_term(m):
        return lambda i, j: dg(WU[0:width, :], pair(GP, m, i, j), NN)

    def in_term(m):
        return lambda i, j: dg(WQ[0 : 3 * local_width, :], pair(QKV, m, i, j), TN)

    def give_output(m):
        OB[m] = (HS[m] + y_sum[m].finish()).astype(BF)
        swapped(out_swap[m].start)
        kept(out_keep[m].start)

    def sum_add(i):
        sum_copies[i].wait()
        NG[...] = NG[...] + NR[i]

    def place(ref, height, value):
        n, m = value.shape
        ref[0:n, 0:m] = value.astype(BF)
        ref[n:height, :] = jnp.zeros((height - n, ref.shape[1]), BF)
        if m < ref.shape[1]:
            ref[0:n, m:] = jnp.zeros((n, ref.shape[1] - m), BF)

    def micros(ref):
        return jnp.concatenate([ref[m] for m in range(micro)], axis=1)

    def begin(w, i):
        swapped(lambda: w.first(w.hops[i], lambda cp: cp.start()))

    def hop(w, i, j):
        swapped(lambda: w.pass_on(w.hops[i], j))

    swapped(lab_swap.start, x_swap[0].start)
    begin(wq, 0)
    begin(wq, 1)
    kept(*[cp.start for cp in x_load])
    for w in (wq, wo, wu, wd):
        w.load()
    kept(*[cp.start for cp in c_load])

    @pl.when(jnp.logical_not(sw))
    def _():
        LAB[b] = seg_ref[...]

    NG[...] = jnp.zeros_like(NG)
    widen()
    swapped(lab_swap.wait_recv)
    lab_gather.start()
    first_norm(0)
    begin(wq, 2)
    kept(lambda: first_norm(1))
    lab_gather.forward()
    hop(wq, 0, 0)
    begin(wq, 3)
    a1_gather[0].forward()
    hop(wq, 1, 0)
    begin(wo, 0)
    hop(wq, 0, 1)
    lab_gather.finish()
    labels_wide()
    make_bias(0)
    hop(wq, 2, 0)
    begin(wo, 1)
    hop(wq, 1, 1)
    hop(wq, 3, 0)
    swapped(x_swap[1].start)
    hop(wq, 2, 1)
    hop(wo, 0, 0)
    begin(wu, 0)
    hop(wq, 3, 1)
    hop(wo, 1, 0)
    begin(wu, 1)
    a1_gather[0].finish()
    kept(lambda: loss_grad(0), lambda: loss_grad(1))
    wq.finish()

    project(0)
    hop(wo, 0, 1)
    hop(wo, 1, 1)
    attend(0)
    swapped(lambda: first_norm(1))
    begin(wu, 2)
    wo.finish()
    attn_sum[0].start(out_term(0))
    hop(wu, 0, 0)
    begin(wu, 3)
    a1_gather[1].forward()
    hop(wu, 1, 0)
    swapped(c_swap[0].start)
    hop(wu, 0, 1)
    make_bias(1)
    a1_gather[1].finish()
    project(1)
    hop(wu, 2, 0)
    swapped(c_swap[1].start)
    hop(wu, 1, 1)
    attend(1)
    attn_sum[1].start(out_term(1))
    hop(wu, 3, 0)
    begin(wd, 0)
    hop(wu, 2, 1)
    second_norm(0, attn_sum[0].finish())
    swapped(lambda: loss_grad(0))
    begin(wd, 1)
    hop(wu, 3, 1)
    second_norm(1, attn_sum[1].finish())
    a2_gather[0].forward()
    swapped(lambda: loss_grad(1))
    begin(wd, 2)
    wu.finish()
    a2_gather[0].finish()
    up(0)
    hop(wd, 0, 0)
    begin(wd, 3)
    a2_gather[1].forward()
    hop(wd, 1, 0)
    hop(wd, 0, 1)
    a2_gather[1].finish()
    up(1)
    gb_gather[0].forward()
    hop(wd, 2, 0)
    hop(wd, 1, 1)
    gb_gather[1].forward()
    hop(wd, 3, 0)
    hop(wd, 2, 1)
    gb_gather[0].finish()
    gb_gather[1].finish()
    hop(wd, 3, 1)
    place(GD, GD.shape[0], dg(micros(Z), both(GB), NT))
    wave(gd, 1)
    wd.finish()

    down_back(0)
    mid_sum[0].start(mid_term(0))
    down_back(1)
    mid_sum[1].start(mid_term(1))
    place(GU, GU.shape[0], dg(both(A2), micros(GP), NT))
    second_norm_back(0, mid_sum[0].finish())
    wave(gd, 2)
    wave(gu, 1)
    second_norm_back(1, mid_sum[1].finish())
    for w in (wq, wo, wu, wd):
        w.sent()
    y_sum[0].start(y_term(0))
    dhb_gather[0].forward()
    dhb_gather[0].finish()
    heads_back(0)
    wave(gd, 3)
    y_sum[1].start(y_term(1))
    dhb_gather[1].forward()
    in_sum[0].start(in_term(0))
    dhb_gather[1].finish()
    place(WD, go[0].ch * COLS, dg(micros(O), both(DHB), NT))
    wave(go, 1)
    heads_back(1)
    wave(gu, 2)
    in_sum[1].start(in_term(1))
    place(WU, gq[0].ch * COLS, dg(micros(QKV), both(A1), NT))
    wave(gq, 1)
    give_output(0)
    wave(go, 2)
    wave(gu, 3)
    wave(gd, 4)
    wave(go, 3)
    wave(gq, 2)
    wave(gd, 5)
    wave(gq, 3)
    give_output(1)
    wave(gu, 5)
    wave(gd, 6)
    first_norm_back(0, in_sum[0].finish())
    first_norm_back(1, in_sum[1].finish())
    sum_copies[0].start()
    give_input_grad(0)
    give_input_grad(1)
    wave(gd, 7)
    wave(gu, 6)
    sweep(gq + go, 4)
    sum_add(0)
    sum_copies[1].start()
    sweep(gq + go, 5)
    wave(gu, 7)
    sum_add(1)
    sum_copies[2].start()
    sweep(gq + go, 6)
    sum_add(2)
    sum_copies[3].start()
    sum_add(3)
    sum_copies[4].start()
    sweep(gq + go, 7)
    sum_add(4)
    ng_ref[...] = NG[...]
    for m in range(micro):

        @pl.when(sw)
        def _():
            ig_swap[m].wait()
            DH[m] = CS[m].astype(F32)
            ig_keep[m].start()
            out_swap[m].wait()
            x_swap[m].wait_send()
            c_swap[m].wait_send()

        ig_keep[m].wait()
        kept(out_keep[m].wait)
    swapped(lab_swap.wait_send)
    for cp in pending:
        cp.wait_send()
    for p in gd + gu + gq + go:
        p.finish()


def layer(
    inputs, segments, norm1_gain, norm1_bias, qkv_weight, out_weight, norm2_gain, norm2_bias, up_weight, down_weight,
    cotangent,
):
    micro, tok, width = inputs.shape
    local_width = qkv_weight.shape[2]
    ff = up_weight.shape[1]
    row = 4 * tok
    heads = local_width // HD
    three = 3 * local_width
    lw, lf = up_to(width, 128), up_to(ff, 128)
    half = row // 2
    cq, co, cu, cd = chunk_rows(three), chunk_rows(local_width), chunk_rows(width), chunk_rows(ff)
    wq = jnp.transpose(qkv_weight, (0, 2, 1)).reshape(three, width)

    def tail(w, ch):
        rest = w[(COLS - 1) * ch :]
        return [rest, jnp.zeros((ch - rest.shape[0], width), BF)]

    ends = jnp.concatenate(tail(wq, cq) + tail(out_weight, co), axis=0)

    def v(shape, dtype=BF):
        return pltpu.VMEM(shape, dtype)

    def recv(ch, lanes):
        return v((COLS - 1, ch, lanes))

    any_spec = pl.BlockSpec(memory_space=pl.ANY)
    vmem = pl.BlockSpec(memory_space=pltpu.VMEM)
    block = (width, tok)
    scratch = [
        v((COLS * cq, width)), v((COLS * co, width)), v((COLS * cu, ff)), v((COLS * cd, width)),
        v((COLS * cu, lf)), v((COLS * cd, lw)),
        recv(cq, width), recv(co, width), recv(cu, lf), recv(cd, lw),
        v((cq, width)), v((co, width)), v((cu, lf)), v((cd, lw)),
        v((cq, width)), v((co, width)), v((cu, lf)), v((cd, lw)),
        v((micro, *block)), v((micro, *block)), v((4, micro, tok), jnp.int32), v((micro, row, tok), F32),
        v((row, row), F32), v((4, *block), F32),
        v((4 * micro, *block)), v((micro, three, row)),
        v((micro, heads, half, half)), v((micro, heads, row, half)), v((micro, local_width, row)),
        v((micro, *block), F32),
        v((4 * micro, *block)), v((micro, ff, row)), v((micro, ff, row)), v((4 * micro, *block)),
        v((4 * micro, *block)), v((micro, local_width, row)), v((micro, *block), F32), v((ff, half), F32),
        v((2 * micro + 1, *block), F32),
        v((2 * micro, 2, *block)), v((2 * micro, *block)), v((2 * micro, 2, *block)), v((2 * micro, *block)),
        v((micro, *block)),
        v((8, width), F32), v((5, 8, width), F32),
        pltpu.SemaphoreType.DMA((NSEM,)), pltpu.SemaphoreType.DMA((NSEM,)), pltpu.SemaphoreType.DMA((24,)),
    ]
    out, input_grad, gq, go, gu, gd, ng = pl.pallas_call(
        kernel,
        out_shape=[
            jax.ShapeDtypeStruct((micro, *block), BF),
            jax.ShapeDtypeStruct((micro, *block), F32),
            jax.ShapeDtypeStruct((COLS * cq, width), BF),
            jax.ShapeDtypeStruct((COLS * co, width), BF),
            jax.ShapeDtypeStruct((COLS * cu, lf), BF),
            jax.ShapeDtypeStruct((COLS * cd, lw), BF),
            jax.ShapeDtypeStruct((8, width), F32),
        ],
        in_specs=[any_spec, vmem, vmem, vmem] + [any_spec] * 3 + [vmem, vmem] + [any_spec] * 3,
        out_specs=[any_spec] * 6 + [vmem],
        scratch_shapes=scratch,
        compiler_params=pltpu.CompilerParams(
            collective_id=0, has_side_effects=True, vmem_limit_bytes=64 * 1024 * 1024
        ),
    )(
        jnp.transpose(inputs, (0, 2, 1)), segments, norm1_gain, norm1_bias,
        wq, ends, out_weight, norm2_gain, norm2_bias, up_weight, down_weight,
        jnp.transpose(cotangent, (0, 2, 1)),
    )
    grads = (
        jnp.transpose(gq[:three].astype(F32).reshape(3, local_width, width), (0, 2, 1)),
        go[:local_width].astype(F32),
        gu[:width, :ff].astype(F32),
        gd[:ff, :width].astype(F32),
    )
    extent = lax.axis_size("dp")
    block = 2 * COLS
    if extent > block:
        groups = [[r + block * j for j in range(extent // block)] for r in range(block)]
        grads = lax.psum(grads, "dp", axis_index_groups=groups)
        ng = lax.psum(ng, "dp", axis_index_groups=groups)
    gq, go, gu, gd = grads
    out, input_grad = jnp.transpose(out, (0, 2, 1)), jnp.transpose(input_grad, (0, 2, 1))
    return out, input_grad, ng[0], ng[1], gq, go, ng[2], ng[3], gu, gd


def solution(mesh):
    tokens = P(None, ("dp", "tensor"), None)
    weights = (P(None, None, "tensor"), P("tensor", None))
    mlp = (P(None, "tensor"), P("tensor", None))
    return jax.shard_map(
        layer,
        mesh=mesh,
        in_specs=(tokens, P(None, ("dp", "tensor")), P(), P(), *weights, P(), P(), *mlp, tokens),
        out_specs=(tokens, tokens, P(), P(), *weights, P(), P(), *mlp),
        check_vma=False,
    )
```

```python
import functools

import jax
import jax.numpy as jnp
from jax import lax
from jax.experimental import pallas as pl
from jax.experimental.pallas import tpu as pltpu
from jax.sharding import PartitionSpec as P


HD = 56
BF = jnp.bfloat16
F32 = jnp.float32
MESH = pl.DeviceIdType.MESH
NN = (((1,), (0,)), ((), ()))
NT = (((1,), (1,)), ((), ()))
TN = (((0,), (0,)), ((), ()))
COLS = 4
BITS = (1, 2)
NSEM = 217


def up_to(n, m):
    return -(-n // m) * m


def chunk_rows(rows):
    return up_to(-(-rows // COLS), 16)


def parts_of(ch, n):
    out, off = [], 0
    for i in range(n):
        size = up_to(-(-(ch - off) // (n - i)), 16)
        out.append((off, size, BITS if i % 2 == 0 else BITS[::-1], i % 2))
        off += size
    return out


def dg(a, b, dims):
    return lax.dot_general(a, b, dims, preferred_element_type=F32)


def normed(v):
    center = v - jnp.mean(v, axis=0, keepdims=True)
    rstd = lax.rsqrt(jnp.mean(center * center, axis=0, keepdims=True) + 1e-05)
    return center * rstd, rstd


def kernel(
    x_hbm, seg_ref, n1g, n1b, wq_hbm, ends, wo_hbm, n2g, n2b, wu_hbm, wd_hbm, c_hbm,
    out_hbm, ig_hbm, gq_hbm, go_hbm, gu_hbm, gd_hbm, ng_ref,
    WQ, WO, WU, WD, GU, GD, RQ, RO, RU, RD, SQ, SO, SU, SD, KQ, KO, KU, KD,
    XS, CS, LAB, LT, BIAS, NW, A1, QKV, PB0, PB1, O, HS, A2, Z, GP, GB, DHB, DO, DH, U,
    T2, S1, SZ, R1, RZ, OB, NG, NR,
    ssem, rsem, lsem,
):
    d = lax.axis_index("dp")
    z = lax.axis_index("tensor")
    c = lax.rem(d, 2)
    q = lax.rem(d // 2, COLS)
    zl = lax.rem(z, 2)
    zh = z // 2
    b = zl + 2 * c
    sw = zh != c
    dc = d + 1 - 2 * c
    z1 = z + 1 - 2 * zl
    z2 = z + 2 - 4 * zh
    core = (dc, z)
    zpeer = (d, z1)
    sigma = (dc, z2)

    def flip(owner, bit):
        on = lax.rem(owner // bit, 2)
        return owner + bit * (1 - 2 * on)

    def col(bit):
        return (d + 2 * (flip(q, bit) - q), z)

    def masked(owner, s):
        for k in BITS:
            if s & k:
                owner = flip(owner, k)
        return owner

    xpeer, ypeer = col(1), col(2)
    micro, width, tok = XS.shape
    row = 4 * tok
    half = row // 2
    local_width = O.shape[1]
    ff = Z.shape[1]
    heads = local_width // HD
    scale = HD ** (-0.5)
    counts = dict(r=0, l=0)
    pending = []

    def rcopy(src, dst, peer):
        i = counts["r"]
        counts["r"] = i + 1
        assert i < NSEM
        return pltpu.make_async_remote_copy(
            src_ref=src, dst_ref=dst, send_sem=ssem.at[i], recv_sem=rsem.at[i], device_id=peer, device_id_type=MESH
        )

    def lcopy(src, dst):
        i = counts["l"]
        counts["l"] = i + 1
        return pltpu.make_async_copy(src, dst, lsem.at[i])

    def rows(start, size, step=16):
        return pl.ds(pl.multiple_of(start, step), size)

    def cols(j):
        return pl.ds(pl.multiple_of(j * tok, tok), tok)

    def swapped(*fs):
        @pl.when(sw)
        def _():
            for f in fs:
                f()

    def kept(*fs):
        @pl.when(jnp.logical_not(sw))
        def _():
            for f in fs:
                f()

    barrier = pltpu.get_barrier_semaphore()
    peers = (core, zpeer, sigma, xpeer, ypeer)
    for p in peers:
        pl.semaphore_signal(barrier, 1, device_id=p, device_id_type=MESH)
    pl.semaphore_wait(barrier, len(peers))

    class Gather:
        def __init__(self, view):
            self.own = view(b)
            self.cz = rcopy(view(b), view(b), zpeer)
            self.cc = rcopy(view(b), view(b), core)
            far = 1 - zl + 2 * c
            self.cf = rcopy(view(far), view(far), core)

        def start(self):
            self.cz.start()
            self.cc.start()

        def forward(self):
            self.cz.wait_recv()
            self.cf.start()

        def finish(self):
            self.cc.wait_recv()
            self.cf.wait_recv()
            pending.extend([self.cz, self.cc, self.cf])

    def gather_rows(ref, m):
        return Gather(lambda j: ref.at[m * 4 + j])

    class Scatter:
        def __init__(self, s):
            self.s = s
            self.idx = counts["r"]
            counts["r"] += 2
            self.cz = rcopy(SZ.at[s], RZ.at[s], zpeer)

        def give(self, i):
            return pltpu.make_async_remote_copy(
                src_ref=S1.at[self.s, i], dst_ref=R1.at[self.s, i], send_sem=ssem.at[self.idx + i],
                recv_sem=rsem.at[self.idx + i], device_id=core, device_id_type=MESH,
            )

        def start(self, term):
            s = self.s

            def body(i, carry):
                side = lax.rem(1 - zl + i, 2)
                part = term(side + 2 * (1 - c), side + 2 * c)
                S1[s, i] = part[:, :tok].astype(BF)
                T2[s * i + 2 * micro * (1 - i)] = part[:, tok:]
                self.give(i).start()
                return carry

            lax.fori_loop(0, 2, body, 0)
            self.give(0).wait_recv()
            SZ[s] = (T2[2 * micro] + R1[s, 0].astype(F32)).astype(BF)
            self.cz.start()

        def finish(self):
            s = self.s
            self.give(1).wait_recv()
            self.cz.wait_recv()
            total = T2[s] + R1[s, 1].astype(F32) + RZ[s].astype(F32)
            self.give(0).wait_send()
            self.give(1).wait_send()
            self.cz.wait_send()
            return total

    class Weight:
        def __init__(self, hbm, ref, n, end=None):
            ch = ref.shape[0] // COLS
            whole = hbm.shape[0] if end is None else (COLS - 1) * ch
            self.locals = [lcopy(hbm.at[0:whole], ref.at[0:whole])]
            if end is not None:
                self.locals.append(lcopy(end, ref.at[whole : whole + ch]))
            self.hops = []
            for off, size, order, _ in parts_of(ch, n):
                i = counts["r"]
                counts["r"] = i + 1

                def first(src, at, i=i):
                    return pltpu.make_async_remote_copy(
                        src_ref=src, dst_ref=ref.at[at], send_sem=ssem.at[i], recv_sem=rsem.at[i],
                        device_id=sigma, device_id_type=MESH,
                    )

                at = rows(q * ch + off, size)
                usual = first(hbm.at[at], at)
                last_at = (COLS - 1) * ch + off
                last_size = max(0, min(size, whole - last_at))
                at = slice(last_at, last_at + last_size)
                last = usual if last_size == size else first(hbm.at[at], at) if last_size else None
                if end is not None:
                    last = first(end.at[off : off + size], slice(last_at, last_at + size))
                steps, done = [], [0]
                for bit in order:
                    copies = []
                    for s in done:
                        at = rows(masked(q, s) * ch + off, size)
                        copies.append(rcopy(ref.at[at], ref.at[at], col(bit)))
                    steps.append(copies)
                    done = done + [s | bit for s in done]
                self.hops.append(((usual, last), steps))

        def first(self, hop, act):
            usual, last = hop[0]
            if last is usual:
                act(usual)
                return
            pl.when(q < COLS - 1)(lambda: act(usual))
            if last is not None:
                pl.when(q == COLS - 1)(lambda: act(last))

        def load(self):
            kept(*[cp.start for cp in self.locals])

        def pass_on(self, h, j):
            if j == 0:
                self.first(h, lambda cp: cp.wait_recv())
            else:
                for cp in h[1][j - 1]:
                    cp.wait_recv()
            for cp in h[1][j]:
                cp.start()

        def finish(self):
            def go():
                for h in self.hops:
                    for cp in h[1][-1]:
                        cp.wait_recv()

            swapped(go)
            kept(*[cp.wait for cp in self.locals])

        def sent(self):
            def go():
                for h in self.hops:
                    self.first(h, lambda cp: cp.wait_send())
                    for copies in h[1]:
                        for cp in copies:
                            cp.wait_send()

            swapped(go)

    class Piece:
        def __init__(self, ref, recv, far, near, hbm, off, size, order, fin):
            self.ref, self.recv, self.far, self.near, self.hbm = ref, recv, far, near, hbm
            self.off, self.size, self.fin = off, size, fin
            self.ch = recv.shape[1]
            self.place = slice(off, off + size)
            base, self.sums = 0, []
            for j, bit in enumerate(order):
                rest = [0]
                for k in order[j + 1 :]:
                    rest = rest + [s | k for s in rest]
                copies = []
                for i, s in enumerate(rest):
                    mine = masked(q, s)
                    slot = recv.at[base + i, self.place]
                    copies.append((mine, base + i, rcopy(ref.at[self.at(flip(mine, bit))], slot, col(bit))))
                base += len(rest)
                self.sums.append(copies)
            own, out = ref.at[self.at(q)], hbm.at[self.at(q)]
            self.trade = rcopy(own, far.at[self.place], sigma)
            self.join = rcopy(own, near.at[self.place], core)
            self.own = lcopy(own, out)
            self.own_core = rcopy(own, out, core)
            done, self.spreads = [0], []
            for bit in order:
                copies = []
                for s in done:
                    owner = masked(q, s)
                    src = own if s == 0 else hbm.at[self.at(owner)]
                    got = hbm.at[self.at(flip(owner, bit))]
                    copies.append((rcopy(src, hbm.at[self.at(owner)], col(bit)), rcopy(got, got, core)))
                self.spreads.append(copies)
                done = done + [s | bit for s in done]
            self.steps = [self.send_first, self.add_send, self.add_trade, self.take_join, self.join_spread]
            self.steps += [functools.partial(self.spread, j) for j in range(len(self.spreads))]
            self.done = 0

        def at(self, owner):
            return rows(owner * self.ch + self.off, self.size)

        def run(self, upto):
            while self.done < min(upto, len(self.steps)):
                self.steps[self.done]()
                self.done += 1

        def by_rows(self, owner, more, plain=False):
            base = owner * self.ch + self.off

            def body(i, carry):
                r = rows(base + i * 16, 16)
                other = more[rows(self.off + i * 16, 16), :]
                if not plain:
                    other = (self.ref[r, :].astype(F32) + other.astype(F32)).astype(BF)
                self.ref[r, :] = other
                return carry

            lax.fori_loop(0, self.size // 16, body, 0)

        def add(self, j):
            for mine, slot, cp in self.sums[j]:
                cp.wait_recv()
                self.by_rows(mine, self.recv.at[slot])
                pending.append(cp)

        def send_first(self):
            for _, _, cp in self.sums[0]:
                cp.start()

        def add_send(self):
            self.add(0)
            for _, _, cp in self.sums[1]:
                cp.start()

        def add_trade(self):
            self.add(1)
            swapped(self.trade.start)

        def take_join(self):
            def go():
                self.trade.wait()
                self.by_rows(q, self.far, plain=True)

            swapped(go)
            pl.when(c != self.fin)(self.join.start)

        def join_spread(self):
            def take():
                self.join.wait_recv()
                self.by_rows(q, self.near)
                for cp, _ in self.spreads[0]:
                    cp.start()
                self.own_core.start()
                self.own.start()

            pl.when(c == self.fin)(take)

        def spread(self, j):
            def go():
                for cp, _ in self.spreads[j]:
                    cp.wait_recv()
                if j + 1 < len(self.spreads):
                    for cp, _ in self.spreads[j + 1]:
                        cp.start()
                for _, cp in self.spreads[j]:
                    cp.start()

            pl.when(c == self.fin)(go)

        def finish(self):
            def owner():
                self.own.wait()
                self.own_core.wait_send()
                for copies in self.spreads:
                    for a, f in copies:
                        a.wait_send()
                        f.wait_send()

            def other():
                self.join.wait_send()
                self.own_core.wait_recv()
                for copies in self.spreads:
                    for _, f in copies:
                        f.wait_recv()

            pl.when(c == self.fin)(owner)
            pl.when(c != self.fin)(other)

    def pieces(ref, recv, far, near, hbm, n):
        return [Piece(ref, recv, far, near, hbm, *p) for p in parts_of(recv.shape[1], n)]

    def wave(group, last):
        first = min(p.done for p in group)
        for t in range(first, last + len(group)):
            for i, p in enumerate(group):
                p.run(min(last, t - i + 1))

    def sweep(group, last):
        for t in range(min(p.done for p in group), last):
            for p in group:
                p.run(t + 1)

    wq = Weight(wq_hbm, WQ, 4, ends.at[0 : WQ.shape[0] // COLS])
    wo = Weight(wo_hbm, WO, 2, ends.at[WQ.shape[0] // COLS :])
    wu, wd = Weight(wu_hbm, WU, 4), Weight(wd_hbm, WD, 4)
    other_b = zl + 2 * (1 - c)
    x_swap = [rcopy(x_hbm.at[m], XS.at[m], sigma) for m in range(micro)]
    x_load = [lcopy(x_hbm.at[m], XS.at[m]) for m in range(micro)]
    c_swap = [rcopy(c_hbm.at[m], CS.at[m], sigma) for m in range(micro)]
    c_load = [lcopy(c_hbm.at[m], CS.at[m]) for m in range(micro)]
    lab_swap = rcopy(seg_ref, LAB.at[other_b], sigma)
    lab_gather = Gather(lambda j: LAB.at[j])
    a1_gather = [gather_rows(A1, m) for m in range(micro)]
    gb_gather = [gather_rows(GB, m) for m in range(micro)]
    a2_gather = [gather_rows(A2, m) for m in range(micro)]
    dhb_gather = [gather_rows(DHB, m) for m in range(micro)]
    attn_sum = [Scatter(2 * m) for m in range(micro)]
    mid_sum = [Scatter(2 * m) for m in range(micro)]
    y_sum = [Scatter(2 * m + 1) for m in range(micro)]
    in_sum = [Scatter(2 * m) for m in range(micro)]
    gd = pieces(GD, RD, SD, KD, gd_hbm, 2)
    gu = pieces(GU, RU, SU, KU, gu_hbm, 2)
    gq = pieces(WU, RQ, SQ, KQ, gq_hbm, 2)
    go = pieces(WD, RO, SO, KO, go_hbm, 2)
    out_swap = [rcopy(OB.at[m], out_hbm.at[m], sigma) for m in range(micro)]
    out_keep = [lcopy(OB.at[m], out_hbm.at[m]) for m in range(micro)]
    ig_swap = [rcopy(XS.at[m], CS.at[m], sigma) for m in range(micro)]
    ig_keep = [lcopy(DH.at[m], ig_hbm.at[m]) for m in range(micro)]
    sum_copies = [rcopy(NG, NR.at[i], p) for i, p in enumerate((sigma, xpeer, ypeer, zpeer, core))]

    def widen():
        for i, ref in enumerate((n1g, n1b, n2g, n2b)):
            NW[i] = jnp.transpose(jnp.broadcast_to(ref[...].reshape(1, width), (tok, width)))

    def first_norm(m):
        swapped(x_swap[m].wait_recv)
        kept(x_load[m].wait)
        xhat, _ = normed(XS[m].astype(F32))
        A1[m * 4 + b] = (xhat * NW[0] + NW[1]).astype(BF)
        a1_gather[m].start()

    def loss_grad(m):
        swapped(c_swap[m].wait_recv)
        kept(c_load[m].wait)
        labels = LAB[b]
        live = (labels[m : m + 1, :] >= 0).astype(F32)
        GB[m * 4 + b] = (CS[m].astype(F32) * live).astype(BF)
        gb_gather[m].start()

    def labels_wide():
        for m in range(micro):
            for j in range(4):
                lab = LAB[j, m : m + 1, :].astype(F32)
                LT[m, j * tok : (j + 1) * tok, :] = jnp.transpose(jnp.broadcast_to(lab, (tok, tok)))

    def make_bias(m):
        for j in range(4):
            lab = LAB[j, m : m + 1, :].astype(F32)
            place_k = lax.broadcasted_iota(jnp.int32, (row, tok), 0)
            place_q = lax.broadcasted_iota(jnp.int32, (row, tok), 1) + j * tok
            ok = (LT[m] == lab) & (place_k <= place_q)
            BIAS[:, j * tok : (j + 1) * tok] = jnp.where(ok, 0.0, -1e30)

    def whole(ref, m):
        return jnp.concatenate([ref[m * 4 + j] for j in range(4)], axis=1)

    def both(ref):
        return jnp.concatenate([ref[j] for j in range(ref.shape[0])], axis=1)

    def pair(ref, m, i, j):
        return jnp.concatenate([ref[m, :, cols(i)], ref[m, :, cols(j)]], axis=1)

    def project(m):
        QKV[m] = dg(WQ[0 : 3 * local_width, :], whole(A1, m), NN).astype(BF)

    def head_slices(h, qb):
        e = [slice(i * local_width + h * HD, i * local_width + (h + 1) * HD) for i in range(3)]
        return slice(qb * half, (qb + 1) * half), slice(0, (qb + 1) * half), *e

    def attend(m):
        for h in range(heads):
            for qb, PB in ((0, PB0), (1, PB1)):
                at, upto, eq, ek, ev = head_slices(h, qb)
                s = dg(QKV[m, ek, upto], QKV[m, eq, at], TN) * scale + BIAS[upto, at]
                e = jnp.exp(s - jnp.max(s, axis=0, keepdims=True))
                p = (e * (1.0 / jnp.sum(e, axis=0, keepdims=True))).astype(BF)
                PB[m, h] = p
                O[m, eq, at] = dg(QKV[m, ev, upto], p, NN).astype(BF)

    def heads_back(m):
        DO[m] = dg(WO[0:local_width, :], whole(DHB, m), NN).astype(BF)
        for h in range(heads):
            for qb, PB in ((1, PB1), (0, PB0)):
                at, upto, eq, ek, ev = head_slices(h, qb)
                qv, do, pb, kv = QKV[m, eq, at], DO[m, eq, at], PB[m, h], QKV[m, ek, upto]
                p = pb.astype(F32)
                pdp = p * dg(QKV[m, ev, upto], do, TN)
                ds = (pdp - p * jnp.sum(pdp, axis=0, keepdims=True)).astype(BF)
                dq = (dg(kv, ds, NN) * scale).astype(BF)
                dk, dv = dg(qv, ds, NT), dg(do, pb, NT)
                if qb == 1:
                    dq1, dk1, dv1, at1 = dq, dk, dv, at
                else:
                    QKV[m, eq, at] = dq
                    QKV[m, eq, at1] = dq1
                    QKV[m, ek, at] = ((dk1[:, :half] + dk) * scale).astype(BF)
                    QKV[m, ek, at1] = (dk1[:, half:] * scale).astype(BF)
                    QKV[m, ev, at] = (dv1[:, :half] + dv).astype(BF)
                    QKV[m, ev, at1] = dv1[:, half:].astype(BF)

    def second_norm(m, total):
        h = XS[m].astype(F32) + total
        HS[m] = h
        xhat, _ = normed(h)
        A2[m * 4 + b] = (xhat * NW[2] + NW[3]).astype(BF)
        a2_gather[m].start()

    def up(m):
        c0 = 0.7978845608028654
        step = 32

        def side(j, carry):
            blocks = jnp.concatenate([A2[m * 4 + 2 * j], A2[m * 4 + 2 * j + 1]], axis=1)
            U[...] = dg(WU[0:width, :], blocks, TN)
            at = pl.ds(pl.multiple_of(j * half, half), half)

            def body(i, carry):
                r = rows(i * step, step, step)
                u = U[r, :]
                u2 = u * u
                t = jnp.tanh(c0 * u * (1.0 + 0.044715 * u2))
                hp = 0.5 * (1.0 + t)
                Z[m, r, at] = (u * hp).astype(BF)
                GP[m, r, at] = (hp + (0.5 * c0) * u * (1.0 - t * t) * (1.0 + (3 * 0.044715) * u2)).astype(BF)
                return carry

            return lax.fori_loop(0, ff // step, body, carry)

        lax.fori_loop(0, 2, side, 0)

    def down_back(m):
        dz = dg(WD[0:ff, :], whole(GB, m), NN)
        GP[m] = (dz * GP[m].astype(F32)).astype(BF)

    def over_tokens(v):
        ones = jnp.ones((8, tok), BF)
        high = v.astype(BF)
        low = (v - high.astype(F32)).astype(BF)
        return (dg(ones, high, NT) + dg(ones, low, NT))[0:1, :]

    def norm_back(v, gain, grad, i):
        xhat, rstd = normed(v)
        dn = grad * gain
        dv = rstd * (
            dn - jnp.mean(dn, axis=0, keepdims=True) - xhat * jnp.mean(dn * xhat, axis=0, keepdims=True)
        )
        return dv, grad * xhat

    def second_norm_back(m, total):
        dv, gains = norm_back(HS[m], NW[2], total, 2)
        dh = GB[m * 4 + b].astype(F32) + dv
        DH[m] = dh
        DHB[m * 4 + b] = dh.astype(BF)
        dhb_gather[m].start()
        NG[2:3, :] += over_tokens(gains)
        NG[3:4, :] += over_tokens(total)

    def first_norm_back(m, total):
        dv, gains = norm_back(XS[m].astype(F32), NW[0], total, 0)
        DH[m] = DH[m] + dv
        NG[0:1, :] += over_tokens(gains)
        NG[1:2, :] += over_tokens(total)

    def give_input_grad(m):
        @pl.when(sw)
        def _():
            XS[m] = DH[m].astype(BF)
            ig_swap[m].start()

        kept(ig_keep[m].start)

    def out_term(m):
        return lambda i, j: dg(WO[0:local_width, :], pair(O, m, i, j), TN)

    def y_term(m):
        return lambda i, j: dg(WD[0:ff, :], pair(Z, m, i, j), TN)

    def mid_term(m):
        return lambda i, j: dg(WU[0:width, :], pair(GP, m, i, j), NN)

    def in_term(m):
        return lambda i, j: dg(WQ[0 : 3 * local_width, :], pair(QKV, m, i, j), TN)

    def give_output(m):
        OB[m] = (HS[m] + y_sum[m].finish()).astype(BF)
        swapped(out_swap[m].start)
        kept(out_keep[m].start)

    def sum_add(i):
        sum_copies[i].wait()
        NG[...] = NG[...] + NR[i]

    def place(ref, height, value):
        n, m = value.shape
        ref[0:n, 0:m] = value.astype(BF)
        ref[n:height, :] = jnp.zeros((height - n, ref.shape[1]), BF)
        if m < ref.shape[1]:
            ref[0:n, m:] = jnp.zeros((n, ref.shape[1] - m), BF)

    def micros(ref):
        return jnp.concatenate([ref[m] for m in range(micro)], axis=1)

    def begin(w, i):
        swapped(lambda: w.first(w.hops[i], lambda cp: cp.start()))

    def hop(w, i, j):
        swapped(lambda: w.pass_on(w.hops[i], j))

    swapped(lab_swap.start, x_swap[0].start)
    begin(wq, 0)
    begin(wq, 1)
    kept(*[cp.start for cp in x_load])
    for w in (wq, wo, wu, wd):
        w.load()
    kept(*[cp.start for cp in c_load])

    @pl.when(jnp.logical_not(sw))
    def _():
        LAB[b] = seg_ref[...]

    NG[...] = jnp.zeros_like(NG)
    widen()
    swapped(lab_swap.wait_recv)
    lab_gather.start()
    first_norm(0)
    begin(wq, 2)
    kept(lambda: first_norm(1))
    lab_gather.forward()
    hop(wq, 0, 0)
    begin(wq, 3)
    a1_gather[0].forward()
    hop(wq, 1, 0)
    begin(wo, 0)
    hop(wq, 0, 1)
    lab_gather.finish()
    labels_wide()
    make_bias(0)
    hop(wq, 2, 0)
    begin(wo, 1)
    hop(wq, 1, 1)
    hop(wq, 3, 0)
    swapped(x_swap[1].start)
    hop(wq, 2, 1)
    hop(wo, 0, 0)
    begin(wu, 0)
    hop(wq, 3, 1)
    hop(wo, 1, 0)
    begin(wu, 1)
    a1_gather[0].finish()
    kept(lambda: loss_grad(0), lambda: loss_grad(1))
    wq.finish()

    project(0)
    hop(wo, 0, 1)
    hop(wo, 1, 1)
    attend(0)
    swapped(lambda: first_norm(1))
    begin(wu, 2)
    wo.finish()
    attn_sum[0].start(out_term(0))
    hop(wu, 0, 0)
    begin(wu, 3)
    a1_gather[1].forward()
    hop(wu, 1, 0)
    swapped(c_swap[0].start)
    hop(wu, 0, 1)
    make_bias(1)
    a1_gather[1].finish()
    project(1)
    hop(wu, 2, 0)
    swapped(c_swap[1].start)
    hop(wu, 1, 1)
    attend(1)
    attn_sum[1].start(out_term(1))
    hop(wu, 3, 0)
    begin(wd, 0)
    hop(wu, 2, 1)
    second_norm(0, attn_sum[0].finish())
    swapped(lambda: loss_grad(0))
    begin(wd, 1)
    hop(wu, 3, 1)
    second_norm(1, attn_sum[1].finish())
    a2_gather[0].forward()
    swapped(lambda: loss_grad(1))
    begin(wd, 2)
    wu.finish()
    a2_gather[0].finish()
    up(0)
    hop(wd, 0, 0)
    begin(wd, 3)
    a2_gather[1].forward()
    hop(wd, 1, 0)
    hop(wd, 0, 1)
    a2_gather[1].finish()
    up(1)
    gb_gather[0].forward()
    hop(wd, 2, 0)
    hop(wd, 1, 1)
    gb_gather[1].forward()
    hop(wd, 3, 0)
    hop(wd, 2, 1)
    gb_gather[0].finish()
    gb_gather[1].finish()
    hop(wd, 3, 1)
    place(GD, GD.shape[0], dg(micros(Z), both(GB), NT))
    wave(gd, 1)
    wd.finish()

    down_back(0)
    mid_sum[0].start(mid_term(0))
    down_back(1)
    mid_sum[1].start(mid_term(1))
    place(GU, GU.shape[0], dg(both(A2), micros(GP), NT))
    wave(gd, 2)
    wave(gu, 1)
    second_norm_back(0, mid_sum[0].finish())
    second_norm_back(1, mid_sum[1].finish())
    for w in (wq, wo, wu, wd):
        w.sent()
    y_sum[0].start(y_term(0))
    dhb_gather[0].forward()
    dhb_gather[0].finish()
    heads_back(0)
    wave(gd, 3)
    y_sum[1].start(y_term(1))
    dhb_gather[1].forward()
    in_sum[0].start(in_term(0))
    dhb_gather[1].finish()
    place(WD, go[0].ch * COLS, dg(micros(O), both(DHB), NT))
    wave(go, 1)
    heads_back(1)
    wave(gu, 2)
    in_sum[1].start(in_term(1))
    place(WU, gq[0].ch * COLS, dg(micros(QKV), both(A1), NT))
    wave(gq, 1)
    give_output(0)
    wave(go, 2)
    wave(gu, 3)
    wave(gd, 4)
    wave(go, 3)
    wave(gq, 2)
    wave(gd, 5)
    wave(gq, 3)
    give_output(1)
    wave(gu, 5)
    wave(gd, 6)
    first_norm_back(0, in_sum[0].finish())
    first_norm_back(1, in_sum[1].finish())
    sum_copies[0].start()
    give_input_grad(0)
    give_input_grad(1)
    wave(gd, 7)
    wave(gu, 6)
    sweep(gq + go, 4)
    sum_add(0)
    sum_copies[1].start()
    sweep(gq + go, 5)
    wave(gu, 7)
    sum_add(1)
    sum_copies[2].start()
    sweep(gq + go, 6)
    sum_add(2)
    sum_copies[3].start()
    sum_add(3)
    sum_copies[4].start()
    sweep(gq + go, 7)
    sum_add(4)
    ng_ref[...] = NG[...]
    for m in range(micro):

        @pl.when(sw)
        def _():
            ig_swap[m].wait()
            DH[m] = CS[m].astype(F32)
            ig_keep[m].start()
            out_swap[m].wait()
            x_swap[m].wait_send()
            c_swap[m].wait_send()

        ig_keep[m].wait()
        kept(out_keep[m].wait)
    swapped(lab_swap.wait_send)
    for cp in pending:
        cp.wait_send()
    for p in gd + gu + gq + go:
        p.finish()


def layer(
    inputs, segments, norm1_gain, norm1_bias, qkv_weight, out_weight, norm2_gain, norm2_bias, up_weight, down_weight,
    cotangent,
):
    micro, tok, width = inputs.shape
    local_width = qkv_weight.shape[2]
    ff = up_weight.shape[1]
    row = 4 * tok
    heads = local_width // HD
    three = 3 * local_width
    lw, lf = up_to(width, 128), up_to(ff, 128)
    half = row // 2
    cq, co, cu, cd = chunk_rows(three), chunk_rows(local_width), chunk_rows(width), chunk_rows(ff)
    wq = jnp.transpose(qkv_weight, (0, 2, 1)).reshape(three, width)

    def tail(w, ch):
        rest = w[(COLS - 1) * ch :]
        return [rest, jnp.zeros((ch - rest.shape[0], width), BF)]

    ends = jnp.concatenate(tail(wq, cq) + tail(out_weight, co), axis=0)

    def v(shape, dtype=BF):
        return pltpu.VMEM(shape, dtype)

    def recv(ch, lanes):
        return v((COLS - 1, ch, lanes))

    any_spec = pl.BlockSpec(memory_space=pl.ANY)
    vmem = pl.BlockSpec(memory_space=pltpu.VMEM)
    block = (width, tok)
    scratch = [
        v((COLS * cq, width)), v((COLS * co, width)), v((COLS * cu, ff)), v((COLS * cd, width)),
        v((COLS * cu, lf)), v((COLS * cd, lw)),
        recv(cq, width), recv(co, width), recv(cu, lf), recv(cd, lw),
        v((cq, width)), v((co, width)), v((cu, lf)), v((cd, lw)),
        v((cq, width)), v((co, width)), v((cu, lf)), v((cd, lw)),
        v((micro, *block)), v((micro, *block)), v((4, micro, tok), jnp.int32), v((micro, row, tok), F32),
        v((row, row), F32), v((4, *block), F32),
        v((4 * micro, *block)), v((micro, three, row)),
        v((micro, heads, half, half)), v((micro, heads, row, half)), v((micro, local_width, row)),
        v((micro, *block), F32),
        v((4 * micro, *block)), v((micro, ff, row)), v((micro, ff, row)), v((4 * micro, *block)),
        v((4 * micro, *block)), v((micro, local_width, row)), v((micro, *block), F32), v((ff, half), F32),
        v((2 * micro + 1, *block), F32),
        v((2 * micro, 2, *block)), v((2 * micro, *block)), v((2 * micro, 2, *block)), v((2 * micro, *block)),
        v((micro, *block)),
        v((8, width), F32), v((5, 8, width), F32),
        pltpu.SemaphoreType.DMA((NSEM,)), pltpu.SemaphoreType.DMA((NSEM,)), pltpu.SemaphoreType.DMA((24,)),
    ]
    out, input_grad, gq, go, gu, gd, ng = pl.pallas_call(
        kernel,
        out_shape=[
            jax.ShapeDtypeStruct((micro, *block), BF),
            jax.ShapeDtypeStruct((micro, *block), F32),
            jax.ShapeDtypeStruct((COLS * cq, width), BF),
            jax.ShapeDtypeStruct((COLS * co, width), BF),
            jax.ShapeDtypeStruct((COLS * cu, lf), BF),
            jax.ShapeDtypeStruct((COLS * cd, lw), BF),
            jax.ShapeDtypeStruct((8, width), F32),
        ],
        in_specs=[any_spec, vmem, vmem, vmem] + [any_spec] * 3 + [vmem, vmem] + [any_spec] * 3,
        out_specs=[any_spec] * 6 + [vmem],
        scratch_shapes=scratch,
        compiler_params=pltpu.CompilerParams(
            collective_id=0, has_side_effects=True, vmem_limit_bytes=64 * 1024 * 1024
        ),
    )(
        jnp.transpose(inputs, (0, 2, 1)), segments, norm1_gain, norm1_bias,
        wq, ends, out_weight, norm2_gain, norm2_bias, up_weight, down_weight,
        jnp.transpose(cotangent, (0, 2, 1)),
    )
    grads = (
        jnp.transpose(gq[:three].astype(F32).reshape(3, local_width, width), (0, 2, 1)),
        go[:local_width].astype(F32),
        gu[:width, :ff].astype(F32),
        gd[:ff, :width].astype(F32),
    )
    extent = lax.axis_size("dp")
    block = 2 * COLS
    if extent > block:
        groups = [[r + block * j for j in range(extent // block)] for r in range(block)]
        grads = lax.psum(grads, "dp", axis_index_groups=groups)
        ng = lax.psum(ng, "dp", axis_index_groups=groups)
    gq, go, gu, gd = grads
    out, input_grad = jnp.transpose(out, (0, 2, 1)), jnp.transpose(input_grad, (0, 2, 1))
    return out, input_grad, ng[0], ng[1], gq, go, ng[2], ng[3], gu, gd


def solution(mesh):
    tokens = P(None, ("dp", "tensor"), None)
    weights = (P(None, None, "tensor"), P("tensor", None))
    mlp = (P(None, "tensor"), P("tensor", None))
    return jax.shard_map(
        layer,
        mesh=mesh,
        in_specs=(tokens, P(None, ("dp", "tensor")), P(), P(), *weights, P(), P(), *mlp, tokens),
        out_specs=(tokens, tokens, P(), P(), *weights, P(), P(), *mlp),
        check_vma=False,
    )
```
